256 devices in a mesh: grp: 4 (over y), sub: 64 (over x, z, core).
Axes of the slice: x: 4, y: 4, z: 8, core: 2. Of those that a mesh axis runs over, the one named last changes fastest.
Arguments:
- cotangent: float32 [2, 32, 512, 128], P(None, 'grp', 'sub'), may hold values from -6 to 6
- head: float32 [32, 512, 128], P('grp', 'sub'), may hold values from -6 to 6
- materials: int32 [32, 512, 128], P('grp', 'sub'), may hold values from 0 to 7
- flags: int32 [3, 32, 512, 128], P(None, 'grp', 'sub'), may hold values 0 or 1
- perm_table: float32 [8], replicated, may hold values from 0.3 to 3
- poro_table: float32 [8], replicated, may hold values from 0.1 to 0.45
Outputs:
- adjoint: float32 [2, 32, 512, 128], P(None, 'grp', 'sub')
The draws below stay inside these ranges and needn't reach their ends.
All inputs are finite; a program needn't handle non-finite values. No bound on the sum of `flags` on one device may be relied on, other than what follows from the above.
Results may differ from the reference program's by a relative error of at most 0.0003.
Values sent between devices are 32-bit elements; how exact they have to be, the bound alone decides.
A program may use at most 64 MiB of HBM per device.

```python
import math
import jax
import jax.numpy as jnp
from jax import lax

CX = 8
CY = 8
AGG = 4
ITERS = 4
SWEEPS = 3
CSWEEPS = 4
NMAT = 8
NX = 32
NY = 512
NZ = 128
N_GRP = 4
N_SUB = 64


def with_ends(array, rng, smallest, top_value):
    extent = array.shape
    place = [jax.random.randint(jax.random.fold_in(rng, axis), (), 0, extent[axis]) for axis in range(len(extent))]
    array = array.at[tuple(place)].set(smallest)
    longest = extent.index(max(extent))
    place[longest] = (place[longest] + 1) % extent[longest]
    return array.at[tuple(place)].set(top_value)


def block_levels(rng, shape, shards, low, high):
    def one(axis_at, blocks):
        steps = jax.random.uniform(jax.random.fold_in(jax.random.fold_in(rng, 6), axis_at), (blocks,), jnp.float32, low / len(shards), high / len(shards))
        return jnp.repeat(jnp.exp(steps), shape[axis_at] // blocks).reshape((-1,) + (1,) * (len(shape) - axis_at - 1))

    level = one(*shards[0])
    for cut in shards[1:]:
        level = level * one(*cut)
    return level


def noise(stream_key, extent, deviation, reach, shards=(), kind=jnp.bfloat16):
    array = deviation * jax.random.normal(stream_key, extent, jnp.float32)
    if shards:
        array = array * block_levels(stream_key, extent, shards, -0.22, 0.18)
    return jnp.clip(array, -reach, reach).astype(kind)


def setup_inputs(seed: int = 0) -> dict:
    seeds = jax.random.split(jax.random.key(seed), 7)
    cotangent = noise(seeds[0], (2, NX, NY, NZ), 1.0, 6.0, ((1, 4), (2, 64)), jnp.float32)
    head = noise(seeds[1], (NX, NY, NZ), 1.0, 6.0, ((0, 4), (1, 64)), jnp.float32)
    materials = with_ends(jax.random.randint(seeds[2], (NX, NY, NZ), 0, NMAT), jax.random.fold_in(seeds[2], 1), 0, NMAT - 1).astype(jnp.int32)
    flags = with_ends((jax.random.randint(seeds[3], (3, NX, NY, NZ), 0, 2) < 1).astype(jnp.int32), jax.random.fold_in(seeds[3], 1), 0, 1)
    perm_table = jnp.clip(jnp.exp(jax.random.uniform(seeds[4], (NMAT,), jnp.float32, math.log(0.3), math.log(3.0))), 0.3, 3.0)
    poro_table = jnp.clip(jax.random.uniform(seeds[5], (NMAT,), jnp.float32, 0.1, 0.45), 0.1, 0.45)
    return dict(cotangent=cotangent, head=head, materials=materials, flags=flags, perm_table=perm_table, poro_table=poro_table)


DISP = 0.2
CPL_P = 0.5
CPL_S = 0.3
OMEGA = 0.7
OMEGA_C = 0.7
THETA = 0.5


def lookup(mats, table):
    total = jnp.zeros(mats.shape, jnp.float32)
    for level in range(table.shape[0]):
        total = total + jnp.where(mats == level, table[level], 0.0)
    return total


def pad_xy(arr, width):
    spec = [(0, 0)] * (arr.ndim - 3) + [(width, width), (width, width), (0, 0)]
    return jnp.pad(arr, spec)


def pad_plane(arr):
    return pad_xy(arr, 1)


def shift_down(arr):
    return jnp.concatenate([arr[..., 1:], jnp.zeros_like(arr[..., :1])], axis=-1)


def shift_up(arr):
    return jnp.concatenate([jnp.zeros_like(arr[..., :1]), arr[..., :-1]], axis=-1)


def build_faces(perm_pad, head_pad, flags):
    perm_mid = perm_pad[1:-1, 1:-1]
    head_mid = head_pad[1:-1, 1:-1]
    others = [(perm_pad[2:, 1:-1], head_pad[2:, 1:-1]), (perm_pad[1:-1, 2:], head_pad[1:-1, 2:]), (shift_down(perm_mid), shift_down(head_mid))]
    parts = []
    for axis_num in range(3):
        perm_next, head_next = others[axis_num]
        trans = 2.0 * perm_mid * perm_next / (perm_mid + perm_next)
        flux = trans * (0.5 + jnp.abs(head_mid - head_next))
        upwind = flags[axis_num].astype(jnp.float32)
        parts += [trans, upwind * flux, (1.0 - upwind) * flux]
    return jnp.stack(parts)


def face_pair(faces_pad, member, axis_num):
    arr = faces_pad[member]
    middle = arr[1:-1, 1:-1]
    if axis_num == 0:
        below = arr[:-2, 1:-1]
    elif axis_num == 1:
        below = arr[1:-1, :-2]
    else:
        below = shift_up(middle)
    return middle, below


def neighbour(field_pad, axis_num):
    middle = field_pad[1:-1, 1:-1]
    if axis_num == 0:
        return field_pad[2:, 1:-1], field_pad[:-2, 1:-1]
    if axis_num == 1:
        return field_pad[1:-1, 2:], field_pad[1:-1, :-2]
    return shift_down(middle), shift_up(middle)


def build_diag(faces_pad, poro):
    trans_total = jnp.zeros_like(poro)
    out_flow = jnp.zeros_like(poro)
    for axis_num in range(3):
        trans_here, trans_below = face_pair(faces_pad, 3 * axis_num, axis_num)
        upper_here, upper_below = face_pair(faces_pad, 3 * axis_num + 1, axis_num)
        lower_here, lower_below = face_pair(faces_pad, 3 * axis_num + 2, axis_num)
        trans_total = trans_total + trans_here + trans_below
        out_flow = out_flow + upper_here + lower_below
    return jnp.stack([poro + trans_total, -CPL_S * out_flow, CPL_P * poro, poro + DISP * trans_total + out_flow])


def apply_op(field_pad, faces_pad, diag):
    press_mid = field_pad[0, 1:-1, 1:-1]
    salt_mid = field_pad[1, 1:-1, 1:-1]
    out_press = diag[0] * press_mid + diag[1] * salt_mid
    out_salt = diag[2] * press_mid + diag[3] * salt_mid
    for axis_num in range(3):
        trans_here, trans_below = face_pair(faces_pad, 3 * axis_num, axis_num)
        upper_here, upper_below = face_pair(faces_pad, 3 * axis_num + 1, axis_num)
        lower_here, lower_below = face_pair(faces_pad, 3 * axis_num + 2, axis_num)
        press_above, press_below = neighbour(field_pad[0], axis_num)
        salt_above, salt_below = neighbour(field_pad[1], axis_num)
        out_press = out_press - trans_here * press_above - trans_below * press_below
        out_salt = out_salt - (DISP * trans_here + upper_here) * salt_above - (DISP * trans_below + lower_below) * salt_below
    return jnp.stack([out_press, out_salt])


def invert_blocks(diag, inside):
    determ = diag[0] * diag[3] - diag[1] * diag[2]
    determ = jnp.where(inside, determ, 1.0)
    scale = jnp.where(inside, 1.0 / determ, 0.0)
    return jnp.stack([diag[3] * scale, -diag[1] * scale, -diag[2] * scale, diag[0] * scale])


def apply_inverse(inverse, vec):
    return jnp.stack([inverse[0] * vec[0] + inverse[1] * vec[1], inverse[2] * vec[0] + inverse[3] * vec[1]])


def jacobi(rhs, faces_pad, diag, inverse, count, weight, rim_fn):
    correction = weight * apply_inverse(inverse, rhs)
    for sweep in range(count - 1):
        correction = correction + weight * apply_inverse(inverse, rhs - apply_op(rim_fn(correction), faces_pad, diag))
    return correction


def aggregate(arr):
    lead = arr.shape[:-3]
    sizes = arr.shape[-3:]
    blocks = arr.reshape(lead + (sizes[0] // AGG, AGG, sizes[1] // AGG, AGG, sizes[2] // AGG, AGG))
    count = len(lead)
    return blocks.sum(axis=(count + 1, count + 3, count + 5))


def prolong(coarse):
    sizes = coarse.shape[1:]
    grown = jnp.broadcast_to(coarse[:, :, None, :, None, :, None], (coarse.shape[0], sizes[0], AGG, sizes[1], AGG, sizes[2], AGG))
    return grown.reshape(coarse.shape[0], sizes[0] * AGG, sizes[1] * AGG, sizes[2] * AGG)


def split_faces(arr, axis_num):
    edge = (jnp.arange(arr.shape[axis_num]) % AGG) == AGG - 1
    shape = [1, 1, 1]
    shape[axis_num] = arr.shape[axis_num]
    edge = edge.reshape(tuple(shape))
    crossing = aggregate(jnp.where(edge, arr, 0.0))
    inner = aggregate(jnp.where(edge, 0.0, arr))
    return crossing, inner


def coarse_system(faces, diag):
    rows_coarse = faces.shape[1] // AGG
    keep_rows = ((jnp.arange(rows_coarse) % (CX // AGG)) != CX // AGG - 1).astype(jnp.float32)[:, None, None]
    coarse_faces = []
    inner_press = 0.0
    inner_salt = 0.0
    for axis_num in range(3):
        for member in range(3):
            crossing, inner = split_faces(faces[3 * axis_num + member], axis_num)
            if axis_num == 0:
                crossing = crossing * keep_rows
            coarse_faces.append(crossing)
            if member == 0:
                inner_press = inner_press + 2.0 * inner
                inner_salt = inner_salt + 2.0 * DISP * inner
            else:
                inner_salt = inner_salt + inner
    summed = aggregate(diag)
    coarse_diag = jnp.stack([summed[0] - inner_press, summed[1], summed[2], summed[3] - inner_salt])
    return jnp.stack(coarse_faces), coarse_diag


def reference(cotangent, head, materials, flags, perm_table, poro_table):
    perm = lookup(materials, perm_table)
    poro = lookup(materials, poro_table)
    faces = build_faces(pad_xy(perm, 1), pad_xy(head, 1), flags)
    faces_one = pad_xy(faces, 1)
    diag = build_diag(faces_one, poro)
    faces_two = pad_xy(faces, 2)
    diag_one = pad_xy(diag, 1)
    poro_one = pad_xy(poro, 1)
    inverse_one = invert_blocks(diag_one, poro_one > 0)
    coarse_faces, coarse_diag = coarse_system(faces, diag)
    coarse_inverse = invert_blocks(coarse_diag, coarse_diag[0] > 0)
    coarse_faces_pad = pad_xy(coarse_faces, 1)
    zero = jnp.int32(0)

    adjoint = jnp.zeros(cotangent.shape, jnp.float32)
    for step in range(ITERS):
        residual = cotangent - apply_op(pad_xy(adjoint, 1), faces_one, diag)
        resid_one = pad_xy(residual, 1)

        def solve_block(block):
            start_x = (block // N_SUB) * CX
            start_y = (block % N_SUB) * CY
            region_rhs = lax.dynamic_slice(resid_one, (zero, start_x, start_y, zero), (2, CX + 2, CY + 2, NZ))
            region_faces = lax.dynamic_slice(faces_two, (zero, start_x, start_y, zero), (9, CX + 4, CY + 4, NZ))
            region_diag = lax.dynamic_slice(diag_one, (zero, start_x, start_y, zero), (4, CX + 2, CY + 2, NZ))
            region_inv = lax.dynamic_slice(inverse_one, (zero, start_x, start_y, zero), (4, CX + 2, CY + 2, NZ))
            solved = jacobi(region_rhs, region_faces, region_diag, region_inv, SWEEPS, OMEGA, pad_plane)
            return solved[:, 1:-1, 1:-1]

        blocks = lax.map(solve_block, jnp.arange(N_GRP * N_SUB, dtype=jnp.int32))
        fine = blocks.reshape(N_GRP, N_SUB, 2, CX, CY, NZ).transpose(2, 0, 3, 1, 4, 5).reshape(2, NX, NY, NZ)
        coarse_res = aggregate(residual)
        coarse_sol = jacobi(coarse_res, coarse_faces_pad, coarse_diag, coarse_inverse, CSWEEPS, OMEGA_C, pad_plane)
        adjoint = adjoint + THETA * (fine + prolong(coarse_sol))
    return adjoint
```

```python
import functools

import jax
import jax.numpy as jnp
from jax import lax
from jax.experimental import pallas as pl
from jax.experimental.pallas import tpu as pltpu
from jax.sharding import PartitionSpec as P

CX = 8
AGG = 4
ITERS = 4
DISP = 0.2
CPL_P = 0.5
CPL_S = 0.3
OMEGA = 0.7
OMEGA_C = 0.7
THETA = 0.5

PITCH = 12
BASE = 8
ROWS = 160
LANES = 128
MESH = pl.DeviceIdType.MESH

SIDES = [(-1, 0), (1, 0), (0, -1), (0, 1), (-1, -1), (-1, 1), (1, -1), (1, 1)]
NEAR = [-1, 1, -2, 2]

MAT, HEAD, F0, F1, F2, COT = 0, 1, 2, 3, 4, 5
TX, TXM, TY, TYM, TZ, TZM, SX, SXM, SY, SYM, SZ, SZM, BPP, BPC, BCP, BCC, IPP, IPC, ICP, ICC = range(20)
N_COEF = 20
N_CBLK = 13
C_ROWS = 56


def row(x, y):
    return BASE + (x + 2) * PITCH + y + 2


def rows(x, y, count=8):
    return pl.ds(row(x, y), count)


def column(y):
    return pl.ds(row(0, y), 8, stride=PITCH)


def setup_slots(low, along):
    if low:
        pairs = [(MAT, -2), (MAT, -1), (HEAD, -2), (HEAD, -1), (along, -2)]
        one = -1
    else:
        pairs = [(MAT, 8), (MAT, 9), (HEAD, 8), (HEAD, 9)]
        one = 8
    return pairs + [(field, one) for field in (F0, F1, F2, COT, COT + 1)]


def field_slots(low):
    return [(f, layer) for f in (0, 1) for layer in ((-2, -1) if low else (8, 9))]


def slots_of(side, setup):
    dx, dy = side
    if dx != 0:
        return setup_slots(dx < 0, F0) if setup else field_slots(dx < 0)
    return setup_slots(dy < 0, F1) if setup else field_slots(dy < 0)


def pack(side, setup, src, dst, lead):
    dx, dy = side
    for slot, (field, layer) in enumerate(slots_of(side, setup)):
        if dy == 0:
            dst[lead + (pl.ds(8 * slot, 8),)] = src[field, rows(layer % 8, 0), :]
        elif dx == 0:
            dst[lead + (pl.ds(8 * slot, 8),)] = src[field, column(layer % 8), :]
        else:
            dst[lead + (pl.ds(2 * slot, 2),)] = src[field, rows(layer % 8, 6 if dy < 0 else 0, 2), :]


def unpack(side, setup, src, lead, dst, valid):
    dx, dy = side

    def seen(field, value):
        return jnp.where(valid, value, -1.0) if setup and field == MAT else value

    for slot, (field, layer) in enumerate(slots_of(side, setup)):
        if dy == 0:
            dst[field, rows(layer, 0), :] = seen(field, src[lead + (pl.ds(8 * slot, 8),)])
        elif dx == 0:
            dst[field, column(layer), :] = seen(field, src[lead + (pl.ds(8 * slot, 8),)])
        else:
            dst[field, rows(layer, -2 if dy < 0 else 8, 2), :] = seen(field, src[lead + (pl.ds(2 * slot, 2),)])


def next_lane(value, by=1):
    return pltpu.roll(value, LANES - by, 1)


def last_lane(value, by=1):
    return pltpu.roll(value, by, 1)


def lane_sum(value):
    lane = lax.broadcasted_iota(jnp.int32, value.shape, 1)
    total = value + next_lane(value)
    total = total + next_lane(total, 2)
    total = jnp.where(lane % AGG == 0, total, 0.0)
    total = total + last_lane(total)
    return total + last_lane(total, 2)


def four_sum(value):
    total = value + pltpu.roll(value, 7, 0)
    return total + pltpu.roll(total, 6, 0)


def couple(co, field, lo, n):
    here = pl.ds(lo, n)
    out = []
    for f, first in ((0, TX), (1, SX)):
        mid = field[f, here, :]
        total = co[first, here, :] * field[f, pl.ds(lo + PITCH, n), :]
        total = total + co[first + 1, here, :] * field[f, pl.ds(lo - PITCH, n), :]
        total = total + co[first + 2, here, :] * field[f, pl.ds(lo + 1, n), :]
        total = total + co[first + 3, here, :] * field[f, pl.ds(lo - 1, n), :]
        total = total + co[first + 4, here, :] * next_lane(mid)
        total = total + co[first + 5, here, :] * last_lane(mid)
        out += [mid, total]
    return out


def kernel(
    n_grp,
    n_sub,
    cot_ref,
    head_ref,
    mat_ref,
    flag_ref,
    perm_tab,
    poro_tab,
    out_ref,
    ext,
    perm,
    poro,
    mask,
    face,
    co,
    adj,
    res,
    grd,
    mid,
    fin,
    ssend,
    srecv,
    hsend,
    hrecv,
    ksend,
    krecv,
    cagg,
    cco,
    csend,
    crecv,
    cres,
    s_send,
    s_recv,
    h_send,
    h_recv,
    k_send,
    k_recv,
    c_send,
    c_recv,
):
    g = lax.axis_index("grp")
    s = lax.axis_index("sub")

    def device(dx, dy):
        return {"grp": lax.rem(g + dx + n_grp, n_grp), "sub": lax.rem(s + dy + n_sub, n_sub)}

    barrier = pltpu.get_barrier_semaphore()
    partners = SIDES + [(0, -2), (0, 2)]
    for dx, dy in partners:
        pl.semaphore_signal(barrier, inc=1, device_id=device(dx, dy), device_id_type=MESH)

    zero_rows = jnp.zeros((ROWS, LANES), jnp.float32)
    ext[MAT] = zero_rows - 1.0
    for f in range(1, 7):
        ext[f] = zero_rows
    mask[...] = zero_rows
    for f in range(2):
        adj[f] = zero_rows
        grd[f] = zero_rows
        mid[f] = zero_rows
    for x in range(8):
        ext[MAT, rows(x, 0), :] = mat_ref[x].astype(jnp.float32)
        ext[HEAD, rows(x, 0), :] = head_ref[x]
        for d in range(3):
            ext[F0 + d, rows(x, 0), :] = flag_ref[d, x].astype(jnp.float32)
        for f in range(2):
            ext[COT + f, rows(x, 0), :] = cot_ref[f, x]
    for i, side in enumerate(SIDES):
        pack(side, True, ext, ssend, (i,))
    for x in range(-1, 9):
        mask[rows(x, -1, 10), :] = jnp.ones((10, LANES), jnp.float32)

    def exchange(i, setup, k):
        dx, dy = SIDES[i]
        count = len(slots_of((dx, dy), setup)) * (2 if dx != 0 and dy != 0 else 8)
        part = pl.ds(0, -(-count // 8) * 8)
        if setup:
            refs = (ssend.at[i, part], srecv.at[i, part], s_send.at[i], s_recv.at[i])
        else:
            refs = (hsend.at[k, i, part], hrecv.at[k, i, part], h_send.at[k, i], h_recv.at[k, i])
        return pltpu.make_async_remote_copy(*refs, device_id=device(-dx, -dy), device_id_type=MESH)

    def coarse_copy(j, k):
        return pltpu.make_async_remote_copy(
            csend.at[k], crecv.at[k, j], c_send.at[k, j], c_recv.at[k, j], device_id=device(0, -NEAR[j]), device_id_type=MESH
        )

    def coef_copy(j):
        return pltpu.make_async_remote_copy(
            ksend, krecv.at[j], k_send.at[j], k_recv.at[j], device_id=device(0, -NEAR[j]), device_id_type=MESH
        )

    pl.semaphore_wait(barrier, len(partners))
    for i in range(8):
        exchange(i, True, 0).start()

    def send_coarse(k, src, at):
        for f in range(2):
            for cx in range(2):
                total = src[at + f, rows(4 * cx, 0), :]
                for x in range(4 * cx + 1, 4 * cx + 4):
                    total = total + src[at + f, rows(x, 0), :]
                total = four_sum(total)
                first = 4 * f + 2 * cx
                cagg[pl.ds(first, 1), :] = total[0:1]
                cagg[pl.ds(first + 1, 1), :] = total[4:5]
        csend[k] = lane_sum(cagg[pl.ds(0, 8), :])
        for j in range(4):
            coarse_copy(j, k).start()

    send_coarse(0, ext, COT)

    for i, (dx, dy) in enumerate(SIDES):
        exchange(i, True, 0).wait_recv()
        fits = None
        for there, count, step in ((g, n_grp, dx), (s, n_sub, dy)):
            if step != 0:
                one = (there > 0) if step < 0 else (there < count - 1)
                fits = one if fits is None else jnp.logical_and(fits, one)
        unpack((dx, dy), True, srecv, (i,), ext, fits)

    for lo in range(0, ROWS, 32):
        here = pl.ds(lo, 32)
        mats = ext[MAT, here, :]
        perm_here = jnp.zeros_like(mats)
        poro_here = jnp.zeros_like(mats)
        for level in range(perm_tab.shape[0]):
            same = mats == float(level)
            perm_here = jnp.where(same, perm_tab[level], perm_here)
            poro_here = jnp.where(same, poro_tab[level], poro_here)
        perm[here, :] = perm_here
        poro[here, :] = poro_here

    for lo in range(0, 144, 24):
        here = pl.ds(lo, 24)
        perm_here, head_here = perm[here, :], ext[HEAD, here, :]
        lane = lax.broadcasted_iota(jnp.int32, (24, LANES), 1)
        for d in range(3):
            if d < 2:
                there = pl.ds(lo + (PITCH, 1)[d], 24)
                perm_next, head_next = perm[there, :], ext[HEAD, there, :]
            else:
                perm_next = jnp.where(lane == LANES - 1, 0.0, next_lane(perm_here))
                head_next = jnp.where(lane == LANES - 1, 0.0, next_lane(head_here))
            both = perm_here + perm_next
            trans = 2.0 * perm_here * perm_next / jnp.where(both > 0.0, both, 1.0)
            flux = trans * (0.5 + jnp.abs(head_here - head_next))
            upwind = ext[F0 + d, here, :]
            face[3 * d, here, :] = trans
            face[3 * d + 1, here, :] = upwind * flux
            face[3 * d + 2, here, :] = (1.0 - upwind) * flux

    for lo in range(16, 144, 16):
        here = pl.ds(lo, 16)
        total = jnp.zeros((16, LANES), jnp.float32)
        out = total
        for d in range(3):
            trans, upper, lower = (face[3 * d + m, here, :] for m in range(3))
            if d < 2:
                back = pl.ds(lo - (PITCH, 1)[d], 16)
                trans_m, lower_m = face[3 * d, back, :], face[3 * d + 2, back, :]
            else:
                trans_m, lower_m = last_lane(trans), last_lane(lower)
            co[TX + 2 * d, here, :] = trans
            co[TX + 2 * d + 1, here, :] = trans_m
            co[SX + 2 * d, here, :] = DISP * trans + upper
            co[SX + 2 * d + 1, here, :] = DISP * trans_m + lower_m
            total = total + trans + trans_m
            out = out + upper + lower_m
        store = poro[here, :]
        bpp, bpc, bcp, bcc = store + total, -CPL_S * out, CPL_P * store, store + DISP * total + out
        inside = jnp.logical_and(store > 0.0, mask[here, :] > 0.0)
        determ = jnp.where(inside, bpp * bcc - bpc * bcp, 1.0)
        scale = jnp.where(inside, OMEGA / determ, 0.0)
        for at, value in (
            (BPP, bpp), (BPC, bpc), (BCP, bcp), (BCC, bcc),
            (IPP, bcc * scale), (IPC, -bpc * scale), (ICP, -bcp * scale), (ICC, bpp * scale),
        ):
            co[at, here, :] = value

    def put(block, cx, cy, value):
        cagg[pl.ds(4 * block + 2 * cx + cy, 1), :] = value

    lane = lax.broadcasted_iota(jnp.int32, (8, LANES), 1)
    for cx in range(2):
        xs = range(4 * cx, 4 * cx + 4)
        store = poro[rows(4 * cx, 0), :]
        out = co[BPC, rows(4 * cx, 0), :]
        zs = [face[6 + m, rows(4 * cx, 0), :] for m in range(3)]
        for x in xs[1:]:
            store = store + poro[rows(x, 0), :]
            out = out + co[BPC, rows(x, 0), :]
            zs = [zs[m] + face[6 + m, rows(x, 0), :] for m in range(3)]
        zs = [jnp.where(lane % AGG == AGG - 1, z, 0.0) for z in zs]
        for block, value in ((0, store), (1, out), (12, zs[0]), (13, zs[1]), (14, zs[2])):
            value = four_sum(value)
            put(block, cx, 0, value[0:1])
            put(block, cx, 1, value[4:5])
    for d in range(2):
        first = 2 + 5 * d
        for member, ahead, behind in ((0, 0, 1), (1, 2, None), (2, 3, 4)):
            for place, edge in enumerate((-1, 3, 7)):
                if d == 0:
                    value = four_sum(face[member, rows(edge, 0), :])
                else:
                    value = four_sum(face[3 + member, column(edge), :])
                for other in range(2):
                    piece = value[4 * other : 4 * other + 1]
                    if place > 0:
                        cell = (place - 1, other) if d == 0 else (other, place - 1)
                        put(first + ahead, *cell, piece)
                    if place < 2 and behind is not None:
                        cell = (place, other) if d == 0 else (other, place)
                        put(first + behind, *cell, piece)
    cagg[pl.ds(60, 4), :] = jnp.zeros((4, LANES), jnp.float32)
    cagg[...] = lane_sum(cagg[...])

    def block(b):
        return cagg[pl.ds(4 * b, 4), :]

    store, cpc = block(0), block(1)
    t_z, a_z, b_z = block(12), block(13), block(14)
    edge_sum = block(2) + block(3) + block(7) + block(8) + t_z + last_lane(t_z, AGG)
    edge_out = block(4) + block(6) + block(9) + block(11) + a_z + last_lane(b_z, AGG)
    cpp, ccp, ccc = store + edge_sum, CPL_P * store, store + DISP * edge_sum + edge_out
    scale = OMEGA_C / (cpp * ccc - cpc * ccp)
    t_x, t_y = block(2), block(7)
    for b, value in enumerate((
        ccc * scale, -cpc * scale, -ccp * scale, cpp * scale,
        t_y, DISP * t_y + block(9), DISP * t_y + block(10),
        t_z, DISP * t_z + a_z, DISP * t_z + b_z,
        t_x, DISP * t_x + block(4), DISP * t_x + block(5),
    )):
        ksend[pl.ds(4 * b, 4), :] = value
    ksend[pl.ds(52, 4), :] = jnp.zeros((4, LANES), jnp.float32)
    for j in range(4):
        coef_copy(j).start()

    def spread(count, own, recv, dst):
        for item in range(count):
            dst(item, pl.ds(3, 2), own(pl.ds(2 * item, 2)))
            dst(item, pl.ds(1, 2), recv(0, pl.ds(2 * item, 2)))
            dst(item, pl.ds(5, 2), recv(1, pl.ds(2 * item, 2)))
            dst(item, pl.ds(0, 1), recv(2, pl.ds(2 * item + 1, 1)))
            dst(item, pl.ds(7, 1), recv(3, pl.ds(2 * item, 1)))

    def fine_solve(src, at):
        for lo in range(16, 144, 32):
            here = pl.ds(lo, 32)
            r_p, r_c = src[at, here, :], src[at + 1, here, :]
            grd[0, here, :] = co[IPP, here, :] * r_p + co[IPC, here, :] * r_c
            grd[1, here, :] = co[ICP, here, :] * r_p + co[ICC, here, :] * r_c
        for lo in range(16, 144, 16):
            here = pl.ds(lo, 16)
            z_p, s_p, z_c, s_c = couple(co, grd, lo, 16)
            mid[0, here, :] = (2.0 - OMEGA) * z_p + co[IPP, here, :] * s_p + co[IPC, here, :] * s_c
            mid[1, here, :] = (2.0 - OMEGA) * z_c + co[ICP, here, :] * s_p + co[ICC, here, :] * s_c
        for lo in range(32, 128, 16):
            here = pl.ds(lo, 16)
            z_p, s_p, z_c, s_c = couple(co, mid, lo, 16)
            fin[0, here, :] = (1.0 - OMEGA) * z_p + grd[0, here, :] + co[IPP, here, :] * s_p + co[IPC, here, :] * s_c
            fin[1, here, :] = (1.0 - OMEGA) * z_c + grd[1, here, :] + co[ICP, here, :] * s_p + co[ICC, here, :] * s_c

    def coarse_solve(k):
        for j in range(4):
            coarse_copy(j, k).wait_recv()

        def dst(item, where, value):
            cres[item, where, :] = value

        spread(4, lambda part: csend[k, part, :], lambda j, part: crecv[k, j, part, :], dst)
        ipp, ipc, icp, icc = ([cco[b, cx] for cx in range(2)] for b in range(4))
        t_y, a_y, b_y, t_z, a_z, b_z = ([cco[b, cx] for cx in range(2)] for b in range(4, 10))
        t_x, a_x, b_x = (cco[b, 0] for b in range(10, 13))
        ahead = {0: (t_y, t_z), 1: (a_y, a_z)}
        behind = {
            0: ([pltpu.roll(v, 1, 0) for v in t_y], [last_lane(v, AGG) for v in t_z]),
            1: ([pltpu.roll(v, 1, 0) for v in b_y], [last_lane(v, AGG) for v in b_z]),
        }
        across = {0: (t_x, t_x), 1: (a_x, b_x)}
        r = [[cres[2 * f + cx] for cx in range(2)] for f in range(2)]
        base = [
            [ipp[cx] * r[0][cx] + ipc[cx] * r[1][cx] for cx in range(2)],
            [icp[cx] * r[0][cx] + icc[cx] * r[1][cx] for cx in range(2)],
        ]
        z = base
        for sweep in range(3):
            acc = [[None] * 2 for f in range(2)]
            for f in range(2):
                for cx in range(2):
                    v = z[f][cx]
                    total = across[f][cx] * z[f][1 - cx]
                    total = total + ahead[f][0][cx] * pltpu.roll(v, 7, 0)
                    total = total + behind[f][0][cx] * pltpu.roll(v, 1, 0)
                    total = total + ahead[f][1][cx] * next_lane(v, AGG)
                    acc[f][cx] = total + behind[f][1][cx] * last_lane(v, AGG)
            z = [
                [(1.0 - OMEGA_C) * z[0][cx] + base[0][cx] + ipp[cx] * acc[0][cx] + ipc[cx] * acc[1][cx] for cx in range(2)],
                [(1.0 - OMEGA_C) * z[1][cx] + base[1][cx] + icp[cx] * acc[0][cx] + icc[cx] * acc[1][cx] for cx in range(2)],
            ]
        upper = lax.broadcasted_iota(jnp.int32, (8, LANES), 0) < AGG
        return [
            [
                jnp.where(upper, jnp.broadcast_to(v[3:4], (8, LANES)), jnp.broadcast_to(v[4:5], (8, LANES)))
                for v in z[f]
            ]
            for f in range(2)
        ]

    def update(k, last):
        grown = coarse_solve(k)
        for f in range(2):
            for x in range(8):
                here = rows(x, 0)
                new = adj[f, here, :] + THETA * (fin[f, here, :] + grown[f][x // 4])
                if last:
                    out_ref[f, x] = new
                else:
                    adj[f, here, :] = new

    def refresh(k):
        for i, side in enumerate(SIDES):
            pack(side, False, adj, hsend, (k, i))
            exchange(i, False, k).start()
        for i, side in enumerate(SIDES):
            exchange(i, False, k).wait_recv()
            unpack(side, False, hrecv, (k, i), adj, None)
        for lo in range(16, 144, 16):
            here = pl.ds(lo, 16)
            z_p, s_p, z_c, s_c = couple(co, adj, lo, 16)
            res[0, here, :] = ext[COT, here, :] + s_p - co[BPP, here, :] * z_p - co[BPC, here, :] * z_c
            res[1, here, :] = ext[COT + 1, here, :] + s_c - co[BCP, here, :] * z_p - co[BCC, here, :] * z_c

    fine_solve(ext, COT)

    def coef_dst(item, where, value):
        cco[item // 2, item % 2, where, :] = value

    for j in range(4):
        coef_copy(j).wait_recv()
    spread(2 * N_CBLK, lambda part: ksend[part, :], lambda j, part: krecv[j, part, :], coef_dst)
    update(0, False)
    refresh(0)

    def step(k, carry):
        send_coarse(k, res, 0)
        fine_solve(res, 0)
        update(k, False)
        refresh(k)
        return carry

    lax.fori_loop(1, ITERS - 1, step, 0)
    send_coarse(ITERS - 1, res, 0)
    fine_solve(res, 0)
    update(ITERS - 1, True)

    for i in range(8):
        exchange(i, True, 0).wait_send()
        for k in range(ITERS - 1):
            exchange(i, False, k).wait_send()
    for j in range(4):
        coef_copy(j).wait_send()
        for k in range(ITERS):
            coarse_copy(j, k).wait_send()


def solution(mesh):
    n_grp, n_sub = mesh.shape["grp"], mesh.shape["sub"]

    def local(cotangent, head, materials, flags, perm_table, poro_table):
        def tile(*shape):
            return pltpu.VMEM(shape + (LANES,), jnp.float32)

        dma = pltpu.SemaphoreType.DMA
        vmem = pl.BlockSpec(memory_space=pltpu.VMEM)
        smem = pl.BlockSpec(memory_space=pltpu.SMEM)
        return pl.pallas_call(
            functools.partial(kernel, n_grp, n_sub),
            out_shape=jax.ShapeDtypeStruct(cotangent.shape, jnp.float32),
            in_specs=[vmem] * 4 + [smem] * 2,
            out_specs=vmem,
            scratch_shapes=[
                tile(7, ROWS),
                tile(ROWS),
                tile(ROWS),
                tile(ROWS),
                tile(9, ROWS),
                tile(N_COEF, ROWS),
                tile(2, ROWS),
                tile(2, ROWS),
                tile(2, ROWS),
                tile(2, ROWS),
                tile(2, ROWS),
                tile(8, 80),
                tile(8, 80),
                tile(ITERS - 1, 8, 32),
                tile(ITERS - 1, 8, 32),
                tile(C_ROWS),
                tile(4, C_ROWS),
                tile(64),
                tile(N_CBLK, 2, 8),
                tile(ITERS, 8),
                tile(ITERS, 4, 8),
                tile(4, 8),
                dma((8,)),
                dma((8,)),
                dma((ITERS - 1, 8)),
                dma((ITERS - 1, 8)),
                dma((4,)),
                dma((4,)),
                dma((ITERS, 4)),
                dma((ITERS, 4)),
            ],
            compiler_params=pltpu.CompilerParams(
                collective_id=0, has_side_effects=True, vmem_limit_bytes=32 * 1024 * 1024
            ),
        )(cotangent, head, materials, flags, perm_table, poro_table)

    return jax.shard_map(
        local,
        mesh=mesh,
        in_specs=(
            P(None, "grp", "sub", None),
            P("grp", "sub", None),
            P("grp", "sub", None),
            P(None, "grp", "sub", None),
            P(),
            P(),
        ),
        out_specs=P(None, "grp", "sub", None),
        check_vma=False,
    )
```

```python
import functools

import jax
import jax.numpy as jnp
from jax import lax
from jax.experimental import pallas as pl
from jax.experimental.pallas import tpu as pltpu
from jax.sharding import PartitionSpec as P

CX = 8
AGG = 4
ITERS = 4
DISP = 0.2
CPL_P = 0.5
CPL_S = 0.3
OMEGA = 0.7
OMEGA_C = 0.7
THETA = 0.5

PITCH = 12
BASE = 8
ROWS = 160
LANES = 128
MESH = pl.DeviceIdType.MESH

SIDES = [(-1, 0), (1, 0), (0, -1), (0, 1), (-1, -1), (-1, 1), (1, -1), (1, 1)]
FAR = [(-1, -2), (-1, 2), (1, -2), (1, 2), (0, -2), (0, 2)]
PARTNERS = FAR + SIDES[4:] + SIDES[:4]
NEAR = [(0, -2), (0, 2), (0, -1), (0, 1)]

MAT, HEAD, F0, F1, F2, COT = 0, 1, 2, 3, 4, 5
TX, TXM, TY, TYM, TZ, TZM, SX, SXM, SY, SYM, SZ, SZM, BPP, BPC, BCP, BCC, IPP, IPC, ICP, ICC = range(20)
N_COEF = 20
N_CBLK = 13
C_ROWS = 64
ROUNDS = ITERS - 1


def row(x, y):
    return BASE + (x + 2) * PITCH + y + 2


def rows(x, y, count=8):
    return pl.ds(row(x, y), count)


def column(y):
    return pl.ds(row(0, y), 8, stride=PITCH)


def setup_slots(low, along):
    if low:
        pairs = [(MAT, -2), (MAT, -1), (HEAD, -2), (HEAD, -1), (along, -2)]
        one = -1
    else:
        pairs = [(MAT, 8), (MAT, 9), (HEAD, 8), (HEAD, 9)]
        one = 8
    return pairs + [(field, one) for field in (F0, F1, F2, COT, COT + 1)]


def field_slots(low):
    return [(f, layer) for f in (0, 1) for layer in ((-2, -1) if low else (8, 9))]


def slots_of(side, setup):
    dx, dy = side
    if dx != 0:
        return setup_slots(dx < 0, F0) if setup else field_slots(dx < 0)
    return setup_slots(dy < 0, F1) if setup else field_slots(dy < 0)


def pack(side, setup, src, dst, lead):
    dx, dy = side
    for slot, (field, layer) in enumerate(slots_of(side, setup)):
        if dy == 0:
            dst[lead + (pl.ds(8 * slot, 8),)] = src[field, rows(layer % 8, 0), :]
        elif dx == 0:
            dst[lead + (pl.ds(8 * slot, 8),)] = src[field, column(layer % 8), :]
        else:
            dst[lead + (pl.ds(2 * slot, 2),)] = src[field, rows(layer % 8, 6 if dy < 0 else 0, 2), :]


def unpack(side, setup, src, lead, dst, valid):
    dx, dy = side

    def seen(field, value):
        return jnp.where(valid, value, -1.0) if setup and field == MAT else value

    for slot, (field, layer) in enumerate(slots_of(side, setup)):
        if dy == 0:
            dst[field, rows(layer, 0), :] = seen(field, src[lead + (pl.ds(8 * slot, 8),)])
        elif dx == 0:
            dst[field, column(layer), :] = seen(field, src[lead + (pl.ds(8 * slot, 8),)])
        else:
            dst[field, rows(layer, -2 if dy < 0 else 8, 2), :] = seen(field, src[lead + (pl.ds(2 * slot, 2),)])


def next_lane(value, by=1):
    return pltpu.roll(value, LANES - by, 1)


def last_lane(value, by=1):
    return pltpu.roll(value, by, 1)


def lane_sum(value):
    lane = lax.broadcasted_iota(jnp.int32, value.shape, 1)
    total = value + next_lane(value)
    total = total + next_lane(total, 2)
    total = jnp.where(lane % AGG == 0, total, 0.0)
    total = total + last_lane(total)
    return total + last_lane(total, 2)


def four_sum(value):
    total = value + pltpu.roll(value, 7, 0)
    return total + pltpu.roll(total, 6, 0)


def couple(co, field, lo, n):
    here = pl.ds(lo, n)
    out = []
    for f, first in ((0, TX), (1, SX)):
        mid = field[f, here, :]
        total = co[first, here, :] * field[f, pl.ds(lo + PITCH, n), :]
        total = total + co[first + 1, here, :] * field[f, pl.ds(lo - PITCH, n), :]
        total = total + co[first + 2, here, :] * field[f, pl.ds(lo + 1, n), :]
        total = total + co[first + 3, here, :] * field[f, pl.ds(lo - 1, n), :]
        total = total + co[first + 4, here, :] * next_lane(mid)
        total = total + co[first + 5, here, :] * last_lane(mid)
        out += [mid, total]
    return out


def kernel(
    n_grp,
    n_sub,
    cot_hbm,
    head_hbm,
    mat_hbm,
    flag_hbm,
    perm_hbm,
    poro_hbm,
    out_ref,
    cot_ref,
    head_ref,
    mat_ref,
    flag_ref,
    perm_tab,
    poro_tab,
    ext,
    perm,
    poro,
    mask,
    face,
    co,
    adj,
    inc,
    res,
    grd,
    mid,
    fin,
    ssend,
    srecv,
    rsend,
    rrecv,
    ksend,
    krecv,
    cagg,
    ring,
    cco,
    cres,
    layer,
    l_sem,
    s_send,
    s_recv,
    r_send,
    r_recv,
    k_send,
    k_recv,
):
    g = lax.axis_index("grp")
    s = lax.axis_index("sub")

    def device(dx, dy):
        return {"grp": lax.rem(g + dx + n_grp, n_grp), "sub": lax.rem(s + dy + n_sub, n_sub)}

    def fits(dx, dy):
        found = []
        for at, count, step in ((g, n_grp, dx), (s, n_sub, dy)):
            if step < 0:
                found.append(at >= -step)
            elif step > 0:
                found.append(at < count - step)
        return found[0] if len(found) == 1 else jnp.logical_and(*found)

    loads = [
        pltpu.make_async_copy(src, dst, l_sem.at[i])
        for i, (src, dst) in enumerate((
            (mat_hbm, mat_ref), (head_hbm, head_ref), (flag_hbm, flag_ref), (cot_hbm, cot_ref), (perm_hbm, perm_tab), (poro_hbm, poro_tab)
        ))
    ]
    for load in loads:
        load.start()

    barrier = pltpu.get_barrier_semaphore()
    expected = jnp.int32(0)
    for dx, dy in PARTNERS:
        there = fits(dx, dy)

        @pl.when(there)
        def _():
            pl.semaphore_signal(barrier, inc=1, device_id=device(dx, dy), device_id_type=MESH)

        expected = expected + there.astype(jnp.int32)

    def rows_of(side, setup):
        dx, dy = side
        if side in FAR:
            return 0
        if setup:
            count = len(slots_of(side, True)) * (2 if dx != 0 and dy != 0 else 8)
            return -(-count // 8) * 8
        return 8 if dx != 0 and dy != 0 else 32

    def setup_copy(i):
        dx, dy = SIDES[i]
        part = pl.ds(0, rows_of((dx, dy), True))
        return pltpu.make_async_remote_copy(
            ssend.at[i, part], srecv.at[i, part], s_send.at[i], s_recv.at[i], device_id=device(-dx, -dy), device_id_type=MESH
        )

    def round_copy(i, k):
        dx, dy = PARTNERS[i]
        part = pl.ds(0, rows_of((dx, dy), False) + (16 if dx == 0 else 8))
        return pltpu.make_async_remote_copy(
            rsend.at[k, i, part], rrecv.at[k, i, part], r_send.at[k, i], r_recv.at[k, i], device_id=device(-dx, -dy), device_id_type=MESH
        )

    def coef_copy(j):
        dx, dy = NEAR[j]
        return pltpu.make_async_remote_copy(
            ksend, krecv.at[j], k_send.at[j], k_recv.at[j], device_id=device(-dx, -dy), device_id_type=MESH
        )

    def when_sent(side, act):
        pl.when(fits(-side[0], -side[1]))(act)

    def when_there(side, act):
        pl.when(fits(*side))(act)

    zero_rows = jnp.zeros((ROWS, LANES), jnp.float32)
    ext[MAT] = zero_rows - 1.0
    for f in range(1, 7):
        ext[f] = zero_rows
    mask[...] = zero_rows
    perm[...] = zero_rows
    poro[...] = zero_rows
    for f in range(2):
        adj[f] = zero_rows
        inc[f] = zero_rows
        grd[f] = zero_rows
        mid[f] = zero_rows
    for m in range(9):
        face[m, pl.ds(0, 32), :] = jnp.zeros((32, LANES), jnp.float32)
    for x in range(-1, 9):
        mask[rows(x, -1, 10), :] = jnp.ones((10, LANES), jnp.float32)
    for i, side in enumerate(SIDES):

        @pl.when(jnp.logical_not(fits(*side)))
        def _():
            srecv[i] = jnp.zeros((80, LANES), jnp.float32)

    for i, side in enumerate(PARTNERS):

        @pl.when(jnp.logical_not(fits(*side)))
        def _():
            for k in range(ROUNDS):
                rrecv[k, i] = jnp.zeros((48, LANES), jnp.float32)

    for j, side in enumerate(NEAR):

        @pl.when(jnp.logical_not(fits(*side)))
        def _():
            krecv[j] = jnp.zeros((C_ROWS, LANES), jnp.float32)

    for load in loads:
        load.wait()
    for x in range(8):
        ext[MAT, rows(x, 0), :] = mat_ref[x].astype(jnp.float32)
        ext[HEAD, rows(x, 0), :] = head_ref[x]
        for d in range(3):
            ext[F0 + d, rows(x, 0), :] = flag_ref[d, x].astype(jnp.float32)
        for f in range(2):
            ext[COT + f, rows(x, 0), :] = cot_ref[f, x]
    for i, side in enumerate(SIDES):
        pack(side, True, ext, ssend, (i,))

    pl.semaphore_wait(barrier, expected)
    for i in reversed(range(8)):
        when_sent(SIDES[i], lambda: setup_copy(i).start())

    def look_up(mats):
        perm_here = jnp.zeros_like(mats)
        poro_here = jnp.zeros_like(mats)
        for level in range(perm_tab.shape[0]):
            same = mats == float(level)
            perm_here = jnp.where(same, perm_tab[level], perm_here)
            poro_here = jnp.where(same, poro_tab[level], poro_here)
        return perm_here, poro_here

    def one_face(perm_here, head_here, perm_next, head_next, upwind):
        both = perm_here + perm_next
        trans = 2.0 * perm_here * perm_next / jnp.where(both > 0.0, both, 1.0)
        flux = trans * (0.5 + jnp.abs(head_here - head_next))
        return trans, upwind * flux, (1.0 - upwind) * flux

    def look_up_rows(first, end, n):
        for lo in range(first, end, n):
            here = pl.ds(lo, n)
            perm[here, :], poro[here, :] = look_up(ext[MAT, here, :])

    def face_rows(first, end, n):
        for lo in range(first, end, n):
            here = pl.ds(lo, n)
            perm_here, head_here = perm[here, :], ext[HEAD, here, :]
            lane = lax.broadcasted_iota(jnp.int32, (n, LANES), 1)
            for d in range(3):
                if d < 2:
                    there = pl.ds(lo + (PITCH, 1)[d], n)
                    perm_next, head_next = perm[there, :], ext[HEAD, there, :]
                else:
                    perm_next = jnp.where(lane == LANES - 1, 0.0, next_lane(perm_here))
                    head_next = next_lane(head_here)
                values = one_face(perm_here, head_here, perm_next, head_next, ext[F0 + d, here, :])
                for m in range(3):
                    face[3 * d + m, here, :] = values[m]

    look_up_rows(32, 128, 32)
    face_rows(32, 128, 24)

    def put(block, cx, cy, value):
        cagg[pl.ds(4 * block + 2 * cx + cy, 1), :] = value

    def put_y(block, cx, value):
        value = four_sum(value)
        put(block, cx, 0, value[0:1])
        put(block, cx, 1, value[4:5])

    def put_x(block, cy, value):
        value = four_sum(value)
        put(block, 0, cy, value[0:1])
        put(block, 1, cy, value[4:5])

    cagg[...] = jnp.zeros((64, LANES), jnp.float32)
    lane = lax.broadcasted_iota(jnp.int32, (8, LANES), 1)
    for cx in range(2):
        sums = [0.0] * 5
        for x in range(4 * cx, 4 * cx + 4):
            here = rows(x, 0)
            zs = [face[6 + m, here, :] for m in range(3)]
            out = face[1, here, :] + face[4, here, :] + zs[1]
            out = out + face[2, rows(x - 1, 0), :] + face[5, rows(x, -1), :] + last_lane(zs[2])
            sums = [old + new for old, new in zip(sums, [poro[here, :], out] + zs)]
        for m in range(2, 5):
            sums[m] = jnp.where(lane % AGG == AGG - 1, sums[m], 0.0)
        for b, value in zip((0, 1, 12, 13, 14), sums):
            put_y(b, cx, value)
    for b, cx, m in ((2, 0, 0), (3, 1, 0), (4, 0, 1), (5, 0, 2), (6, 1, 2)):
        put_y(b, cx, face[m, rows(3, 0), :])
    for b, cy, m in ((7, 0, 0), (8, 1, 0), (9, 0, 1), (10, 0, 2), (11, 1, 2)):
        put_x(b, cy, face[3 + m, column(3), :])
    for f in range(2):
        for cx in range(2):
            total = ext[COT + f, rows(4 * cx, 0), :]
            for x in range(4 * cx + 1, 4 * cx + 4):
                total = total + ext[COT + f, rows(x, 0), :]
            total = four_sum(total)
            first = 4 * f + 2 * cx
            ring[pl.ds(first, 1), :] = total[0:1]
            ring[pl.ds(first + 1, 1), :] = total[4:5]
    ksend[pl.ds(52, 8), :] = lane_sum(ring[pl.ds(0, 8), :])
    ksend[pl.ds(60, 4), :] = jnp.zeros((4, LANES), jnp.float32)

    def take(i):
        when_there(SIDES[i], lambda: setup_copy(i).wait_recv())
        unpack(SIDES[i], True, srecv, (i,), ext, fits(*SIDES[i]))

    for i in range(4):
        take(i)

    def edge(axis, here, there):
        perm_here, _ = look_up(ext[MAT, here, :])
        perm_next, _ = look_up(ext[MAT, there, :])
        return one_face(perm_here, ext[HEAD, here, :], perm_next, ext[HEAD, there, :], ext[F0 + axis, here, :])

    trans, _, lower = edge(0, rows(-1, 0), rows(0, 0))
    put_y(3, 0, trans)
    put_y(6, 0, lower)
    trans, upper, _ = edge(0, rows(7, 0), rows(8, 0))
    put_y(2, 1, trans)
    put_y(4, 1, upper)
    trans, _, lower = edge(1, column(-1), column(0))
    put_x(8, 0, trans)
    put_x(11, 0, lower)
    trans, upper, lower = edge(1, column(7), column(8))
    put_x(7, 1, trans)
    put_x(9, 1, upper)
    put_x(10, 1, lower)
    cagg[...] = lane_sum(cagg[...])

    def block(b):
        return cagg[pl.ds(4 * b, 4), :]

    place = lax.broadcasted_iota(jnp.int32, (4, LANES), 0)
    store = block(0)
    t_z, a_z, b_z = block(12), block(13), block(14)
    edge_sum = block(2) + block(3) + block(7) + block(8) + t_z + last_lane(t_z, AGG)
    edge_out = block(4) + block(6) + block(9) + block(11) + a_z + last_lane(b_z, AGG)
    out = block(1) + jnp.where(place < 2, block(6), block(4)) + jnp.where(place % 2 == 0, block(11), block(9))
    cpp, cpc, ccp, ccc = store + edge_sum, -CPL_S * out, CPL_P * store, store + DISP * edge_sum + edge_out
    scale = OMEGA_C / (cpp * ccc - cpc * ccp)
    t_x, t_y = block(2), block(7)
    for b, value in enumerate((
        ccc * scale, -cpc * scale, -ccp * scale, cpp * scale,
        t_y, DISP * t_y + block(9), DISP * t_y + block(10),
        t_z, DISP * t_z + a_z, DISP * t_z + b_z,
        t_x, DISP * t_x + block(4), DISP * t_x + block(5),
    )):
        ksend[pl.ds(4 * b, 4), :] = value
    for j in range(4):
        when_sent(NEAR[j], lambda: coef_copy(j).start())

    for i in range(4, 8):
        take(i)
    look_up_rows(0, ROWS, 32)
    face_rows(0, 144, 24)
    for lo in range(16, 144, 16):
        here = pl.ds(lo, 16)
        total = jnp.zeros((16, LANES), jnp.float32)
        out = total
        for d in range(3):
            trans, upper, lower = (face[3 * d + m, here, :] for m in range(3))
            if d < 2:
                back = pl.ds(lo - (PITCH, 1)[d], 16)
                trans_m, lower_m = face[3 * d, back, :], face[3 * d + 2, back, :]
            else:
                trans_m, lower_m = last_lane(trans), last_lane(lower)
            co[TX + 2 * d, here, :] = trans
            co[TX + 2 * d + 1, here, :] = trans_m
            co[SX + 2 * d, here, :] = DISP * trans + upper
            co[SX + 2 * d + 1, here, :] = DISP * trans_m + lower_m
            total = total + trans + trans_m
            out = out + upper + lower_m
        store = poro[here, :]
        bpp, bpc, bcp, bcc = store + total, -CPL_S * out, CPL_P * store, store + DISP * total + out
        inside = jnp.logical_and(store > 0.0, mask[here, :] > 0.0)
        determ = jnp.where(inside, bpp * bcc - bpc * bcp, 1.0)
        scale = jnp.where(inside, OMEGA / determ, 0.0)
        for at, value in (
            (BPP, bpp), (BPC, bpc), (BCP, bcp), (BCC, bcc),
            (IPP, bcc * scale), (IPC, -bpc * scale), (ICP, -bcp * scale), (ICC, bpp * scale),
        ):
            co[at, here, :] = value

    def fine_solve(src, at):
        for lo in range(16, 144, 32):
            here = pl.ds(lo, 32)
            r_p, r_c = src[at, here, :], src[at + 1, here, :]
            grd[0, here, :] = co[IPP, here, :] * r_p + co[IPC, here, :] * r_c
            grd[1, here, :] = co[ICP, here, :] * r_p + co[ICC, here, :] * r_c
        for lo in range(16, 144, 16):
            here = pl.ds(lo, 16)
            z_p, s_p, z_c, s_c = couple(co, grd, lo, 16)
            mid[0, here, :] = (2.0 - OMEGA) * z_p + co[IPP, here, :] * s_p + co[IPC, here, :] * s_c
            mid[1, here, :] = (2.0 - OMEGA) * z_c + co[ICP, here, :] * s_p + co[ICC, here, :] * s_c
        for lo in range(32, 128, 16):
            here = pl.ds(lo, 16)
            z_p, s_p, z_c, s_c = couple(co, mid, lo, 16)
            fin[0, here, :] = (1.0 - OMEGA) * z_p + grd[0, here, :] + co[IPP, here, :] * s_p + co[IPC, here, :] * s_c
            fin[1, here, :] = (1.0 - OMEGA) * z_c + grd[1, here, :] + co[ICP, here, :] * s_p + co[ICC, here, :] * s_c

    def coarse_solve():
        ipp, ipc, icp, icc = ([cco[b, cx] for cx in range(2)] for b in range(4))
        t_y, a_y, b_y, t_z, a_z, b_z = ([cco[b, cx] for cx in range(2)] for b in range(4, 10))
        t_x, a_x, b_x = (cco[b, 0] for b in range(10, 13))
        ahead = {0: (t_y, t_z), 1: (a_y, a_z)}
        behind = {
            0: ([pltpu.roll(v, 1, 0) for v in t_y], [last_lane(v, AGG) for v in t_z]),
            1: ([pltpu.roll(v, 1, 0) for v in b_y], [last_lane(v, AGG) for v in b_z]),
        }
        across = {0: (t_x, t_x), 1: (a_x, b_x)}
        r = [[cres[2 * f + cx] for cx in range(2)] for f in range(2)]
        base = [
            [ipp[cx] * r[0][cx] + ipc[cx] * r[1][cx] for cx in range(2)],
            [icp[cx] * r[0][cx] + icc[cx] * r[1][cx] for cx in range(2)],
        ]
        z = base
        for sweep in range(3):
            acc = [[None] * 2 for f in range(2)]
            for f in range(2):
                for cx in range(2):
                    v = z[f][cx]
                    total = across[f][cx] * z[f][1 - cx]
                    total = total + ahead[f][0][cx] * pltpu.roll(v, 7, 0)
                    total = total + behind[f][0][cx] * pltpu.roll(v, 1, 0)
                    total = total + ahead[f][1][cx] * next_lane(v, AGG)
                    acc[f][cx] = total + behind[f][1][cx] * last_lane(v, AGG)
            z = [
                [(1.0 - OMEGA_C) * z[0][cx] + base[0][cx] + ipp[cx] * acc[0][cx] + ipc[cx] * acc[1][cx] for cx in range(2)],
                [(1.0 - OMEGA_C) * z[1][cx] + base[1][cx] + icp[cx] * acc[0][cx] + icc[cx] * acc[1][cx] for cx in range(2)],
            ]
        upper = lax.broadcasted_iota(jnp.int32, (8, LANES), 0) < AGG
        return [
            [
                jnp.where(upper, jnp.broadcast_to(v[3:4], (8, LANES)), jnp.broadcast_to(v[4:5], (8, LANES)))
                for v in z[f]
            ]
            for f in range(2)
        ]

    def update():
        grown = coarse_solve()
        for f in range(2):
            for x in range(8):
                here = rows(x, 0)
                more = THETA * (fin[f, here, :] + grown[f][x // 4])
                new = adj[f, here, :] + more
                inc[f, here, :] = more
                adj[f, here, :] = new
                out_ref[f, x] = new

    def send(k):
        for lo in range(16, 144, 16):
            here = pl.ds(lo, 16)
            z_p, s_p, z_c, s_c = couple(co, inc, lo, 16)
            res[0, here, :] = co[BPP, here, :] * z_p + co[BPC, here, :] * z_c - s_p
            res[1, here, :] = co[BCP, here, :] * z_p + co[BCC, here, :] * z_c - s_c

        def place(at, value):
            ring[pl.ds(at, 1), :] = value

        for f in range(2):
            for cx in range(2):
                total = res[f, rows(4 * cx, 0), :]
                for x in range(4 * cx + 1, 4 * cx + 4):
                    total = total + res[f, rows(x, 0), :]
                total = four_sum(total)
                place(8 * f + 4 * cx + 1, total[0:1])
                place(8 * f + 4 * cx + 2, total[4:5])
            for at, y in ((0, -1), (3, 8)):
                total = four_sum(res[f, column(y), :])
                place(8 * f + at, total[0:1])
                place(8 * f + 4 + at, total[4:5])
            for at, x in ((16, -1), (20, 8)):
                total = four_sum(res[f, rows(x, 0), :])
                place(at + 2 * f, total[0:1])
                place(at + 2 * f + 1, total[4:5])
        ring[...] = lane_sum(ring[...])
        along, beside = ring[pl.ds(0, 16), :], ring[pl.ds(16, 8), :]
        for i, side in enumerate(PARTNERS):
            if side not in FAR:
                pack(side, False, adj, rsend, (k, i))
            at = rows_of(side, False)
            if side[0] == 0:
                rsend[k, i, pl.ds(at, 16), :] = along
            else:
                rsend[k, i, pl.ds(at, 8), :] = beside
            when_sent(side, lambda: round_copy(i, k).start())

    def receive(k):
        for i, side in enumerate(PARTNERS):
            when_there(side, lambda: round_copy(i, k).wait_recv())
            if side not in FAR:
                unpack(side, False, rrecv, (k, i), adj, None)
        for f in range(2):
            for cx in range(2):
                item = 2 * f + cx

                def along(dy, first, count):
                    i = PARTNERS.index((0, dy))
                    return rrecv[k, i, pl.ds(rows_of((0, dy), False) + 4 * item + first, count), :]

                layer[0, item, pl.ds(0, 4), :] = along(-1, 0, 4)
                layer[0, item, pl.ds(4, 4), :] = along(1, 0, 4)
                layer[1, item, pl.ds(0, 2), :] = along(-2, 2, 2)
                layer[1, item, pl.ds(2, 4), :] = ring[pl.ds(4 * item, 4), :]
                layer[1, item, pl.ds(6, 2), :] = along(2, 0, 2)
                dx = 2 * cx - 1
                for dy in range(-2, 3):
                    first, count = max(2 * dy + 3, 0), 1 if abs(dy) == 2 else 2
                    at = rows_of((dx, dy), False) + (4 if dx < 0 else 0) + 2 * f + (1 if dy == -2 else 0)
                    layer[2, item, pl.ds(first, count), :] = rrecv[k, PARTNERS.index((dx, dy)), pl.ds(at, count), :]
                cres[item] = cres[item] - layer[0, item] - layer[1, item] - layer[2, item]
        for lo in range(16, 144, 16):
            here = pl.ds(lo, 16)
            z_p, s_p, z_c, s_c = couple(co, adj, lo, 16)
            res[0, here, :] = ext[COT, here, :] + s_p - co[BPP, here, :] * z_p - co[BPC, here, :] * z_c
            res[1, here, :] = ext[COT + 1, here, :] + s_c - co[BCP, here, :] * z_p - co[BCC, here, :] * z_c

    fine_solve(ext, COT)

    for j in range(4):
        when_there(NEAR[j], lambda: coef_copy(j).wait_recv())
    for item in range(2 * N_CBLK + 4):

        def put_coarse(where, value):
            if item < 2 * N_CBLK:
                cco[item // 2, item % 2, where, :] = value
            else:
                cres[item - 2 * N_CBLK, where, :] = value

        put_coarse(pl.ds(0, 1), krecv[0, pl.ds(2 * item + 1, 1), :])
        put_coarse(pl.ds(1, 2), krecv[2, pl.ds(2 * item, 2), :])
        put_coarse(pl.ds(3, 2), ksend[pl.ds(2 * item, 2), :])
        put_coarse(pl.ds(5, 2), krecv[3, pl.ds(2 * item, 2), :])
        put_coarse(pl.ds(7, 1), krecv[1, pl.ds(2 * item, 1), :])
    update()
    send(0)

    def step(k, carry):
        receive(k - 1)
        fine_solve(res, 0)
        update()
        pl.when(k < ITERS - 1)(lambda: send(k))
        return carry

    lax.fori_loop(1, ITERS, step, 0)

    for i, side in enumerate(SIDES):
        when_sent(side, lambda: setup_copy(i).wait_send())
    for i, side in enumerate(PARTNERS):

        def sent():
            for k in range(ROUNDS):
                round_copy(i, k).wait_send()

        when_sent(side, sent)
    for j, side in enumerate(NEAR):
        when_sent(side, lambda: coef_copy(j).wait_send())


def solution(mesh):
    n_grp, n_sub = mesh.shape["grp"], mesh.shape["sub"]

    def local(cotangent, head, materials, flags, perm_table, poro_table):
        def tile(*shape):
            return pltpu.VMEM(shape + (LANES,), jnp.float32)

        dma = pltpu.SemaphoreType.DMA
        vmem = pl.BlockSpec(memory_space=pltpu.VMEM)
        hbm = pl.BlockSpec(memory_space=pltpu.HBM)
        n_part = len(PARTNERS)
        return pl.pallas_call(
            functools.partial(kernel, n_grp, n_sub),
            out_shape=jax.ShapeDtypeStruct(cotangent.shape, jnp.float32),
            in_specs=[hbm] * 6,
            out_specs=vmem,
            scratch_shapes=[
                pltpu.VMEM(cotangent.shape, jnp.float32),
                pltpu.VMEM(head.shape, jnp.float32),
                pltpu.VMEM(materials.shape, jnp.int32),
                pltpu.VMEM(flags.shape, jnp.int32),
                pltpu.SMEM(perm_table.shape, jnp.float32),
                pltpu.SMEM(poro_table.shape, jnp.float32),
                tile(7, ROWS),
                tile(ROWS),
                tile(ROWS),
                tile(ROWS),
                tile(9, ROWS),
                tile(N_COEF, ROWS),
                tile(2, ROWS),
                tile(2, ROWS),
                tile(2, ROWS),
                tile(2, ROWS),
                tile(2, ROWS),
                tile(2, ROWS),
                tile(8, 80),
                tile(8, 80),
                tile(ROUNDS, n_part, 48),
                tile(ROUNDS, n_part, 48),
                tile(C_ROWS),
                tile(4, C_ROWS),
                tile(64),
                tile(24),
                tile(N_CBLK, 2, 8),
                tile(4, 8),
                tile(3, 4, 8),
                dma((6,)),
                dma((8,)),
                dma((8,)),
                dma((ROUNDS, n_part)),
                dma((ROUNDS, n_part)),
                dma((4,)),
                dma((4,)),
            ],
            compiler_params=pltpu.CompilerParams(
                collective_id=0, has_side_effects=True, vmem_limit_bytes=32 * 1024 * 1024
            ),
        )(cotangent, head, materials, flags, perm_table, poro_table)

    return jax.shard_map(
        local,
        mesh=mesh,
        in_specs=(
            P(None, "grp", "sub", None),
            P("grp", "sub", None),
            P("grp", "sub", None),
            P(None, "grp", "sub", None),
            P(),
            P(),
        ),
        out_specs=P(None, "grp", "sub", None),
        check_vma=False,
    )
```

```python
import functools

import jax
import jax.numpy as jnp
from jax import lax
from jax.experimental import pallas as pl
from jax.experimental.pallas import tpu as pltpu
from jax.sharding import PartitionSpec as P

CX = 8
AGG = 4
ITERS = 4
DISP = 0.2
CPL_P = 0.5
CPL_S = 0.3
OMEGA = 0.7
OMEGA_C = 0.7
THETA = 0.5

PITCH = 12
BASE = 8
ROWS = 160
LANES = 128
MESH = pl.DeviceIdType.MESH

SIDES = [(-1, 0), (1, 0), (0, -1), (0, 1), (-1, -1), (-1, 1), (1, -1), (1, 1)]
FAR = [(-1, -2), (-1, 2), (1, -2), (1, 2), (0, -2), (0, 2)]
PARTNERS = FAR + SIDES[4:] + SIDES[:4]
NEAR = [(0, -2), (0, 2), (0, -1), (0, 1)]

MAT, HEAD, F0, F1, F2, COT = 0, 1, 2, 3, 4, 5
TX, TXM, TY, TYM, TZ, TZM, SX, SXM, SY, SYM, SZ, SZM, BPP, BPC, BCP, BCC, IPP, IPC, ICP, ICC = range(20)
N_COEF = 20
N_CBLK = 13
C_ROWS = 64
ROUNDS = ITERS - 1


def row(x, y):
    return BASE + (x + 2) * PITCH + y + 2


def rows(x, y, count=8):
    return pl.ds(row(x, y), count)


def column(y):
    return pl.ds(row(0, y), 8, stride=PITCH)


def setup_slots(low, along):
    one, two = (-1, -2) if low else (8, 9)
    first = [(MAT, one), (HEAD, one), (along, one)]
    others = [(field, one) for field in (F0, F1, F2) if field != along]
    return first + others + [(MAT, two), (HEAD, two)] + ([(along, two)] if low else []) + [(COT, one), (COT + 1, one)]


def field_slots(low):
    return [(f, layer) for f in (0, 1) for layer in ((-2, -1) if low else (8, 9))]


def slots_of(side, setup):
    dx, dy = side
    if dx != 0:
        return setup_slots(dx < 0, F0) if setup else field_slots(dx < 0)
    return setup_slots(dy < 0, F1) if setup else field_slots(dy < 0)


def pack(side, setup, src, dst, lead):
    dx, dy = side
    for slot, (field, layer) in enumerate(slots_of(side, setup)):
        if dy == 0:
            dst[lead + (pl.ds(8 * slot, 8),)] = src[field, rows(layer % 8, 0), :]
        elif dx == 0:
            dst[lead + (pl.ds(8 * slot, 8),)] = src[field, column(layer % 8), :]
        else:
            dst[lead + (pl.ds(2 * slot, 2),)] = src[field, rows(layer % 8, 6 if dy < 0 else 0, 2), :]


def unpack(side, setup, src, lead, dst, valid, first=0, end=None):
    dx, dy = side

    def seen(field, value):
        return jnp.where(valid, value, -1.0) if setup and field == MAT else value

    for slot, (field, layer) in list(enumerate(slots_of(side, setup)))[first:end]:
        if dy == 0:
            dst[field, rows(layer, 0), :] = seen(field, src[lead + (pl.ds(8 * slot, 8),)])
        elif dx == 0:
            dst[field, column(layer), :] = seen(field, src[lead + (pl.ds(8 * slot, 8),)])
        else:
            dst[field, rows(layer, -2 if dy < 0 else 8, 2), :] = seen(field, src[lead + (pl.ds(2 * slot, 2),)])


def next_lane(value, by=1):
    return pltpu.roll(value, LANES - by, 1)


def last_lane(value, by=1):
    return pltpu.roll(value, by, 1)


def lane_sum(value):
    lane = lax.broadcasted_iota(jnp.int32, value.shape, 1)
    total = value + next_lane(value)
    total = total + next_lane(total, 2)
    total = jnp.where(lane % AGG == 0, total, 0.0)
    total = total + last_lane(total)
    return total + last_lane(total, 2)


def four_sum(value):
    total = value + pltpu.roll(value, 7, 0)
    return total + pltpu.roll(total, 6, 0)


def couple(co, field, lo, n):
    here = pl.ds(lo, n)
    out = []
    for f, first in ((0, TX), (1, SX)):
        mid = field[f, here, :]
        total = co[first, here, :] * field[f, pl.ds(lo + PITCH, n), :]
        total = total + co[first + 1, here, :] * field[f, pl.ds(lo - PITCH, n), :]
        total = total + co[first + 2, here, :] * field[f, pl.ds(lo + 1, n), :]
        total = total + co[first + 3, here, :] * field[f, pl.ds(lo - 1, n), :]
        total = total + co[first + 4, here, :] * next_lane(mid)
        total = total + co[first + 5, here, :] * last_lane(mid)
        out += [mid, total]
    return out


def kernel(
    n_grp,
    n_sub,
    cot_hbm,
    head_hbm,
    mat_hbm,
    flag_hbm,
    perm_hbm,
    poro_hbm,
    out_ref,
    cot_ref,
    head_ref,
    mat_ref,
    flag_ref,
    perm_tab,
    poro_tab,
    ext,
    perm,
    poro,
    mask,
    face,
    co,
    adj,
    inc,
    res,
    grd,
    mid,
    fin,
    ssend,
    srecv,
    rsend,
    rrecv,
    ksend,
    krecv,
    cagg,
    ring,
    cco,
    cres,
    layer,
    l_sem,
    s_send,
    s_recv,
    r_send,
    r_recv,
    k_send,
    k_recv,
):
    g = lax.axis_index("grp")
    s = lax.axis_index("sub")

    def device(dx, dy):
        return {"grp": g + dx, "sub": s + dy}

    def fits(dx, dy):
        found = []
        for at, count, step in ((g, n_grp, dx), (s, n_sub, dy)):
            if step < 0:
                found.append(at >= -step)
            elif step > 0:
                found.append(at < count - step)
        return found[0] if len(found) == 1 else jnp.logical_and(*found)

    loads = [
        pltpu.make_async_copy(src, dst, l_sem.at[i])
        for i, (src, dst) in enumerate((
            (mat_hbm, mat_ref), (head_hbm, head_ref), (flag_hbm, flag_ref), (cot_hbm, cot_ref), (perm_hbm, perm_tab), (poro_hbm, poro_tab)
        ))
    ]
    for load in loads:
        load.start()

    barrier = pltpu.get_barrier_semaphore()
    expected = jnp.int32(0)
    for dx, dy in SIDES:
        there = fits(dx, dy)

        @pl.when(there)
        def _():
            pl.semaphore_signal(barrier, inc=1, device_id=device(dx, dy), device_id_type=MESH)

        expected = expected + there.astype(jnp.int32)

    def rows_of(side, setup):
        dx, dy = side
        if side in FAR:
            return 0
        if setup:
            count = len(slots_of(side, True)) * (2 if dx != 0 and dy != 0 else 8)
            return -(-count // 8) * 8
        return 8 if dx != 0 and dy != 0 else 32

    def setup_copy(i, first=False):
        dx, dy = SIDES[i]
        start, end, at = 0, rows_of((dx, dy), True), i
        if first:
            end, at = 24, 8 + i
        elif i < 4:
            start = 24
        part = pl.ds(start, end - start)
        return pltpu.make_async_remote_copy(
            ssend.at[i, part], srecv.at[i, part], s_send.at[at], s_recv.at[at], device_id=device(-dx, -dy), device_id_type=MESH
        )

    def round_copy(i, k):
        dx, dy = PARTNERS[i]
        part = pl.ds(0, rows_of((dx, dy), False) + (16 if dx == 0 else 8))
        return pltpu.make_async_remote_copy(
            rsend.at[k, i, part], rrecv.at[k, i, part], r_send.at[k, i], r_recv.at[k, i], device_id=device(-dx, -dy), device_id_type=MESH
        )

    def coef_copy(j):
        dx, dy = NEAR[j]
        return pltpu.make_async_remote_copy(
            ksend, krecv.at[j], k_send.at[j], k_recv.at[j], device_id=device(-dx, -dy), device_id_type=MESH
        )

    def when_sent(side, act):
        pl.when(fits(-side[0], -side[1]))(act)

    def when_there(side, act):
        pl.when(fits(*side))(act)

    zero_rows = jnp.zeros((ROWS, LANES), jnp.float32)
    ext[MAT] = zero_rows - 1.0
    for f in range(1, 7):
        ext[f] = zero_rows
    mask[...] = zero_rows
    perm[...] = zero_rows
    poro[...] = zero_rows
    for f in range(2):
        adj[f] = zero_rows
        inc[f] = zero_rows
        grd[f] = zero_rows
        mid[f] = zero_rows
    for m in range(9):
        face[m, pl.ds(0, 32), :] = jnp.zeros((32, LANES), jnp.float32)
    for x in range(-1, 9):
        mask[rows(x, -1, 10), :] = jnp.ones((10, LANES), jnp.float32)
    for i, side in enumerate(SIDES):

        @pl.when(jnp.logical_not(fits(*side)))
        def _():
            srecv[i] = jnp.zeros((80, LANES), jnp.float32)

    for i, side in enumerate(PARTNERS):

        @pl.when(jnp.logical_not(fits(*side)))
        def _():
            for k in range(ROUNDS):
                rrecv[k, i] = jnp.zeros((48, LANES), jnp.float32)

    for j, side in enumerate(NEAR):

        @pl.when(jnp.logical_not(fits(*side)))
        def _():
            krecv[j] = jnp.zeros((C_ROWS, LANES), jnp.float32)

    for load in loads:
        load.wait()
    for x in range(8):
        ext[MAT, rows(x, 0), :] = mat_ref[x].astype(jnp.float32)
        ext[HEAD, rows(x, 0), :] = head_ref[x]
        for d in range(3):
            ext[F0 + d, rows(x, 0), :] = flag_ref[d, x].astype(jnp.float32)
        for f in range(2):
            ext[COT + f, rows(x, 0), :] = cot_ref[f, x]
    for i, side in enumerate(SIDES):
        pack(side, True, ext, ssend, (i,))

    pl.semaphore_wait(barrier, expected)
    for i in range(4):
        when_sent(SIDES[i], lambda: setup_copy(i, True).start())
    for i in reversed(range(8)):
        when_sent(SIDES[i], lambda: setup_copy(i).start())

    def look_up(mats):
        perm_here = jnp.zeros_like(mats)
        poro_here = jnp.zeros_like(mats)
        for level in range(perm_tab.shape[0]):
            same = mats == float(level)
            perm_here = jnp.where(same, perm_tab[level], perm_here)
            poro_here = jnp.where(same, poro_tab[level], poro_here)
        return perm_here, poro_here

    def one_face(perm_here, head_here, perm_next, head_next, upwind):
        both = perm_here + perm_next
        trans = 2.0 * perm_here * perm_next / jnp.where(both > 0.0, both, 1.0)
        flux = trans * (0.5 + jnp.abs(head_here - head_next))
        return trans, upwind * flux, (1.0 - upwind) * flux

    def look_up_rows(first, end, n):
        for lo in range(first, end, n):
            here = pl.ds(lo, n)
            perm[here, :], poro[here, :] = look_up(ext[MAT, here, :])

    def face_rows(first, end, n):
        for lo in range(first, end, n):
            here = pl.ds(lo, n)
            perm_here, head_here = perm[here, :], ext[HEAD, here, :]
            lane = lax.broadcasted_iota(jnp.int32, (n, LANES), 1)
            for d in range(3):
                if d < 2:
                    there = pl.ds(lo + (PITCH, 1)[d], n)
                    perm_next, head_next = perm[there, :], ext[HEAD, there, :]
                else:
                    perm_next = jnp.where(lane == LANES - 1, 0.0, next_lane(perm_here))
                    head_next = next_lane(head_here)
                values = one_face(perm_here, head_here, perm_next, head_next, ext[F0 + d, here, :])
                for m in range(3):
                    face[3 * d + m, here, :] = values[m]

    look_up_rows(32, 128, 32)
    face_rows(32, 128, 24)

    def put(block, cx, cy, value):
        cagg[pl.ds(4 * block + 2 * cx + cy, 1), :] = value

    def put_y(block, cx, value):
        value = four_sum(value)
        put(block, cx, 0, value[0:1])
        put(block, cx, 1, value[4:5])

    def put_x(block, cy, value):
        value = four_sum(value)
        put(block, 0, cy, value[0:1])
        put(block, 1, cy, value[4:5])

    cagg[...] = jnp.zeros((64, LANES), jnp.float32)
    lane = lax.broadcasted_iota(jnp.int32, (8, LANES), 1)
    for cx in range(2):
        sums = [0.0] * 5
        for x in range(4 * cx, 4 * cx + 4):
            here = rows(x, 0)
            zs = [face[6 + m, here, :] for m in range(3)]
            out = face[1, here, :] + face[4, here, :] + zs[1]
            out = out + face[2, rows(x - 1, 0), :] + face[5, rows(x, -1), :] + last_lane(zs[2])
            sums = [old + new for old, new in zip(sums, [poro[here, :], out] + zs)]
        for m in range(2, 5):
            sums[m] = jnp.where(lane % AGG == AGG - 1, sums[m], 0.0)
        for b, value in zip((0, 1, 12, 13, 14), sums):
            put_y(b, cx, value)
    for b, cx, m in ((2, 0, 0), (3, 1, 0), (4, 0, 1), (5, 0, 2), (6, 1, 2)):
        put_y(b, cx, face[m, rows(3, 0), :])
    for b, cy, m in ((7, 0, 0), (8, 1, 0), (9, 0, 1), (10, 0, 2), (11, 1, 2)):
        put_x(b, cy, face[3 + m, column(3), :])
    for f in range(2):
        for cx in range(2):
            total = ext[COT + f, rows(4 * cx, 0), :]
            for x in range(4 * cx + 1, 4 * cx + 4):
                total = total + ext[COT + f, rows(x, 0), :]
            total = four_sum(total)
            first = 4 * f + 2 * cx
            ring[pl.ds(first, 1), :] = total[0:1]
            ring[pl.ds(first + 1, 1), :] = total[4:5]
    ksend[pl.ds(52, 8), :] = lane_sum(ring[pl.ds(0, 8), :])
    ksend[pl.ds(60, 4), :] = jnp.zeros((4, LANES), jnp.float32)

    def take(i, first):
        when_there(SIDES[i], lambda: setup_copy(i, first).wait_recv())
        span = (0, 3) if first else (3 if i < 4 else 0, None)
        unpack(SIDES[i], True, srecv, (i,), ext, fits(*SIDES[i]), *span)

    for i in range(4):
        take(i, True)

    def edge(axis, here, there):
        perm_here, _ = look_up(ext[MAT, here, :])
        perm_next, _ = look_up(ext[MAT, there, :])
        return one_face(perm_here, ext[HEAD, here, :], perm_next, ext[HEAD, there, :], ext[F0 + axis, here, :])

    trans, _, lower = edge(0, rows(-1, 0), rows(0, 0))
    put_y(3, 0, trans)
    put_y(6, 0, lower)
    trans, upper, _ = edge(0, rows(7, 0), rows(8, 0))
    put_y(2, 1, trans)
    put_y(4, 1, upper)
    trans, _, lower = edge(1, column(-1), column(0))
    put_x(8, 0, trans)
    put_x(11, 0, lower)
    trans, upper, lower = edge(1, column(7), column(8))
    put_x(7, 1, trans)
    put_x(9, 1, upper)
    put_x(10, 1, lower)
    cagg[...] = lane_sum(cagg[...])

    def block(b):
        return cagg[pl.ds(4 * b, 4), :]

    place = lax.broadcasted_iota(jnp.int32, (4, LANES), 0)
    store = block(0)
    t_z, a_z, b_z = block(12), block(13), block(14)
    edge_sum = block(2) + block(3) + block(7) + block(8) + t_z + last_lane(t_z, AGG)
    edge_out = block(4) + block(6) + block(9) + block(11) + a_z + last_lane(b_z, AGG)
    out = block(1) + jnp.where(place < 2, block(6), block(4)) + jnp.where(place % 2 == 0, block(11), block(9))
    cpp, cpc, ccp, ccc = store + edge_sum, -CPL_S * out, CPL_P * store, store + DISP * edge_sum + edge_out
    scale = OMEGA_C / (cpp * ccc - cpc * ccp)
    t_x, t_y = block(2), block(7)
    for b, value in enumerate((
        ccc * scale, -cpc * scale, -ccp * scale, cpp * scale,
        t_y, DISP * t_y + block(9), DISP * t_y + block(10),
        t_z, DISP * t_z + a_z, DISP * t_z + b_z,
        t_x, DISP * t_x + block(4), DISP * t_x + block(5),
    )):
        ksend[pl.ds(4 * b, 4), :] = value
    for j in range(4):
        when_sent(NEAR[j], lambda: coef_copy(j).start())

    for i in range(8):
        take(i, False)
    look_up_rows(0, ROWS, 32)
    face_rows(0, 144, 24)
    for lo in range(16, 144, 16):
        here = pl.ds(lo, 16)
        total = jnp.zeros((16, LANES), jnp.float32)
        out = total
        for d in range(3):
            trans, upper, lower = (face[3 * d + m, here, :] for m in range(3))
            if d < 2:
                back = pl.ds(lo - (PITCH, 1)[d], 16)
                trans_m, lower_m = face[3 * d, back, :], face[3 * d + 2, back, :]
            else:
                trans_m, lower_m = last_lane(trans), last_lane(lower)
            co[TX + 2 * d, here, :] = trans
            co[TX + 2 * d + 1, here, :] = trans_m
            co[SX + 2 * d, here, :] = DISP * trans + upper
            co[SX + 2 * d + 1, here, :] = DISP * trans_m + lower_m
            total = total + trans + trans_m
            out = out + upper + lower_m
        store = poro[here, :]
        bpp, bpc, bcp, bcc = store + total, -CPL_S * out, CPL_P * store, store + DISP * total + out
        inside = jnp.logical_and(store > 0.0, mask[here, :] > 0.0)
        determ = jnp.where(inside, bpp * bcc - bpc * bcp, 1.0)
        scale = jnp.where(inside, OMEGA / determ, 0.0)
        for at, value in (
            (BPP, bpp), (BPC, bpc), (BCP, bcp), (BCC, bcc),
            (IPP, bcc * scale), (IPC, -bpc * scale), (ICP, -bcp * scale), (ICC, bpp * scale),
        ):
            co[at, here, :] = value

    def fine_solve(src, at):
        for lo in range(16, 144, 32):
            here = pl.ds(lo, 32)
            r_p, r_c = src[at, here, :], src[at + 1, here, :]
            grd[0, here, :] = co[IPP, here, :] * r_p + co[IPC, here, :] * r_c
            grd[1, here, :] = co[ICP, here, :] * r_p + co[ICC, here, :] * r_c
        for lo in range(16, 144, 16):
            here = pl.ds(lo, 16)
            z_p, s_p, z_c, s_c = couple(co, grd, lo, 16)
            mid[0, here, :] = (2.0 - OMEGA) * z_p + co[IPP, here, :] * s_p + co[IPC, here, :] * s_c
            mid[1, here, :] = (2.0 - OMEGA) * z_c + co[ICP, here, :] * s_p + co[ICC, here, :] * s_c
        for lo in range(32, 128, 16):
            here = pl.ds(lo, 16)
            z_p, s_p, z_c, s_c = couple(co, mid, lo, 16)
            fin[0, here, :] = (1.0 - OMEGA) * z_p + grd[0, here, :] + co[IPP, here, :] * s_p + co[IPC, here, :] * s_c
            fin[1, here, :] = (1.0 - OMEGA) * z_c + grd[1, here, :] + co[ICP, here, :] * s_p + co[ICC, here, :] * s_c

    def coarse_solve():
        ipp, ipc, icp, icc = ([cco[b, cx] for cx in range(2)] for b in range(4))
        t_y, a_y, b_y, t_z, a_z, b_z = ([cco[b, cx] for cx in range(2)] for b in range(4, 10))
        t_x, a_x, b_x = (cco[b, 0] for b in range(10, 13))
        ahead = {0: (t_y, t_z), 1: (a_y, a_z)}
        behind = {
            0: ([pltpu.roll(v, 1, 0) for v in t_y], [last_lane(v, AGG) for v in t_z]),
            1: ([pltpu.roll(v, 1, 0) for v in b_y], [last_lane(v, AGG) for v in b_z]),
        }
        across = {0: (t_x, t_x), 1: (a_x, b_x)}
        r = [[cres[2 * f + cx] for cx in range(2)] for f in range(2)]
        base = [
            [ipp[cx] * r[0][cx] + ipc[cx] * r[1][cx] for cx in range(2)],
            [icp[cx] * r[0][cx] + icc[cx] * r[1][cx] for cx in range(2)],
        ]
        z = base
        for sweep in range(3):
            acc = [[None] * 2 for f in range(2)]
            for f in range(2):
                for cx in range(2):
                    v = z[f][cx]
                    total = across[f][cx] * z[f][1 - cx]
                    total = total + ahead[f][0][cx] * pltpu.roll(v, 7, 0)
                    total = total + behind[f][0][cx] * pltpu.roll(v, 1, 0)
                    total = total + ahead[f][1][cx] * next_lane(v, AGG)
                    acc[f][cx] = total + behind[f][1][cx] * last_lane(v, AGG)
            z = [
                [(1.0 - OMEGA_C) * z[0][cx] + base[0][cx] + ipp[cx] * acc[0][cx] + ipc[cx] * acc[1][cx] for cx in range(2)],
                [(1.0 - OMEGA_C) * z[1][cx] + base[1][cx] + icp[cx] * acc[0][cx] + icc[cx] * acc[1][cx] for cx in range(2)],
            ]
        upper = lax.broadcasted_iota(jnp.int32, (8, LANES), 0) < AGG
        return [
            [
                jnp.where(upper, jnp.broadcast_to(v[3:4], (8, LANES)), jnp.broadcast_to(v[4:5], (8, LANES)))
                for v in z[f]
            ]
            for f in range(2)
        ]

    def update():
        grown = coarse_solve()
        for f in range(2):
            for x in range(8):
                here = rows(x, 0)
                more = THETA * (fin[f, here, :] + grown[f][x // 4])
                new = adj[f, here, :] + more
                inc[f, here, :] = more
                adj[f, here, :] = new
                out_ref[f, x] = new

    def send(k):
        for lo in range(16, 144, 16):
            here = pl.ds(lo, 16)
            z_p, s_p, z_c, s_c = couple(co, inc, lo, 16)
            res[0, here, :] = co[BPP, here, :] * z_p + co[BPC, here, :] * z_c - s_p
            res[1, here, :] = co[BCP, here, :] * z_p + co[BCC, here, :] * z_c - s_c

        def place(at, value):
            ring[pl.ds(at, 1), :] = value

        for f in range(2):
            for cx in range(2):
                total = res[f, rows(4 * cx, 0), :]
                for x in range(4 * cx + 1, 4 * cx + 4):
                    total = total + res[f, rows(x, 0), :]
                total = four_sum(total)
                place(8 * f + 4 * cx + 1, total[0:1])
                place(8 * f + 4 * cx + 2, total[4:5])
            for at, y in ((0, -1), (3, 8)):
                total = four_sum(res[f, column(y), :])
                place(8 * f + at, total[0:1])
                place(8 * f + 4 + at, total[4:5])
            for at, x in ((16, -1), (20, 8)):
                total = four_sum(res[f, rows(x, 0), :])
                place(at + 2 * f, total[0:1])
                place(at + 2 * f + 1, total[4:5])
        ring[...] = lane_sum(ring[...])
        along, beside = ring[pl.ds(0, 16), :], ring[pl.ds(16, 8), :]
        for i, side in enumerate(PARTNERS):
            if side not in FAR:
                pack(side, False, adj, rsend, (k, i))
            at = rows_of(side, False)
            if side[0] == 0:
                rsend[k, i, pl.ds(at, 16), :] = along
            else:
                rsend[k, i, pl.ds(at, 8), :] = beside
            when_sent(side, lambda: round_copy(i, k).start())

    def receive(k):
        for i, side in enumerate(PARTNERS):
            when_there(side, lambda: round_copy(i, k).wait_recv())
            if side not in FAR:
                unpack(side, False, rrecv, (k, i), adj, None)
        for f in range(2):
            for cx in range(2):
                item = 2 * f + cx

                def along(dy, first, count):
                    i = PARTNERS.index((0, dy))
                    return rrecv[k, i, pl.ds(rows_of((0, dy), False) + 4 * item + first, count), :]

                layer[0, item, pl.ds(0, 4), :] = along(-1, 0, 4)
                layer[0, item, pl.ds(4, 4), :] = along(1, 0, 4)
                layer[1, item, pl.ds(0, 2), :] = along(-2, 2, 2)
                layer[1, item, pl.ds(2, 4), :] = ring[pl.ds(4 * item, 4), :]
                layer[1, item, pl.ds(6, 2), :] = along(2, 0, 2)
                dx = 2 * cx - 1
                for dy in range(-2, 3):
                    first, count = max(2 * dy + 3, 0), 1 if abs(dy) == 2 else 2
                    at = rows_of((dx, dy), False) + (4 if dx < 0 else 0) + 2 * f + (1 if dy == -2 else 0)
                    layer[2, item, pl.ds(first, count), :] = rrecv[k, PARTNERS.index((dx, dy)), pl.ds(at, count), :]
                cres[item] = cres[item] - layer[0, item] - layer[1, item] - layer[2, item]
        for lo in range(16, 144, 16):
            here = pl.ds(lo, 16)
            z_p, s_p, z_c, s_c = couple(co, adj, lo, 16)
            res[0, here, :] = ext[COT, here, :] + s_p - co[BPP, here, :] * z_p - co[BPC, here, :] * z_c
            res[1, here, :] = ext[COT + 1, here, :] + s_c - co[BCP, here, :] * z_p - co[BCC, here, :] * z_c

    fine_solve(ext, COT)

    for j in range(4):
        when_there(NEAR[j], lambda: coef_copy(j).wait_recv())
    for item in range(2 * N_CBLK + 4):

        def put_coarse(where, value):
            if item < 2 * N_CBLK:
                cco[item // 2, item % 2, where, :] = value
            else:
                cres[item - 2 * N_CBLK, where, :] = value

        put_coarse(pl.ds(0, 1), krecv[0, pl.ds(2 * item + 1, 1), :])
        put_coarse(pl.ds(1, 2), krecv[2, pl.ds(2 * item, 2), :])
        put_coarse(pl.ds(3, 2), ksend[pl.ds(2 * item, 2), :])
        put_coarse(pl.ds(5, 2), krecv[3, pl.ds(2 * item, 2), :])
        put_coarse(pl.ds(7, 1), krecv[1, pl.ds(2 * item, 1), :])
    update()
    send(0)

    def step(k, carry):
        receive(k - 1)
        fine_solve(res, 0)
        update()
        pl.when(k < ITERS - 1)(lambda: send(k))
        return carry

    lax.fori_loop(1, ITERS, step, 0)

    for i, side in enumerate(SIDES):
        when_sent(side, lambda: setup_copy(i).wait_send())
        if i < 4:
            when_sent(side, lambda: setup_copy(i, True).wait_send())
    for i, side in enumerate(PARTNERS):

        def sent():
            for k in range(ROUNDS):
                round_copy(i, k).wait_send()

        when_sent(side, sent)
    for j, side in enumerate(NEAR):
        when_sent(side, lambda: coef_copy(j).wait_send())


def solution(mesh):
    n_grp, n_sub = mesh.shape["grp"], mesh.shape["sub"]

    def local(cotangent, head, materials, flags, perm_table, poro_table):
        def tile(*shape):
            return pltpu.VMEM(shape + (LANES,), jnp.float32)

        dma = pltpu.SemaphoreType.DMA
        vmem = pl.BlockSpec(memory_space=pltpu.VMEM)
        hbm = pl.BlockSpec(memory_space=pltpu.HBM)
        n_part = len(PARTNERS)
        return pl.pallas_call(
            functools.partial(kernel, n_grp, n_sub),
            out_shape=pltpu.VMEM(cotangent.shape, jnp.float32),
            in_specs=[hbm] * 6,
            out_specs=vmem,
            scratch_shapes=[
                pltpu.VMEM(cotangent.shape, jnp.float32),
                pltpu.VMEM(head.shape, jnp.float32),
                pltpu.VMEM(materials.shape, jnp.int32),
                pltpu.VMEM(flags.shape, jnp.int32),
                pltpu.SMEM(perm_table.shape, jnp.float32),
                pltpu.SMEM(poro_table.shape, jnp.float32),
                tile(7, ROWS),
                tile(ROWS),
                tile(ROWS),
                tile(ROWS),
                tile(9, ROWS),
                tile(N_COEF, ROWS),
                tile(2, ROWS),
                tile(2, ROWS),
                tile(2, ROWS),
                tile(2, ROWS),
                tile(2, ROWS),
                tile(2, ROWS),
                tile(8, 80),
                tile(8, 80),
                tile(ROUNDS, n_part, 48),
                tile(ROUNDS, n_part, 48),
                tile(C_ROWS),
                tile(4, C_ROWS),
                tile(64),
                tile(24),
                tile(N_CBLK, 2, 8),
                tile(4, 8),
                tile(3, 4, 8),
                dma((6,)),
                dma((12,)),
                dma((12,)),
                dma((ROUNDS, n_part)),
                dma((ROUNDS, n_part)),
                dma((4,)),
                dma((4,)),
            ],
            compiler_params=pltpu.CompilerParams(
                collective_id=0, has_side_effects=True, vmem_limit_bytes=32 * 1024 * 1024
            ),
        )(*(pltpu.with_memory_space_constraint(x, pltpu.HBM) for x in (cotangent, head, materials, flags, perm_table, poro_table)))

    return jax.shard_map(
        local,
        mesh=mesh,
        in_specs=(
            P(None, "grp", "sub", None),
            P("grp", "sub", None),
            P("grp", "sub", None),
            P(None, "grp", "sub", None),
            P(),
            P(),
        ),
        out_specs=P(None, "grp", "sub", None),
        check_vma=False,
    )
```

```python
import functools

import jax
import jax.numpy as jnp
from jax import lax
from jax.experimental import pallas as pl
from jax.experimental.pallas import tpu as pltpu
from jax.sharding import PartitionSpec as P

CX = 8
AGG = 4
ITERS = 4
DISP = 0.2
CPL_P = 0.5
CPL_S = 0.3
OMEGA = 0.7
OMEGA_C = 0.7
THETA = 0.5

PITCH = 12
BASE = 8
ROWS = 160
LANES = 128
MESH = pl.DeviceIdType.MESH

SIDES = [(-1, 0), (1, 0), (0, -1), (0, 1), (-1, -1), (-1, 1), (1, -1), (1, 1)]
FAR = [(-1, -2), (-1, 2), (1, -2), (1, 2), (0, -2), (0, 2)]
PARTNERS = FAR + SIDES[4:] + SIDES[:4]
NEAR = [(0, -2), (0, 2), (0, -1), (0, 1)]

MAT, HEAD, F0, F1, F2, COT = 0, 1, 2, 3, 4, 5
TX, TXM, TY, TYM, TZ, TZM, SX, SXM, SY, SYM, SZ, SZM, BPP, BPC, BCP, BCC, IPP, IPC, ICP, ICC = range(20)
N_COEF = 20
N_CBLK = 13
N_INNER = 17
C_ROWS = 120
C_RAW = 40
ROUNDS = ITERS - 1
N_PART = 14


def row(x, y):
    return BASE + (x + 2) * PITCH + y + 2


def rows(x, y, count=8):
    return pl.ds(row(x, y), count)


def column(y):
    return pl.ds(row(0, y), 8, stride=PITCH)


def setup_slots(low, along):
    one, two = (-1, -2) if low else (8, 9)
    first = [(MAT, one), (HEAD, one), (along, one)]
    others = [(field, one) for field in (F0, F1, F2) if field != along]
    return first + others + [(MAT, two), (HEAD, two)] + ([(along, two)] if low else []) + [(COT, one), (COT + 1, one)]


def field_slots(low):
    return [(f, layer) for f in (0, 1) for layer in ((-2, -1) if low else (8, 9))]


def slots_of(side, setup):
    dx, dy = side
    if dx != 0:
        return setup_slots(dx < 0, F0) if setup else field_slots(dx < 0)
    return setup_slots(dy < 0, F1) if setup else field_slots(dy < 0)


def pack(side, setup, src, dst, lead):
    dx, dy = side
    for slot, (field, layer) in enumerate(slots_of(side, setup)):
        if dy == 0:
            dst[lead + (pl.ds(8 * slot, 8),)] = src[field, rows(layer % 8, 0), :]
        elif dx == 0:
            dst[lead + (pl.ds(8 * slot, 8),)] = src[field, column(layer % 8), :]
        else:
            dst[lead + (pl.ds(2 * slot, 2),)] = src[field, rows(layer % 8, 6 if dy < 0 else 0, 2), :]


def unpack(side, setup, src, lead, dst, valid):
    dx, dy = side

    def seen(field, value):
        return jnp.where(valid, value, -1.0) if setup and field == MAT else value

    for slot, (field, layer) in enumerate(slots_of(side, setup)):
        if dy == 0:
            dst[field, rows(layer, 0), :] = seen(field, src[lead + (pl.ds(8 * slot, 8),)])
        elif dx == 0:
            dst[field, column(layer), :] = seen(field, src[lead + (pl.ds(8 * slot, 8),)])
        else:
            dst[field, rows(layer, -2 if dy < 0 else 8, 2), :] = seen(field, src[lead + (pl.ds(2 * slot, 2),)])


def next_lane(value, by=1):
    return pltpu.roll(value, LANES - by, 1)


def last_lane(value, by=1):
    return pltpu.roll(value, by, 1)


def lane_sum(value):
    lane = lax.broadcasted_iota(jnp.int32, value.shape, 1)
    total = value + next_lane(value)
    total = total + next_lane(total, 2)
    total = jnp.where(lane % AGG == 0, total, 0.0)
    total = total + last_lane(total)
    return total + last_lane(total, 2)


def four_sum(value):
    total = value + pltpu.roll(value, 7, 0)
    return total + pltpu.roll(total, 6, 0)


def couple(co, field, lo, n):
    here = pl.ds(lo, n)
    out = []
    for f, first in ((0, TX), (1, SX)):
        mid = field[f, here, :]
        total = co[first, here, :] * field[f, pl.ds(lo + PITCH, n), :]
        total = total + co[first + 1, here, :] * field[f, pl.ds(lo - PITCH, n), :]
        total = total + co[first + 2, here, :] * field[f, pl.ds(lo + 1, n), :]
        total = total + co[first + 3, here, :] * field[f, pl.ds(lo - 1, n), :]
        total = total + co[first + 4, here, :] * next_lane(mid)
        total = total + co[first + 5, here, :] * last_lane(mid)
        out += [mid, total]
    return out


def kernel(
    n_grp,
    n_sub,
    cot_hbm,
    head_hbm,
    mat_hbm,
    flag_hbm,
    perm_hbm,
    poro_hbm,
    out_ref,
    cot_ref,
    head_ref,
    mat_ref,
    flag_ref,
    perm_tab,
    poro_tab,
    ext,
    perm,
    poro,
    mask,
    face,
    co,
    adj,
    inc,
    res,
    grd,
    mid,
    fin,
    ssend,
    srecv,
    rsend,
    rrecv,
    xsend,
    xrecv,
    ksend,
    krecv,
    cin,
    cedge,
    ring,
    cco,
    cres,
    layer,
    sent,
    came,
):
    g = lax.axis_index("grp")
    s = lax.axis_index("sub")

    def device(dx, dy):
        return {"grp": g + dx, "sub": s + dy}

    def fits(dx, dy):
        found = []
        for at, count, step in ((g, n_grp, dx), (s, n_sub, dy)):
            if step < 0:
                found.append(at >= -step)
            elif step > 0:
                found.append(at < count - step)
        return found[0] if len(found) == 1 else jnp.logical_and(*found)

    loads = [
        pltpu.make_async_copy(src, dst, sent.at[i])
        for i, (src, dst) in enumerate((
            (mat_hbm, mat_ref), (head_hbm, head_ref), (flag_hbm, flag_ref), (cot_hbm, cot_ref), (perm_hbm, perm_tab), (poro_hbm, poro_tab)
        ))
    ]
    for load in loads:
        load.start()

    barrier = pltpu.get_barrier_semaphore()
    expected = jnp.int32(0)
    for dx, dy in PARTNERS:
        there = fits(dx, dy)

        @pl.when(there)
        def _():
            pl.semaphore_signal(barrier, inc=1, device_id=device(dx, dy), device_id_type=MESH)

        expected = expected + there.astype(jnp.int32)

    def rows_of(side, setup):
        dx, dy = side
        if side in FAR:
            return 0
        if setup:
            count = len(slots_of(side, True)) * (2 if dx != 0 and dy != 0 else 8)
            return -(-count // 8) * 8
        return 8 if dx != 0 and dy != 0 else 32

    def setup_copy(i):
        dx, dy = SIDES[i]
        part = pl.ds(0, rows_of((dx, dy), True) + (24 if i >= 4 else 0))
        at = PARTNERS.index((dx, dy))
        return pltpu.make_async_remote_copy(
            ssend.at[i, part], srecv.at[i, part], sent.at[at], came.at[1, at], device_id=device(-dx, -dy), device_id_type=MESH
        )

    def edge_copy(i):
        dx, dy = FAR[i]
        return pltpu.make_async_remote_copy(
            xsend.at[0 if dx < 0 else 1], xrecv.at[i], sent.at[i], came.at[1, i], device_id=device(-dx, -dy), device_id_type=MESH
        )

    def round_copy(i, k):
        dx, dy = PARTNERS[i]
        part = pl.ds(0, rows_of((dx, dy), False) + (16 if dx == 0 else 8))
        return pltpu.make_async_remote_copy(
            rsend.at[k, i, part], rrecv.at[k, i, part], sent.at[i], came.at[lax.rem(k, 2), i], device_id=device(-dx, -dy), device_id_type=MESH
        )

    def coef_copy(j):
        dx, dy = NEAR[j]
        at = PARTNERS.index((dx, dy)) if abs(dy) == 2 else N_PART + j - 2
        return pltpu.make_async_remote_copy(
            ksend, krecv.at[j], sent.at[at], came.at[1, at], device_id=device(-dx, -dy), device_id_type=MESH
        )

    def when_sent(side, act):
        pl.when(fits(-side[0], -side[1]))(act)

    def when_there(side, act):
        pl.when(fits(*side))(act)

    zero_rows = jnp.zeros((ROWS, LANES), jnp.float32)
    ext[MAT] = zero_rows - 1.0
    for f in range(1, 7):
        ext[f] = zero_rows
    for load in loads:
        load.wait()
    for x in range(8):
        ext[MAT, rows(x, 0), :] = mat_ref[x].astype(jnp.float32)
        ext[HEAD, rows(x, 0), :] = head_ref[x]
        for d in range(3):
            ext[F0 + d, rows(x, 0), :] = flag_ref[d, x].astype(jnp.float32)
        for f in range(2):
            ext[COT + f, rows(x, 0), :] = cot_ref[f, x]
    for i, x in enumerate((7, 0)):
        for m, field in enumerate((MAT, HEAD, F0)):
            xsend[i, pl.ds(8 * m, 8), :] = ext[field, rows(x, 0), :]
    for i, side in enumerate(SIDES):
        pack(side, True, ext, ssend, (i,))
        if i >= 4:
            ssend[i, pl.ds(24, 24), :] = xsend[0 if side[0] < 0 else 1]

    pl.semaphore_wait(barrier, expected)
    for i in reversed(range(8)):
        when_sent(SIDES[i], lambda: setup_copy(i).start())
    for i in range(4):
        when_sent(FAR[i], lambda: edge_copy(i).start())

    mask[...] = zero_rows
    perm[...] = zero_rows
    poro[...] = zero_rows
    for f in range(2):
        adj[f] = zero_rows
        inc[f] = zero_rows
        grd[f] = zero_rows
        mid[f] = zero_rows
    for m in range(9):
        face[m, pl.ds(0, 32), :] = jnp.zeros((32, LANES), jnp.float32)
    for x in range(-1, 9):
        mask[rows(x, -1, 10), :] = jnp.ones((10, LANES), jnp.float32)

    def look_up(mats):
        perm_here = jnp.zeros_like(mats)
        poro_here = jnp.zeros_like(mats)
        for level in range(perm_tab.shape[0]):
            same = mats == float(level)
            perm_here = jnp.where(same, perm_tab[level], perm_here)
            poro_here = jnp.where(same, poro_tab[level], poro_here)
        return perm_here, poro_here

    def one_face(perm_here, head_here, perm_next, head_next, upwind):
        both = perm_here + perm_next
        trans = 2.0 * perm_here * perm_next / jnp.where(both > 0.0, both, 1.0)
        flux = trans * (0.5 + jnp.abs(head_here - head_next))
        return trans, upwind * flux, (1.0 - upwind) * flux

    def look_up_rows(first, end, n):
        for lo in range(first, end, n):
            here = pl.ds(lo, n)
            perm[here, :], poro[here, :] = look_up(ext[MAT, here, :])

    def face_rows(first, end, n):
        for lo in range(first, end, n):
            here = pl.ds(lo, n)
            perm_here, head_here = perm[here, :], ext[HEAD, here, :]
            lane = lax.broadcasted_iota(jnp.int32, (n, LANES), 1)
            for d in range(3):
                if d < 2:
                    there = pl.ds(lo + (PITCH, 1)[d], n)
                    perm_next, head_next = perm[there, :], ext[HEAD, there, :]
                else:
                    perm_next = jnp.where(lane == LANES - 1, 0.0, next_lane(perm_here))
                    head_next = next_lane(head_here)
                values = one_face(perm_here, head_here, perm_next, head_next, ext[F0 + d, here, :])
                for m in range(3):
                    face[3 * d + m, here, :] = values[m]

    look_up_rows(32, 128, 32)
    face_rows(32, 128, 24)

    def put(ref, at, value):
        value = four_sum(value)
        ref[pl.ds(at, 1), :] = value[0:1]
        ref[pl.ds(at + 1, 1), :] = value[4:5]

    lane = lax.broadcasted_iota(jnp.int32, (8, LANES), 1)
    for cx in range(2):
        sums = [0.0] * 7
        for x in range(4 * cx, 4 * cx + 4):
            here = rows(x, 0)
            zs = [face[6 + m, here, :] for m in range(3)]
            out = face[1, here, :] + face[4, here, :] + zs[1]
            out = out + face[2, rows(x - 1, 0), :] + face[5, rows(x, -1), :] + last_lane(zs[2])
            news = [poro[here, :], out] + zs + [ext[COT + f, here, :] for f in range(2)]
            sums = [old + new for old, new in zip(sums, news)]
        for m in range(2, 5):
            sums[m] = jnp.where(lane % AGG == AGG - 1, sums[m], 0.0)
        for item, value in zip((0, 2, 4, 6, 8, 13, 15), sums):
            put(ksend, 2 * (item + cx), value)
    for m in range(3):
        put(ksend, 2 * (10 + m), face[m, rows(3, 0), :])
        put(ksend, 2 * (17 + m), face[3 + m, column(3), :])
    ksend[pl.ds(0, C_RAW), :] = lane_sum(ksend[pl.ds(0, C_RAW), :])
    raw = [
        (MAT, rows(0, 0)), (HEAD, rows(0, 0)), (MAT, rows(7, 0)), (HEAD, rows(7, 0)), (F0, rows(7, 0)),
        (MAT, column(0)), (HEAD, column(0)), (MAT, column(7)), (HEAD, column(7)), (F1, column(7)),
    ]
    for slot, (field, where) in enumerate(raw):
        ksend[pl.ds(C_RAW + 8 * slot, 8), :] = ext[field, where, :]
    for j in range(4):
        when_sent(NEAR[j], lambda: coef_copy(j).start())

    for i, side in enumerate(SIDES):

        @pl.when(jnp.logical_not(fits(*side)))
        def _():
            srecv[i] = jnp.zeros((80, LANES), jnp.float32)

    for i, side in enumerate(PARTNERS):

        @pl.when(jnp.logical_not(fits(*side)))
        def _():
            for k in range(ROUNDS):
                rrecv[k, i] = jnp.zeros((48, LANES), jnp.float32)

    for j, side in enumerate(NEAR):

        @pl.when(jnp.logical_not(fits(*side)))
        def _():
            krecv[j] = jnp.zeros((C_ROWS, LANES), jnp.float32)

    for j, side in enumerate(FAR[:4]):

        @pl.when(jnp.logical_not(fits(*side)))
        def _():
            xrecv[j] = jnp.zeros((24, LANES), jnp.float32)

    for i, side in enumerate(SIDES):
        when_there(side, lambda: setup_copy(i).wait_recv())
        unpack(side, True, srecv, (i,), ext, fits(*side))
    look_up_rows(0, ROWS, 32)
    face_rows(0, 144, 24)
    for lo in range(16, 144, 16):
        here = pl.ds(lo, 16)
        total = jnp.zeros((16, LANES), jnp.float32)
        out = total
        for d in range(3):
            trans, upper, lower = (face[3 * d + m, here, :] for m in range(3))
            if d < 2:
                back = pl.ds(lo - (PITCH, 1)[d], 16)
                trans_m, lower_m = face[3 * d, back, :], face[3 * d + 2, back, :]
            else:
                trans_m, lower_m = last_lane(trans), last_lane(lower)
            co[TX + 2 * d, here, :] = trans
            co[TX + 2 * d + 1, here, :] = trans_m
            co[SX + 2 * d, here, :] = DISP * trans + upper
            co[SX + 2 * d + 1, here, :] = DISP * trans_m + lower_m
            total = total + trans + trans_m
            out = out + upper + lower_m
        store = poro[here, :]
        bpp, bpc, bcp, bcc = store + total, -CPL_S * out, CPL_P * store, store + DISP * total + out
        inside = jnp.logical_and(store > 0.0, mask[here, :] > 0.0)
        determ = jnp.where(inside, bpp * bcc - bpc * bcp, 1.0)
        scale = jnp.where(inside, OMEGA / determ, 0.0)
        for at, value in (
            (BPP, bpp), (BPC, bpc), (BCP, bcp), (BCC, bcc),
            (IPP, bcc * scale), (IPC, -bpc * scale), (ICP, -bcp * scale), (ICC, bpp * scale),
        ):
            co[at, here, :] = value

    def fine_solve(src, at):
        for lo in range(16, 144, 32):
            here = pl.ds(lo, 32)
            r_p, r_c = src[at, here, :], src[at + 1, here, :]
            grd[0, here, :] = co[IPP, here, :] * r_p + co[IPC, here, :] * r_c
            grd[1, here, :] = co[ICP, here, :] * r_p + co[ICC, here, :] * r_c
        for lo in range(16, 144, 16):
            here = pl.ds(lo, 16)
            z_p, s_p, z_c, s_c = couple(co, grd, lo, 16)
            mid[0, here, :] = (2.0 - OMEGA) * z_p + co[IPP, here, :] * s_p + co[IPC, here, :] * s_c
            mid[1, here, :] = (2.0 - OMEGA) * z_c + co[ICP, here, :] * s_p + co[ICC, here, :] * s_c
        for lo in range(32, 128, 16):
            here = pl.ds(lo, 16)
            z_p, s_p, z_c, s_c = couple(co, mid, lo, 16)
            fin[0, here, :] = (1.0 - OMEGA) * z_p + grd[0, here, :] + co[IPP, here, :] * s_p + co[IPC, here, :] * s_c
            fin[1, here, :] = (1.0 - OMEGA) * z_c + grd[1, here, :] + co[ICP, here, :] * s_p + co[ICC, here, :] * s_c

    def coarse_solve():
        ipp, ipc, icp, icc = ([cco[b, cx] for cx in range(2)] for b in range(4))
        t_y, a_y, b_y, t_z, a_z, b_z = ([cco[b, cx] for cx in range(2)] for b in range(4, 10))
        t_x, a_x, b_x = (cco[b, 0] for b in range(10, 13))
        ahead = {0: (t_y, t_z), 1: (a_y, a_z)}
        behind = {
            0: ([pltpu.roll(v, 1, 0) for v in t_y], [last_lane(v, AGG) for v in t_z]),
            1: ([pltpu.roll(v, 1, 0) for v in b_y], [last_lane(v, AGG) for v in b_z]),
        }
        across = {0: (t_x, t_x), 1: (a_x, b_x)}
        r = [[cres[2 * f + cx] for cx in range(2)] for f in range(2)]
        base = [
            [ipp[cx] * r[0][cx] + ipc[cx] * r[1][cx] for cx in range(2)],
            [icp[cx] * r[0][cx] + icc[cx] * r[1][cx] for cx in range(2)],
        ]
        z = base
        for sweep in range(3):
            acc = [[None] * 2 for f in range(2)]
            for f in range(2):
                for cx in range(2):
                    v = z[f][cx]
                    total = across[f][cx] * z[f][1 - cx]
                    total = total + ahead[f][0][cx] * pltpu.roll(v, 7, 0)
                    total = total + behind[f][0][cx] * pltpu.roll(v, 1, 0)
                    total = total + ahead[f][1][cx] * next_lane(v, AGG)
                    acc[f][cx] = total + behind[f][1][cx] * last_lane(v, AGG)
            z = [
                [(1.0 - OMEGA_C) * z[0][cx] + base[0][cx] + ipp[cx] * acc[0][cx] + ipc[cx] * acc[1][cx] for cx in range(2)],
                [(1.0 - OMEGA_C) * z[1][cx] + base[1][cx] + icp[cx] * acc[0][cx] + icc[cx] * acc[1][cx] for cx in range(2)],
            ]
        upper = lax.broadcasted_iota(jnp.int32, (8, LANES), 0) < AGG
        return [
            [
                jnp.where(upper, jnp.broadcast_to(v[3:4], (8, LANES)), jnp.broadcast_to(v[4:5], (8, LANES)))
                for v in z[f]
            ]
            for f in range(2)
        ]

    def update():
        grown = coarse_solve()
        for f in range(2):
            for x in range(8):
                here = rows(x, 0)
                more = THETA * (fin[f, here, :] + grown[f][x // 4])
                new = adj[f, here, :] + more
                inc[f, here, :] = more
                adj[f, here, :] = new
                out_ref[f, x] = new

    def send(k):
        for lo in range(16, 144, 16):
            here = pl.ds(lo, 16)
            z_p, s_p, z_c, s_c = couple(co, inc, lo, 16)
            res[0, here, :] = co[BPP, here, :] * z_p + co[BPC, here, :] * z_c - s_p
            res[1, here, :] = co[BCP, here, :] * z_p + co[BCC, here, :] * z_c - s_c

        def place(at, value):
            ring[pl.ds(at, 1), :] = value

        for f in range(2):
            for cx in range(2):
                total = res[f, rows(4 * cx, 0), :]
                for x in range(4 * cx + 1, 4 * cx + 4):
                    total = total + res[f, rows(x, 0), :]
                total = four_sum(total)
                place(8 * f + 4 * cx + 1, total[0:1])
                place(8 * f + 4 * cx + 2, total[4:5])
            for at, y in ((0, -1), (3, 8)):
                total = four_sum(res[f, column(y), :])
                place(8 * f + at, total[0:1])
                place(8 * f + 4 + at, total[4:5])
            for at, x in ((16, -1), (20, 8)):
                total = four_sum(res[f, rows(x, 0), :])
                place(at + 2 * f, total[0:1])
                place(at + 2 * f + 1, total[4:5])
        ring[...] = lane_sum(ring[...])
        along, beside = ring[pl.ds(0, 16), :], ring[pl.ds(16, 8), :]
        for i, side in enumerate(PARTNERS):
            if side not in FAR:
                pack(side, False, adj, rsend, (k, i))
            at = rows_of(side, False)
            if side[0] == 0:
                rsend[k, i, pl.ds(at, 16), :] = along
            else:
                rsend[k, i, pl.ds(at, 8), :] = beside
            when_sent(side, lambda: round_copy(i, k).start())

    def receive(k):
        for i, side in enumerate(PARTNERS):
            when_sent(side, lambda: round_copy(i, k).wait_send())
        for i, side in enumerate(PARTNERS):
            when_there(side, lambda: round_copy(i, k).wait_recv())
            if side not in FAR:
                unpack(side, False, rrecv, (k, i), adj, None)
        for f in range(2):
            for cx in range(2):
                item = 2 * f + cx

                def along(dy, first, count):
                    i = PARTNERS.index((0, dy))
                    return rrecv[k, i, pl.ds(rows_of((0, dy), False) + 4 * item + first, count), :]

                layer[0, item, pl.ds(0, 4), :] = along(-1, 0, 4)
                layer[0, item, pl.ds(4, 4), :] = along(1, 0, 4)
                layer[1, item, pl.ds(0, 2), :] = along(-2, 2, 2)
                layer[1, item, pl.ds(2, 4), :] = ring[pl.ds(4 * item, 4), :]
                layer[1, item, pl.ds(6, 2), :] = along(2, 0, 2)
                dx = 2 * cx - 1
                for dy in range(-2, 3):
                    first, count = max(2 * dy + 3, 0), 1 if abs(dy) == 2 else 2
                    at = rows_of((dx, dy), False) + (4 if dx < 0 else 0) + 2 * f + (1 if dy == -2 else 0)
                    layer[2, item, pl.ds(first, count), :] = rrecv[k, PARTNERS.index((dx, dy)), pl.ds(at, count), :]
                cres[item] = cres[item] - layer[0, item] - layer[1, item] - layer[2, item]
        for lo in range(16, 144, 16):
            here = pl.ds(lo, 16)
            z_p, s_p, z_c, s_c = couple(co, adj, lo, 16)
            res[0, here, :] = ext[COT, here, :] + s_p - co[BPP, here, :] * z_p - co[BPC, here, :] * z_c
            res[1, here, :] = ext[COT + 1, here, :] + s_c - co[BCP, here, :] * z_p - co[BCC, here, :] * z_c

    fine_solve(ext, COT)

    for i, side in enumerate(SIDES):
        when_sent(side, lambda: setup_copy(i).wait_send())
    for j, side in enumerate(NEAR):
        when_sent(side, lambda: coef_copy(j).wait_send())
        when_sent(FAR[j], lambda: edge_copy(j).wait_send())
    for j in range(4):
        when_there(NEAR[j], lambda: coef_copy(j).wait_recv())
        when_there(FAR[j], lambda: edge_copy(j).wait_recv())

    def near(u):
        return NEAR.index((0, u))

    def inner(u, at, count):
        return (ksend[pl.ds(at, count), :] if u == 0 else krecv[near(u), pl.ds(at, count), :])

    def raw_of(u, slot):
        value = inner(u, C_RAW + 8 * slot, 8)
        return jnp.where(fits(0, u), value, -1.0) if u != 0 and slot in (0, 2, 5, 7) else value

    def beyond(dx, u, m):
        if u == 0:
            return ext[(MAT, HEAD, F0)[m], rows(-1 if dx < 0 else 8, 0), :]
        if abs(u) == 1:
            value = srecv[SIDES.index((dx, u)), pl.ds(24 + 8 * m, 8), :]
        else:
            value = xrecv[FAR.index((dx, u)), pl.ds(8 * m, 8), :]
        return jnp.where(fits(dx, u), value, -1.0) if m == 0 else value

    def between(mat_a, head_a, flag, mat_b, head_b):
        return one_face(look_up(mat_a)[0], head_a, look_up(mat_b)[0], head_b, flag)

    def put_rows(tile, u, value):
        value = four_sum(value)
        if u > -2:
            cedge[tile, pl.ds(2 * u + 3, 1), :] = value[0:1]
        if u < 2:
            cedge[tile, pl.ds(2 * u + 4, 1), :] = value[4:5]

    for tile in range(4, 10):
        cedge[tile] = jnp.zeros((8, LANES), jnp.float32)
    for u in range(-2, 3):
        trans, _, lower = between(*(beyond(-1, u, m) for m in range(3)), raw_of(u, 0), raw_of(u, 1))
        put_rows(0, u, trans)
        put_rows(1, u, lower)
        trans, upper, _ = between(raw_of(u, 2), raw_of(u, 3), raw_of(u, 4), beyond(1, u, 0), beyond(1, u, 1))
        put_rows(2, u, trans)
        put_rows(3, u, upper)
        if u < 2:
            values = between(raw_of(u, 7), raw_of(u, 8), raw_of(u, 9), raw_of(u + 1, 5), raw_of(u + 1, 6))
            for m in range(3):
                value = four_sum(values[m])
                for cx in range(2):
                    cedge[4 + 2 * m + cx, pl.ds(2 * u + 4, 1), :] = value[4 * cx : 4 * cx + 1]
    for tile in range(10):
        cedge[tile] = lane_sum(cedge[tile])
    for m in range(3):
        for cx in range(2):
            for u in range(-1, 3):
                cedge[4 + 2 * m + cx, pl.ds(2 * u + 3, 1), :] = inner(u, 34 + 2 * m + cx, 1)
    for item in range(N_INNER):

        def put_inner(where, value):
            if item < 13:
                cin[item, where, :] = value
            else:
                cres[item - 13, where, :] = value

        put_inner(pl.ds(0, 1), inner(-2, 2 * item + 1, 1))
        put_inner(pl.ds(1, 2), inner(-1, 2 * item, 2))
        put_inner(pl.ds(3, 2), inner(0, 2 * item, 2))
        put_inner(pl.ds(5, 2), inner(1, 2 * item, 2))
        put_inner(pl.ds(7, 1), inner(2, 2 * item, 1))

    place = lax.broadcasted_iota(jnp.int32, (8, LANES), 0)
    m_t, m_a, m_b = (cin[10 + m] for m in range(3))
    for cx in range(2):
        store, out, t_z, a_z, b_z = (cin[2 * m + cx] for m in range(5))
        t_y, a_y, b_y = (cedge[4 + 2 * m + cx] for m in range(3))
        under_t, under_b = (
            jnp.where(place == 0, jnp.broadcast_to(inner(-2, 34 + 2 * m + cx, 1), (8, LANES)), pltpu.roll(value, 1, 0))
            for m, value in ((0, t_y), (2, b_y))
        )
        side_t, side_out = (cedge[0], cedge[1]) if cx == 0 else (cedge[2], cedge[3])
        edge_sum = m_t + side_t + t_y + under_t + t_z + last_lane(t_z, AGG)
        edge_out = (m_a if cx == 0 else m_b) + side_out + a_y + under_b + a_z + last_lane(b_z, AGG)
        out = out + side_out + jnp.where(place % 2 == 0, a_y, under_b)
        cpp, cpc, ccp, ccc = store + edge_sum, -CPL_S * out, CPL_P * store, store + DISP * edge_sum + edge_out
        inside = cpp > 0.0
        determ = jnp.where(inside, cpp * ccc - cpc * ccp, 1.0)
        scale = jnp.where(inside, OMEGA_C / determ, 0.0)
        for b, value in enumerate((
            ccc * scale, -cpc * scale, -ccp * scale, cpp * scale,
            t_y, DISP * t_y + a_y, DISP * t_y + b_y,
            t_z, DISP * t_z + a_z, DISP * t_z + b_z,
            m_t, DISP * m_t + m_a, DISP * m_t + m_b,
        )):
            cco[b, cx] = value
    update()
    send(0)

    def step(k, carry):
        receive(k - 1)
        fine_solve(res, 0)
        update()
        pl.when(k < ITERS - 1)(lambda: send(k))
        return carry

    lax.fori_loop(1, ITERS, step, 0)


def solution(mesh):
    n_grp, n_sub = mesh.shape["grp"], mesh.shape["sub"]

    def local(cotangent, head, materials, flags, perm_table, poro_table):
        def tile(*shape):
            return pltpu.VMEM(shape + (LANES,), jnp.float32)

        dma = pltpu.SemaphoreType.DMA
        vmem = pl.BlockSpec(memory_space=pltpu.VMEM)
        hbm = pl.BlockSpec(memory_space=pltpu.HBM)
        return pl.pallas_call(
            functools.partial(kernel, n_grp, n_sub),
            out_shape=pltpu.VMEM(cotangent.shape, jnp.float32),
            in_specs=[hbm] * 6,
            out_specs=vmem,
            scratch_shapes=[
                pltpu.VMEM(cotangent.shape, jnp.float32),
                pltpu.VMEM(head.shape, jnp.float32),
                pltpu.VMEM(materials.shape, jnp.int32),
                pltpu.VMEM(flags.shape, jnp.int32),
                pltpu.SMEM(perm_table.shape, jnp.float32),
                pltpu.SMEM(poro_table.shape, jnp.float32),
                tile(7, ROWS),
                tile(ROWS),
                tile(ROWS),
                tile(ROWS),
                tile(9, ROWS),
                tile(N_COEF, ROWS),
                tile(2, ROWS),
                tile(2, ROWS),
                tile(2, ROWS),
                tile(2, ROWS),
                tile(2, ROWS),
                tile(2, ROWS),
                tile(8, 80),
                tile(8, 80),
                tile(ROUNDS, N_PART, 48),
                tile(ROUNDS, N_PART, 48),
                tile(2, 24),
                tile(4, 24),
                tile(C_ROWS),
                tile(4, C_ROWS),
                tile(13, 8),
                tile(10, 8),
                tile(24),
                tile(N_CBLK, 2, 8),
                tile(4, 8),
                tile(3, 4, 8),
                dma((N_PART + 2,)),
                dma((2, N_PART + 2)),
            ],
            compiler_params=pltpu.CompilerParams(
                collective_id=0, has_side_effects=True, vmem_limit_bytes=32 * 1024 * 1024
            ),
        )(*(pltpu.with_memory_space_constraint(x, pltpu.HBM) for x in (cotangent, head, materials, flags, perm_table, poro_table)))

    return jax.shard_map(
        local,
        mesh=mesh,
        in_specs=(
            P(None, "grp", "sub", None),
            P("grp", "sub", None),
            P("grp", "sub", None),
            P(None, "grp", "sub", None),
            P(),
            P(),
        ),
        out_specs=P(None, "grp", "sub", None),
        check_vma=False,
    )
```

```python
import functools

import jax
import jax.numpy as jnp
from jax import lax
from jax.experimental import pallas as pl
from jax.experimental.pallas import tpu as pltpu
from jax.sharding import PartitionSpec as P

CX = 8
AGG = 4
ITERS = 4
DISP = 0.2
CPL_P = 0.5
CPL_S = 0.3
OMEGA = 0.7
OMEGA_C = 0.7
THETA = 0.5

PITCH = 12
BASE = 8
ROWS = 160
LANES = 128
MESH = pl.DeviceIdType.MESH

SIDES = [(-1, 0), (1, 0), (0, -1), (0, 1), (-1, -1), (-1, 1), (1, -1), (1, 1)]
FAR = [(-1, -2), (-1, 2), (1, -2), (1, 2), (0, -2), (0, 2)]
PARTNERS = FAR + SIDES[4:] + SIDES[:4]
NEAR = [(0, -2), (0, 2), (0, -1), (0, 1)]

MAT, HEAD, F0, F1, F2, COT = 0, 1, 2, 3, 4, 5
TX, TXM, TY, TYM, TZ, TZM, SX, SXM, SY, SYM, SZ, SZM, BPP, BPC, BCP, BCC, IPP, IPC, ICP, ICC = range(20)
N_COEF = 20
N_CBLK = 14
N_INNER = 17
C_ROWS = 120
C_RAW = 40
PAD = 40
R_ROWS = 64
ROUNDS = ITERS - 1
N_PART = 14


def row(x, y):
    return BASE + (x + 2) * PITCH + y + 2


def rows(x, y, count=8):
    return pl.ds(row(x, y), count)


def column(y):
    return pl.ds(row(0, y), 8, stride=PITCH)


def setup_slots(low, along):
    one, two = (-1, -2) if low else (8, 9)
    first = [(MAT, one), (HEAD, one), (along, one)]
    others = [(field, one) for field in (F0, F1, F2) if field != along]
    return first + others + [(MAT, two), (HEAD, two)] + ([(along, two)] if low else []) + [(COT, one), (COT + 1, one)]


def field_slots(low):
    return [(f, layer) for f in (0, 1) for layer in ((-2, -1) if low else (8, 9))]


def slots_of(side, setup):
    dx, dy = side
    if dx != 0:
        return setup_slots(dx < 0, F0) if setup else field_slots(dx < 0)
    return setup_slots(dy < 0, F1) if setup else field_slots(dy < 0)


def pack(side, setup, src, dst, lead, base=0):
    dx, dy = side
    for slot, (field, layer) in enumerate(slots_of(side, setup)):
        if dy == 0:
            dst[lead + (pl.ds(base + 8 * slot, 8),)] = src[field, rows(layer % 8, 0), :]
        elif dx == 0:
            dst[lead + (pl.ds(base + 8 * slot, 8),)] = src[field, column(layer % 8), :]
        else:
            dst[lead + (pl.ds(base + 2 * slot, 2),)] = src[field, rows(layer % 8, 6 if dy < 0 else 0, 2), :]


def unpack(side, setup, src, lead, dst, valid, base=0):
    dx, dy = side

    def seen(field, value):
        return jnp.where(valid, value, -1.0) if setup and field == MAT else value

    for slot, (field, layer) in enumerate(slots_of(side, setup)):
        if dy == 0:
            dst[field, rows(layer, 0), :] = seen(field, src[lead + (pl.ds(base + 8 * slot, 8),)])
        elif dx == 0:
            dst[field, column(layer), :] = seen(field, src[lead + (pl.ds(base + 8 * slot, 8),)])
        else:
            dst[field, rows(layer, -2 if dy < 0 else 8, 2), :] = seen(field, src[lead + (pl.ds(base + 2 * slot, 2),)])


def next_lane(value, by=1):
    return pltpu.roll(value, LANES - by, 1)


def last_lane(value, by=1):
    return pltpu.roll(value, by, 1)


def lane_sum(value):
    lane = lax.broadcasted_iota(jnp.int32, value.shape, 1)
    total = value + jnp.where(lane % 2 == 0, next_lane(value), last_lane(value))
    return total + jnp.where(lane % AGG < 2, next_lane(total, 2), last_lane(total, 2))


def four_sum(value):
    total = value + pltpu.roll(value, 7, 0)
    return total + pltpu.roll(total, 6, 0)


def couple(co, field, lo, n):
    here = pl.ds(lo, n)
    out = []
    for f, first in ((0, TX), (1, SX)):
        mid = field[f, here, :]
        total = co[first, here, :] * field[f, pl.ds(lo + PITCH, n), :]
        total = total + co[first + 1, here, :] * field[f, pl.ds(lo - PITCH, n), :]
        total = total + co[first + 2, here, :] * field[f, pl.ds(lo + 1, n), :]
        total = total + co[first + 3, here, :] * field[f, pl.ds(lo - 1, n), :]
        total = total + co[first + 4, here, :] * next_lane(mid)
        total = total + co[first + 5, here, :] * last_lane(mid)
        out += [mid, total]
    return out


def kernel(
    n_grp,
    n_sub,
    cot_hbm,
    head_hbm,
    mat_hbm,
    flag_hbm,
    perm_hbm,
    poro_hbm,
    out_ref,
    cot_ref,
    head_ref,
    mat_ref,
    flag_ref,
    perm_tab,
    poro_tab,
    ext,
    perm,
    poro,
    mask,
    face,
    co,
    adj,
    inc,
    res,
    grd,
    mid,
    fin,
    ssend,
    srecv,
    rsend,
    rrecv,
    xsend,
    xrecv,
    ksend,
    krecv,
    cin,
    cedge,
    ring,
    cco,
    cres,
    sent,
    came,
):
    g = lax.axis_index("grp")
    s = lax.axis_index("sub")

    def device(dx, dy):
        return {"grp": g + dx, "sub": s + dy}

    def fits(dx, dy):
        found = []
        for at, count, step in ((g, n_grp, dx), (s, n_sub, dy)):
            if step < 0:
                found.append(at >= -step)
            elif step > 0:
                found.append(at < count - step)
        return found[0] if len(found) == 1 else jnp.logical_and(*found)

    loads = [
        pltpu.make_async_copy(src, dst, sent.at[i])
        for i, (src, dst) in enumerate((
            (mat_hbm, mat_ref), (head_hbm, head_ref), (flag_hbm, flag_ref), (cot_hbm, cot_ref), (perm_hbm, perm_tab), (poro_hbm, poro_tab)
        ))
    ]
    for load in loads:
        load.start()

    barrier = pltpu.get_barrier_semaphore()
    expected = jnp.int32(0)
    for dx, dy in PARTNERS:
        there = fits(dx, dy)

        @pl.when(there)
        def _():
            pl.semaphore_signal(barrier, inc=1, device_id=device(dx, dy), device_id_type=MESH)

        expected = expected + there.astype(jnp.int32)

    def rows_of(side, setup):
        dx, dy = side
        if side in FAR:
            return 0
        if setup:
            count = len(slots_of(side, True)) * (2 if dx != 0 and dy != 0 else 8)
            return -(-count // 8) * 8
        return 8 if dx != 0 and dy != 0 else 32

    def setup_copy(i):
        dx, dy = SIDES[i]
        part = pl.ds(0, rows_of((dx, dy), True) + (24 if i >= 4 else 0))
        at = PARTNERS.index((dx, dy))
        return pltpu.make_async_remote_copy(
            ssend.at[i, part], srecv.at[i, part], sent.at[at], came.at[1, at], device_id=device(-dx, -dy), device_id_type=MESH
        )

    def edge_copy(i):
        dx, dy = FAR[i]
        return pltpu.make_async_remote_copy(
            xsend.at[0 if dx < 0 else 1], xrecv.at[i], sent.at[i], came.at[1, i], device_id=device(-dx, -dy), device_id_type=MESH
        )

    def round_copy(i, k):
        dx, dy = PARTNERS[i]
        halo = rows_of((dx, dy), False)
        part = pl.ds(PAD - halo, halo + (16 if dx == 0 else 8))
        return pltpu.make_async_remote_copy(
            rsend.at[k, i, part], rrecv.at[k, i, part], sent.at[i], came.at[lax.rem(k, 2), i], device_id=device(-dx, -dy), device_id_type=MESH
        )

    def coef_copy(j):
        dx, dy = NEAR[j]
        at = PARTNERS.index((dx, dy)) if abs(dy) == 2 else N_PART + j - 2
        return pltpu.make_async_remote_copy(
            ksend, krecv.at[j], sent.at[at], came.at[1, at], device_id=device(-dx, -dy), device_id_type=MESH
        )

    def when_sent(side, act):
        pl.when(fits(-side[0], -side[1]))(act)

    def when_there(side, act):
        pl.when(fits(*side))(act)

    zero_rows = jnp.zeros((ROWS, LANES), jnp.float32)
    ext[MAT] = zero_rows - 1.0
    for f in range(1, 7):
        ext[f] = zero_rows
    for load in loads:
        load.wait()
    for x in range(8):
        ext[MAT, rows(x, 0), :] = mat_ref[x].astype(jnp.float32)
        ext[HEAD, rows(x, 0), :] = head_ref[x]
        for d in range(3):
            ext[F0 + d, rows(x, 0), :] = flag_ref[d, x].astype(jnp.float32)
        for f in range(2):
            ext[COT + f, rows(x, 0), :] = cot_ref[f, x]
    for i, x in enumerate((7, 0)):
        for m, field in enumerate((MAT, HEAD, F0)):
            xsend[i, pl.ds(8 * m, 8), :] = ext[field, rows(x, 0), :]
    for i, side in enumerate(SIDES):
        pack(side, True, ext, ssend, (i,))
        if i >= 4:
            ssend[i, pl.ds(24, 24), :] = xsend[0 if side[0] < 0 else 1]

    pl.semaphore_wait(barrier, expected)
    for i in reversed(range(8)):
        when_sent(SIDES[i], lambda: setup_copy(i).start())
    for i in range(4):
        when_sent(FAR[i], lambda: edge_copy(i).start())

    mask[...] = zero_rows
    perm[...] = zero_rows
    poro[...] = zero_rows
    for f in range(2):
        adj[f] = zero_rows
        inc[f] = zero_rows
        grd[f] = zero_rows
        mid[f] = zero_rows
    for m in range(9):
        face[m, pl.ds(0, 32), :] = jnp.zeros((32, LANES), jnp.float32)
    for x in range(-1, 9):
        mask[rows(x, -1, 10), :] = jnp.ones((10, LANES), jnp.float32)

    def look_up(mats):
        perm_here = jnp.zeros_like(mats)
        poro_here = jnp.zeros_like(mats)
        for level in range(perm_tab.shape[0]):
            same = mats == float(level)
            perm_here = jnp.where(same, perm_tab[level], perm_here)
            poro_here = jnp.where(same, poro_tab[level], poro_here)
        return perm_here, poro_here

    def one_face(perm_here, head_here, perm_next, head_next, upwind):
        both = perm_here + perm_next
        trans = 2.0 * perm_here * perm_next / jnp.where(both > 0.0, both, 1.0)
        flux = trans * (0.5 + jnp.abs(head_here - head_next))
        return trans, upwind * flux, (1.0 - upwind) * flux

    def look_up_rows(first, end, n):
        for lo in range(first, end, n):
            here = pl.ds(lo, n)
            perm[here, :], poro[here, :] = look_up(ext[MAT, here, :])

    def face_rows(first, end, n):
        for lo in range(first, end, n):
            here = pl.ds(lo, n)
            perm_here, head_here = perm[here, :], ext[HEAD, here, :]
            lane = lax.broadcasted_iota(jnp.int32, (n, LANES), 1)
            for d in range(3):
                if d < 2:
                    there = pl.ds(lo + (PITCH, 1)[d], n)
                    perm_next, head_next = perm[there, :], ext[HEAD, there, :]
                else:
                    perm_next = jnp.where(lane == LANES - 1, 0.0, next_lane(perm_here))
                    head_next = next_lane(head_here)
                values = one_face(perm_here, head_here, perm_next, head_next, ext[F0 + d, here, :])
                for m in range(3):
                    face[3 * d + m, here, :] = values[m]

    look_up_rows(32, 128, 32)
    face_rows(32, 128, 24)

    def put(ref, at, value):
        value = four_sum(value)
        ref[pl.ds(at, 1), :] = value[0:1]
        ref[pl.ds(at + 1, 1), :] = value[4:5]

    lane = lax.broadcasted_iota(jnp.int32, (8, LANES), 1)
    for cx in range(2):
        sums = [0.0] * 7
        for x in range(4 * cx, 4 * cx + 4):
            here = rows(x, 0)
            zs = [face[6 + m, here, :] for m in range(3)]
            out = face[1, here, :] + face[4, here, :] + zs[1]
            out = out + face[2, rows(x - 1, 0), :] + face[5, rows(x, -1), :] + last_lane(zs[2])
            news = [poro[here, :], out] + zs + [ext[COT + f, here, :] for f in range(2)]
            sums = [old + new for old, new in zip(sums, news)]
        for m in range(2, 5):
            sums[m] = jnp.where(lane % AGG == AGG - 1, sums[m], 0.0)
        for item, value in zip((0, 2, 4, 6, 8, 13, 15), sums):
            put(ksend, 2 * (item + cx), value)
    for m in range(3):
        put(ksend, 2 * (10 + m), face[m, rows(3, 0), :])
        put(ksend, 2 * (17 + m), face[3 + m, column(3), :])
    ksend[pl.ds(0, C_RAW), :] = lane_sum(ksend[pl.ds(0, C_RAW), :])
    raw = [
        (MAT, rows(0, 0)), (HEAD, rows(0, 0)), (MAT, rows(7, 0)), (HEAD, rows(7, 0)), (F0, rows(7, 0)),
        (MAT, column(0)), (HEAD, column(0)), (MAT, column(7)), (HEAD, column(7)), (F1, column(7)),
    ]
    for slot, (field, where) in enumerate(raw):
        ksend[pl.ds(C_RAW + 8 * slot, 8), :] = ext[field, where, :]
    for j in range(4):
        when_sent(NEAR[j], lambda: coef_copy(j).start())

    for i, side in enumerate(SIDES):

        @pl.when(jnp.logical_not(fits(*side)))
        def _():
            srecv[i] = jnp.zeros((80, LANES), jnp.float32)

    for i, side in enumerate(PARTNERS):

        @pl.when(jnp.logical_not(fits(*side)))
        def _():
            for k in range(ROUNDS):
                rrecv[k, i] = jnp.zeros((R_ROWS, LANES), jnp.float32)

    for j, side in enumerate(NEAR):

        @pl.when(jnp.logical_not(fits(*side)))
        def _():
            krecv[j] = jnp.zeros((C_ROWS, LANES), jnp.float32)

    for j, side in enumerate(FAR[:4]):

        @pl.when(jnp.logical_not(fits(*side)))
        def _():
            xrecv[j] = jnp.zeros((24, LANES), jnp.float32)

    for i, side in enumerate(SIDES):
        when_there(side, lambda: setup_copy(i).wait_recv())
        unpack(side, True, srecv, (i,), ext, fits(*side))
    look_up_rows(0, ROWS, 32)
    face_rows(0, 144, 24)
    for lo in range(16, 144, 16):
        here = pl.ds(lo, 16)
        total = jnp.zeros((16, LANES), jnp.float32)
        out = total
        for d in range(3):
            trans, upper, lower = (face[3 * d + m, here, :] for m in range(3))
            if d < 2:
                back = pl.ds(lo - (PITCH, 1)[d], 16)
                trans_m, lower_m = face[3 * d, back, :], face[3 * d + 2, back, :]
            else:
                trans_m, lower_m = last_lane(trans), last_lane(lower)
            co[TX + 2 * d, here, :] = trans
            co[TX + 2 * d + 1, here, :] = trans_m
            co[SX + 2 * d, here, :] = DISP * trans + upper
            co[SX + 2 * d + 1, here, :] = DISP * trans_m + lower_m
            total = total + trans + trans_m
            out = out + upper + lower_m
        store = poro[here, :]
        bpp, bpc, bcp, bcc = store + total, -CPL_S * out, CPL_P * store, store + DISP * total + out
        inside = jnp.logical_and(store > 0.0, mask[here, :] > 0.0)
        determ = jnp.where(inside, bpp * bcc - bpc * bcp, 1.0)
        scale = jnp.where(inside, OMEGA / determ, 0.0)
        for at, value in (
            (BPP, bpp), (BPC, bpc), (BCP, bcp), (BCC, bcc),
            (IPP, bcc * scale), (IPC, -bpc * scale), (ICP, -bcp * scale), (ICC, bpp * scale),
        ):
            co[at, here, :] = value

    def fine_solve(src, at):
        for lo in range(16, 144, 32):
            here = pl.ds(lo, 32)
            r_p, r_c = src[at, here, :], src[at + 1, here, :]
            grd[0, here, :] = co[IPP, here, :] * r_p + co[IPC, here, :] * r_c
            grd[1, here, :] = co[ICP, here, :] * r_p + co[ICC, here, :] * r_c
        for lo in range(16, 144, 16):
            here = pl.ds(lo, 16)
            z_p, s_p, z_c, s_c = couple(co, grd, lo, 16)
            mid[0, here, :] = (2.0 - OMEGA) * z_p + co[IPP, here, :] * s_p + co[IPC, here, :] * s_c
            mid[1, here, :] = (2.0 - OMEGA) * z_c + co[ICP, here, :] * s_p + co[ICC, here, :] * s_c
        for lo in range(32, 128, 16):
            here = pl.ds(lo, 16)
            z_p, s_p, z_c, s_c = couple(co, mid, lo, 16)
            fin[0, here, :] = (1.0 - OMEGA) * z_p + grd[0, here, :] + co[IPP, here, :] * s_p + co[IPC, here, :] * s_c
            fin[1, here, :] = (1.0 - OMEGA) * z_c + grd[1, here, :] + co[ICP, here, :] * s_p + co[ICC, here, :] * s_c

    def coarse_solve():
        inv = [[cco[b, cx] for cx in range(2)] for b in range(4)]
        r = [[cres[2 * f + cx] for cx in range(2)] for f in range(2)]

        def inverse(v):
            return [[inv[2 * f][cx] * v[0][cx] + inv[2 * f + 1][cx] * v[1][cx] for cx in range(2)] for f in range(2)]

        base = inverse(r)
        z = base
        for sweep in range(3):
            acc = [[None] * 2 for f in range(2)]
            for f in range(2):
                for cx in range(2):
                    v = z[f][cx]
                    first = 4 + 5 * f
                    along = cco[first, cx] * pltpu.roll(v, 7, 0) + cco[first + 1, cx] * pltpu.roll(v, 1, 0)
                    down = cco[first + 2, cx] * next_lane(v, AGG) + cco[first + 3, cx] * last_lane(v, AGG)
                    acc[f][cx] = cco[first + 4, cx] * z[f][1 - cx] + (along + down)
            more = inverse(acc)
            z = [[((1.0 - OMEGA_C) * z[f][cx] + base[f][cx]) + more[f][cx] for cx in range(2)] for f in range(2)]
        upper = lax.broadcasted_iota(jnp.int32, (8, LANES), 0) < AGG
        return [
            [
                jnp.where(upper, jnp.broadcast_to(v[3:4], (8, LANES)), jnp.broadcast_to(v[4:5], (8, LANES)))
                for v in z[f]
            ]
            for f in range(2)
        ]

    def update():
        grown = coarse_solve()
        for f in range(2):
            for x in range(8):
                here = rows(x, 0)
                more = THETA * (fin[f, here, :] + grown[f][x // 4])
                new = adj[f, here, :] + more
                inc[f, here, :] = more
                adj[f, here, :] = new
                out_ref[f, x] = new

    def send(k):
        for lo in range(16, 144, 16):
            here = pl.ds(lo, 16)
            z_p, s_p, z_c, s_c = couple(co, inc, lo, 16)
            res[0, here, :] = co[BPP, here, :] * z_p + co[BPC, here, :] * z_c - s_p
            res[1, here, :] = co[BCP, here, :] * z_p + co[BCC, here, :] * z_c - s_c

        def place(at, value):
            ring[pl.ds(8 + at, 1), :] = value

        for f in range(2):
            for cx in range(2):
                total = res[f, rows(4 * cx, 0), :]
                for x in range(4 * cx + 1, 4 * cx + 4):
                    total = total + res[f, rows(x, 0), :]
                total = four_sum(total)
                place(8 * f + 4 * cx + 1, total[0:1])
                place(8 * f + 4 * cx + 2, total[4:5])
            for at, y in ((0, -1), (3, 8)):
                total = four_sum(res[f, column(y), :])
                place(8 * f + at, total[0:1])
                place(8 * f + 4 + at, total[4:5])
            for at, x in ((16, -1), (20, 8)):
                total = four_sum(res[f, rows(x, 0), :])
                place(at + 2 * f, total[0:1])
                place(at + 2 * f + 1, total[4:5])
        sums = lane_sum(ring[pl.ds(8, 24), :])
        ring[pl.ds(8, 24), :] = sums
        along, beside = sums[0:16], sums[16:24]
        for i, side in enumerate(PARTNERS):
            if side not in FAR:
                pack(side, False, adj, rsend, (k, i), PAD - rows_of(side, False))
            if side[0] == 0:
                rsend[k, i, pl.ds(PAD, 16), :] = along
            else:
                rsend[k, i, pl.ds(PAD, 8), :] = beside
            when_sent(side, lambda: round_copy(i, k).start())

    def receive(k):
        for i, side in enumerate(PARTNERS):
            when_sent(side, lambda: round_copy(i, k).wait_send())
        for i, side in enumerate(PARTNERS):
            when_there(side, lambda: round_copy(i, k).wait_recv())
            if side not in FAR:
                unpack(side, False, rrecv, (k, i), adj, None, PAD - rows_of(side, False))
        at_row = lax.broadcasted_iota(jnp.int32, (8, LANES), 0)
        for f in range(2):
            for cx in range(2):
                item = 2 * f + cx

                def along(dy, shift):
                    return rrecv[k, PARTNERS.index((0, dy)), pl.ds(PAD + 4 * item + shift, 8), :]

                def beside(dy):
                    dx = 2 * cx - 1
                    at = PAD + (4 if dx < 0 else 0) + 2 * f
                    return rrecv[k, PARTNERS.index((dx, dy)), pl.ds(at - 2 * dy - 3, 8), :]

                one = jnp.where(at_row < 4, along(-1, 0), along(1, -4))
                two = jnp.where(at_row < 2, along(-2, 2), jnp.where(at_row < 6, ring[pl.ds(8 + 4 * item - 2, 8), :], along(2, -6)))
                three = jnp.where(at_row < 1, beside(-2), jnp.where(at_row < 3, beside(-1), beside(0)))
                three = jnp.where(at_row < 5, three, jnp.where(at_row < 7, beside(1), beside(2)))
                cres[item] = cres[item] - ((one + two) + three)
        for lo in range(16, 144, 16):
            here = pl.ds(lo, 16)
            z_p, s_p, z_c, s_c = couple(co, adj, lo, 16)
            res[0, here, :] = ext[COT, here, :] + s_p - co[BPP, here, :] * z_p - co[BPC, here, :] * z_c
            res[1, here, :] = ext[COT + 1, here, :] + s_c - co[BCP, here, :] * z_p - co[BCC, here, :] * z_c

    fine_solve(ext, COT)

    for i, side in enumerate(SIDES):
        when_sent(side, lambda: setup_copy(i).wait_send())
    for j, side in enumerate(NEAR):
        when_sent(side, lambda: coef_copy(j).wait_send())
        when_sent(FAR[j], lambda: edge_copy(j).wait_send())
    for j in range(4):
        when_there(NEAR[j], lambda: coef_copy(j).wait_recv())
        when_there(FAR[j], lambda: edge_copy(j).wait_recv())

    def near(u):
        return NEAR.index((0, u))

    def inner(u, at, count):
        return (ksend[pl.ds(at, count), :] if u == 0 else krecv[near(u), pl.ds(at, count), :])

    def raw_of(u, slot):
        value = inner(u, C_RAW + 8 * slot, 8)
        return jnp.where(fits(0, u), value, -1.0) if u != 0 and slot in (0, 2, 5, 7) else value

    def beyond(dx, u, m):
        if u == 0:
            return ext[(MAT, HEAD, F0)[m], rows(-1 if dx < 0 else 8, 0), :]
        if abs(u) == 1:
            value = srecv[SIDES.index((dx, u)), pl.ds(24 + 8 * m, 8), :]
        else:
            value = xrecv[FAR.index((dx, u)), pl.ds(8 * m, 8), :]
        return jnp.where(fits(dx, u), value, -1.0) if m == 0 else value

    def between(mat_a, head_a, flag, mat_b, head_b):
        return one_face(look_up(mat_a)[0], head_a, look_up(mat_b)[0], head_b, flag)

    def put_rows(tile, u, value):
        value = four_sum(value)
        if u > -2:
            cedge[tile, pl.ds(2 * u + 3, 1), :] = value[0:1]
        if u < 2:
            cedge[tile, pl.ds(2 * u + 4, 1), :] = value[4:5]

    for tile in range(4, 10):
        cedge[tile] = jnp.zeros((8, LANES), jnp.float32)
    for u in range(-2, 3):
        trans, _, lower = between(*(beyond(-1, u, m) for m in range(3)), raw_of(u, 0), raw_of(u, 1))
        put_rows(0, u, trans)
        put_rows(1, u, lower)
        trans, upper, _ = between(raw_of(u, 2), raw_of(u, 3), raw_of(u, 4), beyond(1, u, 0), beyond(1, u, 1))
        put_rows(2, u, trans)
        put_rows(3, u, upper)
        if u < 2:
            values = between(raw_of(u, 7), raw_of(u, 8), raw_of(u, 9), raw_of(u + 1, 5), raw_of(u + 1, 6))
            for m in range(3):
                value = four_sum(values[m])
                for cx in range(2):
                    cedge[4 + 2 * m + cx, pl.ds(2 * u + 4, 1), :] = value[4 * cx : 4 * cx + 1]
    for tile in range(10):
        cedge[tile] = lane_sum(cedge[tile])
    for m in range(3):
        for cx in range(2):
            for u in range(-1, 3):
                cedge[4 + 2 * m + cx, pl.ds(2 * u + 3, 1), :] = inner(u, 34 + 2 * m + cx, 1)
    for item in range(N_INNER):

        def put_inner(where, value):
            if item < 13:
                cin[item, where, :] = value
            else:
                cres[item - 13, where, :] = value

        put_inner(pl.ds(0, 1), inner(-2, 2 * item + 1, 1))
        put_inner(pl.ds(1, 2), inner(-1, 2 * item, 2))
        put_inner(pl.ds(3, 2), inner(0, 2 * item, 2))
        put_inner(pl.ds(5, 2), inner(1, 2 * item, 2))
        put_inner(pl.ds(7, 1), inner(2, 2 * item, 1))

    place = lax.broadcasted_iota(jnp.int32, (8, LANES), 0)
    m_t, m_a, m_b = (cin[10 + m] for m in range(3))
    for cx in range(2):
        store, out, t_z, a_z, b_z = (cin[2 * m + cx] for m in range(5))
        t_y, a_y, b_y = (cedge[4 + 2 * m + cx] for m in range(3))
        under_t, under_b = (
            jnp.where(place == 0, jnp.broadcast_to(inner(-2, 34 + 2 * m + cx, 1), (8, LANES)), pltpu.roll(value, 1, 0))
            for m, value in ((0, t_y), (2, b_y))
        )
        side_t, side_out = (cedge[0], cedge[1]) if cx == 0 else (cedge[2], cedge[3])
        edge_sum = m_t + side_t + t_y + under_t + t_z + last_lane(t_z, AGG)
        edge_out = (m_a if cx == 0 else m_b) + side_out + a_y + under_b + a_z + last_lane(b_z, AGG)
        out = out + side_out + jnp.where(place % 2 == 0, a_y, under_b)
        cpp, cpc, ccp, ccc = store + edge_sum, -CPL_S * out, CPL_P * store, store + DISP * edge_sum + edge_out
        inside = cpp > 0.0
        determ = jnp.where(inside, cpp * ccc - cpc * ccp, 1.0)
        scale = jnp.where(inside, OMEGA_C / determ, 0.0)
        for b, value in enumerate((
            ccc * scale, -cpc * scale, -ccp * scale, cpp * scale,
            t_y, pltpu.roll(t_y, 1, 0), t_z, last_lane(t_z, AGG), m_t,
            DISP * t_y + a_y, pltpu.roll(DISP * t_y + b_y, 1, 0), DISP * t_z + a_z, last_lane(DISP * t_z + b_z, AGG),
            DISP * m_t + (m_a if cx == 0 else m_b),
        )):
            cco[b, cx] = value
    update()
    send(0)

    def step(k, carry):
        receive(k - 1)
        fine_solve(res, 0)
        update()
        pl.when(k < ITERS - 1)(lambda: send(k))
        return carry

    lax.fori_loop(1, ITERS, step, 0)


def solution(mesh):
    n_grp, n_sub = mesh.shape["grp"], mesh.shape["sub"]

    def local(cotangent, head, materials, flags, perm_table, poro_table):
        def tile(*shape):
            return pltpu.VMEM(shape + (LANES,), jnp.float32)

        dma = pltpu.SemaphoreType.DMA
        vmem = pl.BlockSpec(memory_space=pltpu.VMEM)
        hbm = pl.BlockSpec(memory_space=pltpu.HBM)
        return pl.pallas_call(
            functools.partial(kernel, n_grp, n_sub),
            out_shape=pltpu.VMEM(cotangent.shape, jnp.float32),
            in_specs=[hbm] * 6,
            out_specs=vmem,
            scratch_shapes=[
                pltpu.VMEM(cotangent.shape, jnp.float32),
                pltpu.VMEM(head.shape, jnp.float32),
                pltpu.VMEM(materials.shape, jnp.int32),
                pltpu.VMEM(flags.shape, jnp.int32),
                pltpu.SMEM(perm_table.shape, jnp.float32),
                pltpu.SMEM(poro_table.shape, jnp.float32),
                tile(7, ROWS),
                tile(ROWS),
                tile(ROWS),
                tile(ROWS),
                tile(9, ROWS),
                tile(N_COEF, ROWS),
                tile(2, ROWS),
                tile(2, ROWS),
                tile(2, ROWS),
                tile(2, ROWS),
                tile(2, ROWS),
                tile(2, ROWS),
                tile(8, 80),
                tile(8, 80),
                tile(ROUNDS, N_PART, R_ROWS),
                tile(ROUNDS, N_PART, R_ROWS),
                tile(2, 24),
                tile(4, 24),
                tile(C_ROWS),
                tile(4, C_ROWS),
                tile(13, 8),
                tile(10, 8),
                tile(32),
                tile(N_CBLK, 2, 8),
                tile(4, 8),
                dma((N_PART + 2,)),
                dma((2, N_PART + 2)),
            ],
            compiler_params=pltpu.CompilerParams(
                collective_id=0, has_side_effects=True, vmem_limit_bytes=32 * 1024 * 1024
            ),
        )(*(pltpu.with_memory_space_constraint(x, pltpu.HBM) for x in (cotangent, head, materials, flags, perm_table, poro_table)))

    return jax.shard_map(
        local,
        mesh=mesh,
        in_specs=(
            P(None, "grp", "sub", None),
            P("grp", "sub", None),
            P("grp", "sub", None),
            P(None, "grp", "sub", None),
            P(),
            P(),
        ),
        out_specs=P(None, "grp", "sub", None),
        check_vma=False,
    )
```

```python
import functools

import jax
import jax.numpy as jnp
from jax import lax
from jax.experimental import pallas as pl
from jax.experimental.pallas import tpu as pltpu
from jax.sharding import PartitionSpec as P

CX = 8
AGG = 4
ITERS = 4
DISP = 0.2
CPL_P = 0.5
CPL_S = 0.3
OMEGA = 0.7
OMEGA_C = 0.7
THETA = 0.5

PITCH = 12
BASE = 8
ROWS = 160
LANES = 128
MESH = pl.DeviceIdType.MESH

SIDES = [(-1, 0), (1, 0), (0, -1), (0, 1), (-1, -1), (-1, 1), (1, -1), (1, 1)]
FAR = [(-1, -2), (-1, 2), (1, -2), (1, 2), (0, -2), (0, 2)]
PARTNERS = FAR + SIDES[4:] + SIDES[:4]
NEAR = [(0, -2), (0, 2), (0, -1), (0, 1)]

MAT, HEAD, F0, F1, F2, COT = 0, 1, 2, 3, 4, 5
TX, TXM, TY, TYM, TZ, TZM, SX, SXM, SY, SYM, SZ, SZM, BPP, BPC, BCP, BCC, IPP, IPC, ICP, ICC = range(20)
N_COEF = 20
N_CBLK = 14
N_INNER = 17
C_ROWS = 120
C_RAW = 40
PAD = 40
R_ROWS = 64
ROUNDS = ITERS - 1
N_PART = 14


def row(x, y):
    return BASE + (x + 2) * PITCH + y + 2


def rows(x, y, count=8):
    return pl.ds(row(x, y), count)


def column(y):
    return pl.ds(row(0, y), 8, stride=PITCH)


def setup_slots(low, along):
    one, two = (-1, -2) if low else (8, 9)
    first = [(MAT, one), (HEAD, one), (along, one)]
    others = [(field, one) for field in (F0, F1, F2) if field != along]
    return first + others + [(MAT, two), (HEAD, two)] + ([(along, two)] if low else []) + [(COT, one), (COT + 1, one)]


def field_slots(low):
    return [(f, layer) for f in (0, 1) for layer in ((-2, -1) if low else (8, 9))]


def slots_of(side, setup):
    dx, dy = side
    if dx != 0:
        return setup_slots(dx < 0, F0) if setup else field_slots(dx < 0)
    return setup_slots(dy < 0, F1) if setup else field_slots(dy < 0)


def pack(side, setup, src, dst, lead, base=0):
    dx, dy = side
    for slot, (field, layer) in enumerate(slots_of(side, setup)):
        if dy == 0:
            dst[lead + (pl.ds(base + 8 * slot, 8),)] = src[field, rows(layer % 8, 0), :]
        elif dx == 0:
            dst[lead + (pl.ds(base + 8 * slot, 8),)] = src[field, column(layer % 8), :]
        else:
            dst[lead + (pl.ds(base + 2 * slot, 2),)] = src[field, rows(layer % 8, 6 if dy < 0 else 0, 2), :]


def unpack(side, setup, src, lead, dst, valid, base=0):
    dx, dy = side

    def seen(field, value):
        return jnp.where(valid, value, -1.0) if setup and field == MAT else value

    for slot, (field, layer) in enumerate(slots_of(side, setup)):
        if dy == 0:
            dst[field, rows(layer, 0), :] = seen(field, src[lead + (pl.ds(base + 8 * slot, 8),)])
        elif dx == 0:
            dst[field, column(layer), :] = seen(field, src[lead + (pl.ds(base + 8 * slot, 8),)])
        else:
            dst[field, rows(layer, -2 if dy < 0 else 8, 2), :] = seen(field, src[lead + (pl.ds(base + 2 * slot, 2),)])


def next_lane(value, by=1):
    return pltpu.roll(value, LANES - by, 1)


def last_lane(value, by=1):
    return pltpu.roll(value, by, 1)


def lane_sum(value):
    lane = lax.broadcasted_iota(jnp.int32, value.shape, 1)
    total = value + jnp.where(lane % 2 == 0, next_lane(value), last_lane(value))
    return total + jnp.where(lane % AGG < 2, next_lane(total, 2), last_lane(total, 2))


def four_sum(value):
    total = value + pltpu.roll(value, 7, 0)
    return total + pltpu.roll(total, 6, 0)


def couple(co, field, lo, n):
    here = pl.ds(lo, n)
    out = []
    for f, first in ((0, TX), (1, SX)):
        mid = field[f, here, :]
        total = co[first, here, :] * field[f, pl.ds(lo + PITCH, n), :]
        total = total + co[first + 1, here, :] * field[f, pl.ds(lo - PITCH, n), :]
        total = total + co[first + 2, here, :] * field[f, pl.ds(lo + 1, n), :]
        total = total + co[first + 3, here, :] * field[f, pl.ds(lo - 1, n), :]
        total = total + co[first + 4, here, :] * next_lane(mid)
        total = total + co[first + 5, here, :] * last_lane(mid)
        out += [mid, total]
    return out


def kernel(
    n_grp,
    n_sub,
    cot_hbm,
    head_hbm,
    mat_hbm,
    flag_hbm,
    perm_hbm,
    poro_hbm,
    out_ref,
    cot_ref,
    head_ref,
    mat_ref,
    flag_ref,
    perm_tab,
    poro_tab,
    ext,
    perm,
    poro,
    mask,
    face,
    co,
    adj,
    inc,
    res,
    grd,
    mid,
    fin,
    ssend,
    srecv,
    rsend,
    rrecv,
    xsend,
    xrecv,
    ksend,
    krecv,
    cin,
    cedge,
    ring,
    cco,
    cres,
    zeros,
    counted,
    sent,
    came,
):
    g = lax.axis_index("grp")
    s = lax.axis_index("sub")

    def device(dx, dy):
        return {"grp": g + dx, "sub": s + dy}

    def fits(dx, dy):
        found = []
        for at, count, step in ((g, n_grp, dx), (s, n_sub, dy)):
            if step < 0:
                found.append(at >= -step)
            elif step > 0:
                found.append(at < count - step)
        return found[0] if len(found) == 1 else jnp.logical_and(*found)

    loads = [
        pltpu.make_async_copy(src, dst, sent.at[i])
        for i, (src, dst) in enumerate((
            (mat_hbm, mat_ref), (head_hbm, head_ref), (flag_hbm, flag_ref), (cot_hbm, cot_ref), (perm_hbm, perm_tab), (poro_hbm, poro_tab)
        ))
    ]
    for load in loads:
        load.start()

    barrier = pltpu.get_barrier_semaphore()
    expected = jnp.int32(0)
    for dx, dy in PARTNERS:
        there = fits(dx, dy)

        @pl.when(there)
        def _():
            pl.semaphore_signal(barrier, inc=1, device_id=device(dx, dy), device_id_type=MESH)

        expected = expected + there.astype(jnp.int32)

    def rows_of(side, setup):
        dx, dy = side
        if side in FAR:
            return 0
        if setup:
            count = len(slots_of(side, True)) * (2 if dx != 0 and dy != 0 else 8)
            return -(-count // 8) * 8
        return 8 if dx != 0 and dy != 0 else 32

    def halo_part(i, setup):
        side = SIDES[i] if setup else PARTNERS[i]
        halo = rows_of(side, setup)
        if setup:
            return pl.ds(0, halo + (24 if i >= 4 else 0))
        return pl.ds(PAD - halo, halo + (16 if side[0] == 0 else 8))

    def absent(side, dst, at):
        @pl.when(jnp.logical_not(fits(*side)))
        def _():
            pltpu.make_async_copy(zeros.at[pl.ds(0, dst.shape[0])], dst, came.at[at]).start()

    def wait_all(count, at):
        part = counted.at[pl.ds(0, count)]
        pltpu.make_async_copy(part, part, came.at[at]).wait()

    def setup_copy(i):
        dx, dy = SIDES[i]
        part = halo_part(i, True)
        at = PARTNERS.index((dx, dy))
        return pltpu.make_async_remote_copy(
            ssend.at[i, part], srecv.at[i, part], sent.at[at], came.at[0], device_id=device(-dx, -dy), device_id_type=MESH
        )

    def edge_copy(i):
        dx, dy = FAR[i]
        return pltpu.make_async_remote_copy(
            xsend.at[0 if dx < 0 else 1], xrecv.at[i], sent.at[i], came.at[1], device_id=device(-dx, -dy), device_id_type=MESH
        )

    def round_copy(i, k):
        dx, dy = PARTNERS[i]
        part = halo_part(i, False)
        return pltpu.make_async_remote_copy(
            rsend.at[k, i, part], rrecv.at[k, i, part], sent.at[i], came.at[2 - 2 * lax.rem(k, 2)], device_id=device(-dx, -dy), device_id_type=MESH
        )

    def coef_copy(j):
        dx, dy = NEAR[j]
        at = PARTNERS.index((dx, dy)) if abs(dy) == 2 else N_PART + j - 2
        return pltpu.make_async_remote_copy(
            ksend, krecv.at[j], sent.at[at], came.at[1], device_id=device(-dx, -dy), device_id_type=MESH
        )

    def when_sent(side, act):
        pl.when(fits(-side[0], -side[1]))(act)

    zero_rows = jnp.zeros((ROWS, LANES), jnp.float32)
    ext[MAT] = zero_rows - 1.0
    for f in range(1, 7):
        ext[f] = zero_rows
    for load in loads:
        load.wait()
    for x in range(8):
        ext[MAT, rows(x, 0), :] = mat_ref[x].astype(jnp.float32)
        ext[HEAD, rows(x, 0), :] = head_ref[x]
        for d in range(3):
            ext[F0 + d, rows(x, 0), :] = flag_ref[d, x].astype(jnp.float32)
        for f in range(2):
            ext[COT + f, rows(x, 0), :] = cot_ref[f, x]
    for i, x in enumerate((7, 0)):
        for m, field in enumerate((MAT, HEAD, F0)):
            xsend[i, pl.ds(8 * m, 8), :] = ext[field, rows(x, 0), :]
    for i, side in enumerate(SIDES):
        pack(side, True, ext, ssend, (i,))
        if i >= 4:
            ssend[i, pl.ds(24, 24), :] = xsend[0 if side[0] < 0 else 1]

    pl.semaphore_wait(barrier, expected)
    for i in reversed(range(8)):
        when_sent(SIDES[i], lambda: setup_copy(i).start())
    for i in range(4):
        when_sent(FAR[i], lambda: edge_copy(i).start())

    zeros[...] = jnp.zeros((C_ROWS, LANES), jnp.float32)
    for i, side in enumerate(SIDES):
        absent(side, srecv.at[i, halo_part(i, True)], 0)
    for i, side in enumerate(FAR[:4]):
        absent(side, xrecv.at[i], 1)
    for j, side in enumerate(NEAR):
        absent(side, krecv.at[j], 1)
    mask[...] = zero_rows
    perm[...] = zero_rows
    poro[...] = zero_rows
    for f in range(2):
        adj[f] = zero_rows
        inc[f] = zero_rows
        grd[f] = zero_rows
        mid[f] = zero_rows
    for m in range(9):
        face[m, pl.ds(0, 32), :] = jnp.zeros((32, LANES), jnp.float32)
    for x in range(-1, 9):
        mask[rows(x, -1, 10), :] = jnp.ones((10, LANES), jnp.float32)

    def look_up(mats):
        perm_here = jnp.zeros_like(mats)
        poro_here = jnp.zeros_like(mats)
        for level in range(perm_tab.shape[0]):
            same = mats == float(level)
            perm_here = jnp.where(same, perm_tab[level], perm_here)
            poro_here = jnp.where(same, poro_tab[level], poro_here)
        return perm_here, poro_here

    def one_face(perm_here, head_here, perm_next, head_next, upwind):
        both = perm_here + perm_next
        trans = 2.0 * perm_here * perm_next / jnp.where(both > 0.0, both, 1.0)
        flux = trans * (0.5 + jnp.abs(head_here - head_next))
        return trans, upwind * flux, (1.0 - upwind) * flux

    def look_up_rows(first, end, n):
        for lo in range(first, end, n):
            here = pl.ds(lo, n)
            perm[here, :], poro[here, :] = look_up(ext[MAT, here, :])

    def face_rows(first, end, n):
        for lo in range(first, end, n):
            here = pl.ds(lo, n)
            perm_here, head_here = perm[here, :], ext[HEAD, here, :]
            lane = lax.broadcasted_iota(jnp.int32, (n, LANES), 1)
            for d in range(3):
                if d < 2:
                    there = pl.ds(lo + (PITCH, 1)[d], n)
                    perm_next, head_next = perm[there, :], ext[HEAD, there, :]
                else:
                    perm_next = jnp.where(lane == LANES - 1, 0.0, next_lane(perm_here))
                    head_next = next_lane(head_here)
                values = one_face(perm_here, head_here, perm_next, head_next, ext[F0 + d, here, :])
                for m in range(3):
                    face[3 * d + m, here, :] = values[m]

    look_up_rows(32, 128, 32)
    face_rows(32, 128, 24)

    def put(ref, at, value):
        value = four_sum(value)
        ref[pl.ds(at, 1), :] = value[0:1]
        ref[pl.ds(at + 1, 1), :] = value[4:5]

    lane = lax.broadcasted_iota(jnp.int32, (8, LANES), 1)
    for cx in range(2):
        sums = [0.0] * 7
        for x in range(4 * cx, 4 * cx + 4):
            here = rows(x, 0)
            zs = [face[6 + m, here, :] for m in range(3)]
            out = face[1, here, :] + face[4, here, :] + zs[1]
            out = out + face[2, rows(x - 1, 0), :] + face[5, rows(x, -1), :] + last_lane(zs[2])
            news = [poro[here, :], out] + zs + [ext[COT + f, here, :] for f in range(2)]
            sums = [old + new for old, new in zip(sums, news)]
        for m in range(2, 5):
            sums[m] = jnp.where(lane % AGG == AGG - 1, sums[m], 0.0)
        for item, value in zip((0, 2, 4, 6, 8, 13, 15), sums):
            put(ksend, 2 * (item + cx), value)
    for m in range(3):
        put(ksend, 2 * (10 + m), face[m, rows(3, 0), :])
        put(ksend, 2 * (17 + m), face[3 + m, column(3), :])
    ksend[pl.ds(0, C_RAW), :] = lane_sum(ksend[pl.ds(0, C_RAW), :])
    raw = [
        (MAT, rows(0, 0)), (HEAD, rows(0, 0)), (MAT, rows(7, 0)), (HEAD, rows(7, 0)), (F0, rows(7, 0)),
        (MAT, column(0)), (HEAD, column(0)), (MAT, column(7)), (HEAD, column(7)), (F1, column(7)),
    ]
    for slot, (field, where) in enumerate(raw):
        ksend[pl.ds(C_RAW + 8 * slot, 8), :] = ext[field, where, :]
    for j in range(4):
        when_sent(NEAR[j], lambda: coef_copy(j).start())

    wait_all(sum(halo_part(i, True).size for i in range(8)), 0)
    for i, side in enumerate(SIDES):
        unpack(side, True, srecv, (i,), ext, fits(*side))
    look_up_rows(0, ROWS, 32)
    face_rows(0, 144, 24)
    for lo in range(16, 144, 16):
        here = pl.ds(lo, 16)
        total = jnp.zeros((16, LANES), jnp.float32)
        out = total
        for d in range(3):
            trans, upper, lower = (face[3 * d + m, here, :] for m in range(3))
            if d < 2:
                back = pl.ds(lo - (PITCH, 1)[d], 16)
                trans_m, lower_m = face[3 * d, back, :], face[3 * d + 2, back, :]
            else:
                trans_m, lower_m = last_lane(trans), last_lane(lower)
            co[TX + 2 * d, here, :] = trans
            co[TX + 2 * d + 1, here, :] = trans_m
            co[SX + 2 * d, here, :] = DISP * trans + upper
            co[SX + 2 * d + 1, here, :] = DISP * trans_m + lower_m
            total = total + trans + trans_m
            out = out + upper + lower_m
        store = poro[here, :]
        bpp, bpc, bcp, bcc = store + total, -CPL_S * out, CPL_P * store, store + DISP * total + out
        inside = jnp.logical_and(store > 0.0, mask[here, :] > 0.0)
        determ = jnp.where(inside, bpp * bcc - bpc * bcp, 1.0)
        scale = jnp.where(inside, OMEGA / determ, 0.0)
        for at, value in (
            (BPP, bpp), (BPC, bpc), (BCP, bcp), (BCC, bcc),
            (IPP, bcc * scale), (IPC, -bpc * scale), (ICP, -bcp * scale), (ICC, bpp * scale),
        ):
            co[at, here, :] = value

    def fine_solve(src, at):
        for lo in range(16, 144, 32):
            here = pl.ds(lo, 32)
            r_p, r_c = src[at, here, :], src[at + 1, here, :]
            grd[0, here, :] = co[IPP, here, :] * r_p + co[IPC, here, :] * r_c
            grd[1, here, :] = co[ICP, here, :] * r_p + co[ICC, here, :] * r_c
        for lo in range(16, 144, 16):
            here = pl.ds(lo, 16)
            z_p, s_p, z_c, s_c = couple(co, grd, lo, 16)
            mid[0, here, :] = (2.0 - OMEGA) * z_p + co[IPP, here, :] * s_p + co[IPC, here, :] * s_c
            mid[1, here, :] = (2.0 - OMEGA) * z_c + co[ICP, here, :] * s_p + co[ICC, here, :] * s_c
        for lo in range(32, 128, 16):
            here = pl.ds(lo, 16)
            z_p, s_p, z_c, s_c = couple(co, mid, lo, 16)
            fin[0, here, :] = (1.0 - OMEGA) * z_p + grd[0, here, :] + co[IPP, here, :] * s_p + co[IPC, here, :] * s_c
            fin[1, here, :] = (1.0 - OMEGA) * z_c + grd[1, here, :] + co[ICP, here, :] * s_p + co[ICC, here, :] * s_c

    def coarse_solve():
        inv = [[cco[b, cx] for cx in range(2)] for b in range(4)]
        r = [[cres[2 * f + cx] for cx in range(2)] for f in range(2)]

        def inverse(v):
            return [[inv[2 * f][cx] * v[0][cx] + inv[2 * f + 1][cx] * v[1][cx] for cx in range(2)] for f in range(2)]

        base = inverse(r)
        z = base
        for sweep in range(3):
            acc = [[None] * 2 for f in range(2)]
            for f in range(2):
                for cx in range(2):
                    v = z[f][cx]
                    first = 4 + 5 * f
                    along = cco[first, cx] * pltpu.roll(v, 7, 0) + cco[first + 1, cx] * pltpu.roll(v, 1, 0)
                    down = cco[first + 2, cx] * next_lane(v, AGG) + cco[first + 3, cx] * last_lane(v, AGG)
                    acc[f][cx] = cco[first + 4, cx] * z[f][1 - cx] + (along + down)
            more = inverse(acc)
            z = [[((1.0 - OMEGA_C) * z[f][cx] + base[f][cx]) + more[f][cx] for cx in range(2)] for f in range(2)]
        upper = lax.broadcasted_iota(jnp.int32, (8, LANES), 0) < AGG
        return [
            [
                jnp.where(upper, jnp.broadcast_to(v[3:4], (8, LANES)), jnp.broadcast_to(v[4:5], (8, LANES)))
                for v in z[f]
            ]
            for f in range(2)
        ]

    def update():
        grown = coarse_solve()
        for f in range(2):
            for x in range(8):
                here = rows(x, 0)
                more = THETA * (fin[f, here, :] + grown[f][x // 4])
                new = adj[f, here, :] + more
                inc[f, here, :] = more
                adj[f, here, :] = new
                out_ref[f, x] = new

    def send(k):
        for lo in range(16, 144, 16):
            here = pl.ds(lo, 16)
            z_p, s_p, z_c, s_c = couple(co, inc, lo, 16)
            res[0, here, :] = co[BPP, here, :] * z_p + co[BPC, here, :] * z_c - s_p
            res[1, here, :] = co[BCP, here, :] * z_p + co[BCC, here, :] * z_c - s_c

        def place(at, value):
            ring[pl.ds(8 + at, 1), :] = value

        for f in range(2):
            for cx in range(2):
                total = res[f, rows(4 * cx, 0), :]
                for x in range(4 * cx + 1, 4 * cx + 4):
                    total = total + res[f, rows(x, 0), :]
                total = four_sum(total)
                place(8 * f + 4 * cx + 1, total[0:1])
                place(8 * f + 4 * cx + 2, total[4:5])
            for at, y in ((0, -1), (3, 8)):
                total = four_sum(res[f, column(y), :])
                place(8 * f + at, total[0:1])
                place(8 * f + 4 + at, total[4:5])
            for at, x in ((16, -1), (20, 8)):
                total = four_sum(res[f, rows(x, 0), :])
                place(at + 2 * f, total[0:1])
                place(at + 2 * f + 1, total[4:5])
        sums = lane_sum(ring[pl.ds(8, 24), :])
        ring[pl.ds(8, 24), :] = sums
        along, beside = sums[0:16], sums[16:24]
        for i, side in enumerate(PARTNERS):
            if side not in FAR:
                pack(side, False, adj, rsend, (k, i), PAD - rows_of(side, False))
            if side[0] == 0:
                rsend[k, i, pl.ds(PAD, 16), :] = along
            else:
                rsend[k, i, pl.ds(PAD, 8), :] = beside
            when_sent(side, lambda: round_copy(i, k).start())
        for i, side in enumerate(PARTNERS):
            absent(side, rrecv.at[k, i, halo_part(i, False)], 2 - 2 * lax.rem(k, 2))

    def receive(k):
        for i, side in enumerate(PARTNERS):
            when_sent(side, lambda: round_copy(i, k).wait_send())
        wait_all(sum(halo_part(i, False).size for i in range(N_PART)), 2 - 2 * lax.rem(k, 2))
        for i, side in enumerate(PARTNERS):
            if side not in FAR:
                unpack(side, False, rrecv, (k, i), adj, None, PAD - rows_of(side, False))
        at_row = lax.broadcasted_iota(jnp.int32, (8, LANES), 0)
        for f in range(2):
            for cx in range(2):
                item = 2 * f + cx

                def along(dy, shift):
                    return rrecv[k, PARTNERS.index((0, dy)), pl.ds(PAD + 4 * item + shift, 8), :]

                def beside(dy):
                    dx = 2 * cx - 1
                    at = PAD + (4 if dx < 0 else 0) + 2 * f
                    return rrecv[k, PARTNERS.index((dx, dy)), pl.ds(at - 2 * dy - 3, 8), :]

                one = jnp.where(at_row < 4, along(-1, 0), along(1, -4))
                two = jnp.where(at_row < 2, along(-2, 2), jnp.where(at_row < 6, ring[pl.ds(8 + 4 * item - 2, 8), :], along(2, -6)))
                three = jnp.where(at_row < 1, beside(-2), jnp.where(at_row < 3, beside(-1), beside(0)))
                three = jnp.where(at_row < 5, three, jnp.where(at_row < 7, beside(1), beside(2)))
                cres[item] = cres[item] - ((one + two) + three)
        for lo in range(16, 144, 16):
            here = pl.ds(lo, 16)
            z_p, s_p, z_c, s_c = couple(co, adj, lo, 16)
            res[0, here, :] = ext[COT, here, :] + s_p - co[BPP, here, :] * z_p - co[BPC, here, :] * z_c
            res[1, here, :] = ext[COT + 1, here, :] + s_c - co[BCP, here, :] * z_p - co[BCC, here, :] * z_c

    fine_solve(ext, COT)

    for i, side in enumerate(SIDES):
        when_sent(side, lambda: setup_copy(i).wait_send())
    for j, side in enumerate(NEAR):
        when_sent(side, lambda: coef_copy(j).wait_send())
        when_sent(FAR[j], lambda: edge_copy(j).wait_send())
    wait_all(4 * C_ROWS + 4 * 24, 1)

    def near(u):
        return NEAR.index((0, u))

    def inner(u, at, count):
        return (ksend[pl.ds(at, count), :] if u == 0 else krecv[near(u), pl.ds(at, count), :])

    def raw_of(u, slot):
        value = inner(u, C_RAW + 8 * slot, 8)
        return jnp.where(fits(0, u), value, -1.0) if u != 0 and slot in (0, 2, 5, 7) else value

    def beyond(dx, u, m):
        if u == 0:
            return ext[(MAT, HEAD, F0)[m], rows(-1 if dx < 0 else 8, 0), :]
        if abs(u) == 1:
            value = srecv[SIDES.index((dx, u)), pl.ds(24 + 8 * m, 8), :]
        else:
            value = xrecv[FAR.index((dx, u)), pl.ds(8 * m, 8), :]
        return jnp.where(fits(dx, u), value, -1.0) if m == 0 else value

    def between(mat_a, head_a, flag, mat_b, head_b):
        return one_face(look_up(mat_a)[0], head_a, look_up(mat_b)[0], head_b, flag)

    def put_rows(tile, u, value):
        value = four_sum(value)
        if u > -2:
            cedge[tile, pl.ds(2 * u + 3, 1), :] = value[0:1]
        if u < 2:
            cedge[tile, pl.ds(2 * u + 4, 1), :] = value[4:5]

    for tile in range(4, 10):
        cedge[tile] = jnp.zeros((8, LANES), jnp.float32)
    for u in range(-2, 3):
        trans, _, lower = between(*(beyond(-1, u, m) for m in range(3)), raw_of(u, 0), raw_of(u, 1))
        put_rows(0, u, trans)
        put_rows(1, u, lower)
        trans, upper, _ = between(raw_of(u, 2), raw_of(u, 3), raw_of(u, 4), beyond(1, u, 0), beyond(1, u, 1))
        put_rows(2, u, trans)
        put_rows(3, u, upper)
        if u < 2:
            values = between(raw_of(u, 7), raw_of(u, 8), raw_of(u, 9), raw_of(u + 1, 5), raw_of(u + 1, 6))
            for m in range(3):
                value = four_sum(values[m])
                for cx in range(2):
                    cedge[4 + 2 * m + cx, pl.ds(2 * u + 4, 1), :] = value[4 * cx : 4 * cx + 1]
    for tile in range(10):
        cedge[tile] = lane_sum(cedge[tile])
    for m in range(3):
        for cx in range(2):
            for u in range(-1, 3):
                cedge[4 + 2 * m + cx, pl.ds(2 * u + 3, 1), :] = inner(u, 34 + 2 * m + cx, 1)
    for item in range(N_INNER):

        def put_inner(where, value):
            if item < 13:
                cin[item, where, :] = value
            else:
                cres[item - 13, where, :] = value

        put_inner(pl.ds(0, 1), inner(-2, 2 * item + 1, 1))
        put_inner(pl.ds(1, 2), inner(-1, 2 * item, 2))
        put_inner(pl.ds(3, 2), inner(0, 2 * item, 2))
        put_inner(pl.ds(5, 2), inner(1, 2 * item, 2))
        put_inner(pl.ds(7, 1), inner(2, 2 * item, 1))

    place = lax.broadcasted_iota(jnp.int32, (8, LANES), 0)
    m_t, m_a, m_b = (cin[10 + m] for m in range(3))
    for cx in range(2):
        store, out, t_z, a_z, b_z = (cin[2 * m + cx] for m in range(5))
        t_y, a_y, b_y = (cedge[4 + 2 * m + cx] for m in range(3))
        under_t, under_b = (
            jnp.where(place == 0, jnp.broadcast_to(inner(-2, 34 + 2 * m + cx, 1), (8, LANES)), pltpu.roll(value, 1, 0))
            for m, value in ((0, t_y), (2, b_y))
        )
        side_t, side_out = (cedge[0], cedge[1]) if cx == 0 else (cedge[2], cedge[3])
        edge_sum = m_t + side_t + t_y + under_t + t_z + last_lane(t_z, AGG)
        edge_out = (m_a if cx == 0 else m_b) + side_out + a_y + under_b + a_z + last_lane(b_z, AGG)
        out = out + side_out + jnp.where(place % 2 == 0, a_y, under_b)
        cpp, cpc, ccp, ccc = store + edge_sum, -CPL_S * out, CPL_P * store, store + DISP * edge_sum + edge_out
        inside = cpp > 0.0
        determ = jnp.where(inside, cpp * ccc - cpc * ccp, 1.0)
        scale = jnp.where(inside, OMEGA_C / determ, 0.0)
        for b, value in enumerate((
            ccc * scale, -cpc * scale, -ccp * scale, cpp * scale,
            t_y, pltpu.roll(t_y, 1, 0), t_z, last_lane(t_z, AGG), m_t,
            DISP * t_y + a_y, pltpu.roll(DISP * t_y + b_y, 1, 0), DISP * t_z + a_z, last_lane(DISP * t_z + b_z, AGG),
            DISP * m_t + (m_a if cx == 0 else m_b),
        )):
            cco[b, cx] = value
    update()
    send(0)

    def step(k, carry):
        receive(k - 1)
        fine_solve(res, 0)
        update()
        pl.when(k < ITERS - 1)(lambda: send(k))
        return carry

    lax.fori_loop(1, ITERS, step, 0)


def solution(mesh):
    n_grp, n_sub = mesh.shape["grp"], mesh.shape["sub"]

    def local(cotangent, head, materials, flags, perm_table, poro_table):
        def tile(*shape):
            return pltpu.VMEM(shape + (LANES,), jnp.float32)

        dma = pltpu.SemaphoreType.DMA
        vmem = pl.BlockSpec(memory_space=pltpu.VMEM)
        hbm = pl.BlockSpec(memory_space=pltpu.HBM)
        return pl.pallas_call(
            functools.partial(kernel, n_grp, n_sub),
            out_shape=pltpu.VMEM(cotangent.shape, jnp.float32),
            in_specs=[hbm] * 6,
            out_specs=vmem,
            scratch_shapes=[
                pltpu.VMEM(cotangent.shape, jnp.float32),
                pltpu.VMEM(head.shape, jnp.float32),
                pltpu.VMEM(materials.shape, jnp.int32),
                pltpu.VMEM(flags.shape, jnp.int32),
                pltpu.SMEM(perm_table.shape, jnp.float32),
                pltpu.SMEM(poro_table.shape, jnp.float32),
                tile(7, ROWS),
                tile(ROWS),
                tile(ROWS),
                tile(ROWS),
                tile(9, ROWS),
                tile(N_COEF, ROWS),
                tile(2, ROWS),
                tile(2, ROWS),
                tile(2, ROWS),
                tile(2, ROWS),
                tile(2, ROWS),
                tile(2, ROWS),
                tile(8, 80),
                tile(8, 80),
                tile(ROUNDS, N_PART, R_ROWS),
                tile(ROUNDS, N_PART, R_ROWS),
                tile(2, 24),
                tile(4, 24),
                tile(C_ROWS),
                tile(4, C_ROWS),
                tile(13, 8),
                tile(10, 8),
                tile(32),
                tile(N_CBLK, 2, 8),
                tile(4, 8),
                tile(C_ROWS),
                tile(4 * C_ROWS + 4 * 24),
                dma((N_PART + 2,)),
                dma((3,)),
            ],
            compiler_params=pltpu.CompilerParams(
                collective_id=0, has_side_effects=True, vmem_limit_bytes=32 * 1024 * 1024
            ),
        )(*(pltpu.with_memory_space_constraint(x, pltpu.HBM) for x in (cotangent, head, materials, flags, perm_table, poro_table)))

    return jax.shard_map(
        local,
        mesh=mesh,
        in_specs=(
            P(None, "grp", "sub", None),
            P("grp", "sub", None),
            P("grp", "sub", None),
            P(None, "grp", "sub", None),
            P(),
            P(),
        ),
        out_specs=P(None, "grp", "sub", None),
        check_vma=False,
    )
```

```python
import functools

import jax
import jax.numpy as jnp
from jax import lax
from jax.experimental import pallas as pl
from jax.experimental.pallas import tpu as pltpu
from jax.sharding import PartitionSpec as P

CX = 8
AGG = 4
ITERS = 4
DISP = 0.2
CPL_P = 0.5
CPL_S = 0.3
OMEGA = 0.7
OMEGA_C = 0.7
THETA = 0.5

PITCH = 12
BASE = 8
ROWS = 160
LANES = 128
MESH = pl.DeviceIdType.MESH

SIDES = [(-1, 0), (1, 0), (0, -1), (0, 1), (-1, -1), (-1, 1), (1, -1), (1, 1)]
FAR = [(-1, -2), (-1, 2), (1, -2), (1, 2), (0, -2), (0, 2)]
PARTNERS = FAR + SIDES[4:] + SIDES[:4]
NEAR = [(0, -2), (0, 2), (0, -1), (0, 1)]

MAT, HEAD, F0, F1, F2, COT = 0, 1, 2, 3, 4, 5
TX, TXM, TY, TYM, TZ, TZM, SX, SXM, SY, SYM, SZ, SZM, BPP, BPC, BCP, BCC, IPP, IPC, ICP, ICC = range(20)
N_COEF = 20
N_CBLK = 14
N_INNER = 17
C_ROWS = 120
C_RAW = 40
PAD = 40
R_ROWS = 64
ROUNDS = ITERS - 1
N_PART = 14


def row(x, y):
    return BASE + (x + 2) * PITCH + y + 2


def rows(x, y, count=8):
    return pl.ds(row(x, y), count)


def column(y):
    return pl.ds(row(0, y), 8, stride=PITCH)


def setup_slots(low, along):
    one, two = (-1, -2) if low else (8, 9)
    first = [(MAT, one), (HEAD, one), (along, one)]
    others = [(field, one) for field in (F0, F1, F2) if field != along]
    return first + others + [(MAT, two), (HEAD, two)] + ([(along, two)] if low else []) + [(COT, one), (COT + 1, one)]


def field_slots(low):
    return [(f, layer) for f in (0, 1) for layer in ((-2, -1) if low else (8, 9))]


def slots_of(side, setup):
    dx, dy = side
    if dx != 0:
        return setup_slots(dx < 0, F0) if setup else field_slots(dx < 0)
    return setup_slots(dy < 0, F1) if setup else field_slots(dy < 0)


def pack(side, setup, src, dst, lead, base=0):
    dx, dy = side
    for slot, (field, layer) in enumerate(slots_of(side, setup)):
        if dy == 0:
            dst[lead + (pl.ds(base + 8 * slot, 8),)] = src[field, rows(layer % 8, 0), :]
        elif dx == 0:
            dst[lead + (pl.ds(base + 8 * slot, 8),)] = src[field, column(layer % 8), :]
        else:
            dst[lead + (pl.ds(base + 2 * slot, 2),)] = src[field, rows(layer % 8, 6 if dy < 0 else 0, 2), :]


def unpack(side, setup, src, lead, dst, valid, base=0):
    dx, dy = side

    def seen(field, value):
        return jnp.where(valid, value, -1.0) if setup and field == MAT else value

    for slot, (field, layer) in enumerate(slots_of(side, setup)):
        if dy == 0:
            dst[field, rows(layer, 0), :] = seen(field, src[lead + (pl.ds(base + 8 * slot, 8),)])
        elif dx == 0:
            dst[field, column(layer), :] = seen(field, src[lead + (pl.ds(base + 8 * slot, 8),)])
        else:
            dst[field, rows(layer, -2 if dy < 0 else 8, 2), :] = seen(field, src[lead + (pl.ds(base + 2 * slot, 2),)])


def next_lane(value, by=1):
    return pltpu.roll(value, LANES - by, 1)


def last_lane(value, by=1):
    return pltpu.roll(value, by, 1)


def lane_sum(value):
    lane = lax.broadcasted_iota(jnp.int32, value.shape, 1)
    total = value + jnp.where(lane % 2 == 0, next_lane(value), last_lane(value))
    return total + jnp.where(lane % AGG < 2, next_lane(total, 2), last_lane(total, 2))


def four_sum(value):
    total = value + pltpu.roll(value, 7, 0)
    return total + pltpu.roll(total, 6, 0)


def couple(co, field, lo, n):
    here = pl.ds(lo, n)
    out = []
    for f, first in ((0, TX), (1, SX)):
        mid = field[f, here, :]
        one = co[first, here, :] * field[f, pl.ds(lo + PITCH, n), :] + co[first + 1, here, :] * field[f, pl.ds(lo - PITCH, n), :]
        two = co[first + 2, here, :] * field[f, pl.ds(lo + 1, n), :] + co[first + 3, here, :] * field[f, pl.ds(lo - 1, n), :]
        three = co[first + 4, here, :] * next_lane(mid) + co[first + 5, here, :] * last_lane(mid)
        out += [mid, (one + two) + three]
    return out


def kernel(
    n_grp,
    n_sub,
    cot_hbm,
    head_hbm,
    mat_hbm,
    flag_hbm,
    perm_hbm,
    poro_hbm,
    out_ref,
    cot_ref,
    head_ref,
    mat_ref,
    flag_ref,
    perm_tab,
    poro_tab,
    ext,
    perm,
    poro,
    mask,
    face,
    co,
    adj,
    inc,
    res,
    grd,
    mid,
    fin,
    ssend,
    srecv,
    rsend,
    rrecv,
    xsend,
    xrecv,
    ksend,
    krecv,
    cin,
    cedge,
    ring,
    cco,
    cres,
    wt,
    wx,
    zeros,
    counted,
    sent,
    came,
):
    g = lax.axis_index("grp")
    s = lax.axis_index("sub")

    def device(dx, dy):
        return {"grp": g + dx, "sub": s + dy}

    def fits(dx, dy):
        found = []
        for at, count, step in ((g, n_grp, dx), (s, n_sub, dy)):
            if step < 0:
                found.append(at >= -step)
            elif step > 0:
                found.append(at < count - step)
        return found[0] if len(found) == 1 else jnp.logical_and(*found)

    loads = [
        pltpu.make_async_copy(src, dst, sent.at[i])
        for i, (src, dst) in enumerate((
            (mat_hbm, mat_ref), (head_hbm, head_ref), (flag_hbm, flag_ref), (cot_hbm, cot_ref), (perm_hbm, perm_tab), (poro_hbm, poro_tab)
        ))
    ]
    for load in loads:
        load.start()

    barrier = pltpu.get_barrier_semaphore()
    expected = jnp.int32(0)
    for dx, dy in PARTNERS:
        there = fits(dx, dy)

        @pl.when(there)
        def _():
            pl.semaphore_signal(barrier, inc=1, device_id=device(dx, dy), device_id_type=MESH)

        expected = expected + there.astype(jnp.int32)

    def rows_of(side, setup):
        dx, dy = side
        if side in FAR:
            return 0
        if setup:
            count = len(slots_of(side, True)) * (2 if dx != 0 and dy != 0 else 8)
            return -(-count // 8) * 8
        return 8 if dx != 0 and dy != 0 else 32

    def halo_part(i, setup):
        side = SIDES[i] if setup else PARTNERS[i]
        halo = rows_of(side, setup)
        if setup:
            return pl.ds(0, halo + (24 if i >= 4 else 0))
        return pl.ds(PAD - halo, halo + (16 if side[0] == 0 else 8))

    def absent(side, dst, at):
        @pl.when(jnp.logical_not(fits(*side)))
        def _():
            pltpu.make_async_copy(zeros.at[pl.ds(0, dst.shape[0])], dst, came.at[at]).start()

    def wait_all(count, at):
        part = counted.at[pl.ds(0, count)]
        pltpu.make_async_copy(part, part, came.at[at]).wait()

    def setup_copy(i):
        dx, dy = SIDES[i]
        part = halo_part(i, True)
        at = PARTNERS.index((dx, dy))
        return pltpu.make_async_remote_copy(
            ssend.at[i, part], srecv.at[i, part], sent.at[at], came.at[0], device_id=device(-dx, -dy), device_id_type=MESH
        )

    def edge_copy(i):
        dx, dy = FAR[i]
        return pltpu.make_async_remote_copy(
            xsend.at[0 if dx < 0 else 1], xrecv.at[i], sent.at[i], came.at[1], device_id=device(-dx, -dy), device_id_type=MESH
        )

    def round_copy(i, k):
        dx, dy = PARTNERS[i]
        part = halo_part(i, False)
        return pltpu.make_async_remote_copy(
            rsend.at[k, i, part], rrecv.at[k, i, part], sent.at[i], came.at[2 - 2 * lax.rem(k, 2)], device_id=device(-dx, -dy), device_id_type=MESH
        )

    def coef_copy(j):
        dx, dy = NEAR[j]
        at = PARTNERS.index((dx, dy)) if abs(dy) == 2 else N_PART + j - 2
        return pltpu.make_async_remote_copy(
            ksend, krecv.at[j], sent.at[at], came.at[1], device_id=device(-dx, -dy), device_id_type=MESH
        )

    def when_sent(side, act):
        pl.when(fits(-side[0], -side[1]))(act)

    zero_rows = jnp.zeros((ROWS, LANES), jnp.float32)
    ext[MAT] = zero_rows - 1.0
    for f in range(1, 7):
        ext[f] = zero_rows
    perm[...] = zero_rows
    poro[...] = zero_rows
    for m in range(9):
        face[m, pl.ds(0, 32), :] = jnp.zeros((32, LANES), jnp.float32)
    for load in loads:
        load.wait()
    for x in range(8):
        ext[MAT, rows(x, 0), :] = mat_ref[x].astype(jnp.float32)
        ext[HEAD, rows(x, 0), :] = head_ref[x]
        for d in range(3):
            ext[F0 + d, rows(x, 0), :] = flag_ref[d, x].astype(jnp.float32)
        for f in range(2):
            ext[COT + f, rows(x, 0), :] = cot_ref[f, x]
    for i, x in enumerate((7, 0)):
        for m, field in enumerate((MAT, HEAD, F0)):
            xsend[i, pl.ds(8 * m, 8), :] = ext[field, rows(x, 0), :]
    for i, side in enumerate(SIDES):
        pack(side, True, ext, ssend, (i,))
        if i >= 4:
            ssend[i, pl.ds(24, 24), :] = xsend[0 if side[0] < 0 else 1]

    def look_up(mats):
        perm_here = jnp.zeros_like(mats)
        poro_here = jnp.zeros_like(mats)
        for level in range(perm_tab.shape[0]):
            same = mats == float(level)
            perm_here = jnp.where(same, perm_tab[level], perm_here)
            poro_here = jnp.where(same, poro_tab[level], poro_here)
        return perm_here, poro_here

    def one_face(perm_here, head_here, perm_next, head_next, upwind):
        both = perm_here + perm_next
        trans = 2.0 * perm_here * perm_next / jnp.where(both > 0.0, both, 1.0)
        flux = trans * (0.5 + jnp.abs(head_here - head_next))
        return trans, upwind * flux, (1.0 - upwind) * flux

    def look_up_rows(first, end, n):
        for lo in range(first, end, n):
            here = pl.ds(lo, n)
            perm[here, :], poro[here, :] = look_up(ext[MAT, here, :])

    def face_rows(first, end, n):
        for lo in range(first, end, n):
            here = pl.ds(lo, n)
            perm_here, head_here = perm[here, :], ext[HEAD, here, :]
            lane = lax.broadcasted_iota(jnp.int32, (n, LANES), 1)
            for d in range(3):
                if d < 2:
                    there = pl.ds(lo + (PITCH, 1)[d], n)
                    perm_next, head_next = perm[there, :], ext[HEAD, there, :]
                else:
                    perm_next = jnp.where(lane == LANES - 1, 0.0, next_lane(perm_here))
                    head_next = next_lane(head_here)
                values = one_face(perm_here, head_here, perm_next, head_next, ext[F0 + d, here, :])
                for m in range(3):
                    face[3 * d + m, here, :] = values[m]

    look_up_rows(32, 128, 32)
    face_rows(32, 128, 24)

    def put(ref, at, value):
        value = four_sum(value)
        ref[pl.ds(at, 1), :] = value[0:1]
        ref[pl.ds(at + 1, 1), :] = value[4:5]

    lane = lax.broadcasted_iota(jnp.int32, (8, LANES), 1)
    for cx in range(2):
        sums = [0.0] * 7
        for x in range(4 * cx, 4 * cx + 4):
            here = rows(x, 0)
            zs = [face[6 + m, here, :] for m in range(3)]
            out = face[1, here, :] + face[4, here, :] + zs[1]
            out = out + face[2, rows(x - 1, 0), :] + face[5, rows(x, -1), :] + last_lane(zs[2])
            news = [poro[here, :], out] + zs + [ext[COT + f, here, :] for f in range(2)]
            sums = [old + new for old, new in zip(sums, news)]
        for m in range(2, 5):
            sums[m] = jnp.where(lane % AGG == AGG - 1, sums[m], 0.0)
        for item, value in zip((0, 2, 4, 6, 8, 13, 15), sums):
            put(ksend, 2 * (item + cx), value)
    for m in range(3):
        put(ksend, 2 * (10 + m), face[m, rows(3, 0), :])
        put(ksend, 2 * (17 + m), face[3 + m, column(3), :])
    ksend[pl.ds(0, C_RAW), :] = lane_sum(ksend[pl.ds(0, C_RAW), :])
    raw = [
        (MAT, rows(0, 0)), (HEAD, rows(0, 0)), (MAT, rows(7, 0)), (HEAD, rows(7, 0)), (F0, rows(7, 0)),
        (MAT, column(0)), (HEAD, column(0)), (MAT, column(7)), (HEAD, column(7)), (F1, column(7)),
    ]
    for slot, (field, where) in enumerate(raw):
        ksend[pl.ds(C_RAW + 8 * slot, 8), :] = ext[field, where, :]
    pl.semaphore_wait(barrier, expected)
    for i in reversed(range(8)):
        when_sent(SIDES[i], lambda: setup_copy(i).start())
    for i in range(4):
        when_sent(FAR[i], lambda: edge_copy(i).start())

    for j in range(4):
        when_sent(NEAR[j], lambda: coef_copy(j).start())

    zeros[...] = jnp.zeros((C_ROWS, LANES), jnp.float32)
    for i, side in enumerate(SIDES):
        absent(side, srecv.at[i, halo_part(i, True)], 0)
    for i, side in enumerate(FAR[:4]):
        absent(side, xrecv.at[i], 1)
    for j, side in enumerate(NEAR):
        absent(side, krecv.at[j], 1)
    mask[...] = zero_rows
    for f in range(2):
        adj[f] = zero_rows
        grd[f] = zero_rows
        mid[f] = zero_rows
    for x in range(-1, 9):
        mask[rows(x, -1, 10), :] = jnp.ones((10, LANES), jnp.float32)


    wait_all(sum(halo_part(i, True).size for i in range(8)), 0)
    for i, side in enumerate(SIDES):
        unpack(side, True, srecv, (i,), ext, fits(*side))
    look_up_rows(0, ROWS, 32)
    face_rows(0, 144, 24)
    for lo in range(16, 144, 16):
        here = pl.ds(lo, 16)
        total = jnp.zeros((16, LANES), jnp.float32)
        out = total
        for d in range(3):
            trans, upper, lower = (face[3 * d + m, here, :] for m in range(3))
            if d < 2:
                back = pl.ds(lo - (PITCH, 1)[d], 16)
                trans_m, lower_m = face[3 * d, back, :], face[3 * d + 2, back, :]
            else:
                trans_m, lower_m = last_lane(trans), last_lane(lower)
            co[TX + 2 * d, here, :] = trans
            co[TX + 2 * d + 1, here, :] = trans_m
            co[SX + 2 * d, here, :] = DISP * trans + upper
            co[SX + 2 * d + 1, here, :] = DISP * trans_m + lower_m
            total = total + trans + trans_m
            out = out + upper + lower_m
        store = poro[here, :]
        bpp, bpc, bcp, bcc = store + total, -CPL_S * out, CPL_P * store, store + DISP * total + out
        inside = jnp.logical_and(store > 0.0, mask[here, :] > 0.0)
        determ = jnp.where(inside, bpp * bcc - bpc * bcp, 1.0)
        scale = jnp.where(inside, OMEGA / determ, 0.0)
        for at, value in (
            (BPP, bpp), (BPC, bpc), (BCP, bcp), (BCC, bcc),
            (IPP, bcc * scale), (IPC, -bpc * scale), (ICP, -bcp * scale), (ICC, bpp * scale),
        ):
            co[at, here, :] = value

    def fine_solve(src, at):
        for lo in range(16, 144, 32):
            here = pl.ds(lo, 32)
            r_p, r_c = src[at, here, :], src[at + 1, here, :]
            grd[0, here, :] = co[IPP, here, :] * r_p + co[IPC, here, :] * r_c
            grd[1, here, :] = co[ICP, here, :] * r_p + co[ICC, here, :] * r_c
        for lo in range(16, 144, 16):
            here = pl.ds(lo, 16)
            z_p, s_p, z_c, s_c = couple(co, grd, lo, 16)
            mid[0, here, :] = (2.0 - OMEGA) * z_p + co[IPP, here, :] * s_p + co[IPC, here, :] * s_c
            mid[1, here, :] = (2.0 - OMEGA) * z_c + co[ICP, here, :] * s_p + co[ICC, here, :] * s_c
        for lo in range(32, 128, 16):
            here = pl.ds(lo, 16)
            z_p, s_p, z_c, s_c = couple(co, mid, lo, 16)
            fin[0, here, :] = (1.0 - OMEGA) * z_p + grd[0, here, :] + co[IPP, here, :] * s_p + co[IPC, here, :] * s_c
            fin[1, here, :] = (1.0 - OMEGA) * z_c + grd[1, here, :] + co[ICP, here, :] * s_p + co[ICC, here, :] * s_c

    def coarse_solve():
        inv = [[cco[b, cx] for cx in range(2)] for b in range(4)]
        r = [[cres[2 * f + cx] for cx in range(2)] for f in range(2)]

        def inverse(v):
            return [[inv[2 * f][cx] * v[0][cx] + inv[2 * f + 1][cx] * v[1][cx] for cx in range(2)] for f in range(2)]

        base = inverse(r)
        z = base
        for sweep in range(3):
            acc = [[None] * 2 for f in range(2)]
            for f in range(2):
                for cx in range(2):
                    v = z[f][cx]
                    first = 4 + 5 * f
                    along = cco[first, cx] * pltpu.roll(v, 7, 0) + cco[first + 1, cx] * pltpu.roll(v, 1, 0)
                    down = cco[first + 2, cx] * next_lane(v, AGG) + cco[first + 3, cx] * last_lane(v, AGG)
                    acc[f][cx] = cco[first + 4, cx] * z[f][1 - cx] + (along + down)
            more = inverse(acc)
            z = [[((1.0 - OMEGA_C) * z[f][cx] + base[f][cx]) + more[f][cx] for cx in range(2)] for f in range(2)]
        upper = lax.broadcasted_iota(jnp.int32, (8, LANES), 0) < AGG
        return [
            [
                jnp.where(upper, jnp.broadcast_to(v[3:4], (8, LANES)), jnp.broadcast_to(v[4:5], (8, LANES)))
                for v in z[f]
            ]
            for f in range(2)
        ]

    def update():
        grown = coarse_solve()
        for f in range(2):
            for x in range(8):
                here = rows(x, 0)
                more = THETA * (fin[f, here, :] + grown[f][x // 4])
                new = adj[f, here, :] + more
                inc[f, x] = more
                adj[f, here, :] = new
                out_ref[f, x] = new

    def send(k):
        def place(at, value):
            ring[pl.ds(8 + at, 1), :] = value

        e = [[inc[f, x] for x in range(8)] for f in range(2)]
        for f in range(2):
            for cx in range(2):
                terms = [[], [], [], [], []]
                for x in range(4 * cx, 4 * cx + 4):
                    terms[0].append(wt[6 * f, x] * e[f][x] + wt[6 * f + 1, x] * e[1 - f][x])
                    for m in range(4):
                        terms[1 + m].append(wt[6 * f + 2 + m, x] * e[f][x])
                total, y_next, y_last, z_next, z_last = ((t[0] + t[1]) + (t[2] + t[3]) for t in terms)
                total = total - (last_lane(z_next) + next_lane(z_last))
                other = wx[f, 1, 0] * e[f][4] if cx == 0 else wx[f, 0, 1] * e[f][3]
                total = four_sum(total - other)
                at = 8 * f + 4 * cx
                place(at, -y_last[0:1])
                place(at + 1, total[0:1] - y_last[4:5])
                place(at + 2, total[4:5] - y_next[3:4])
                place(at + 3, -y_next[7:8])
            for at, value in ((16, wx[f, 0, 0] * e[f][0]), (20, wx[f, 1, 1] * e[f][7])):
                total = four_sum(value)
                place(at + 2 * f, -total[0:1])
                place(at + 2 * f + 1, -total[4:5])
        sums = lane_sum(ring[pl.ds(8, 24), :])
        ring[pl.ds(8, 24), :] = sums
        along, beside = sums[0:16], sums[16:24]
        for i, side in enumerate(PARTNERS):
            if side not in FAR:
                pack(side, False, adj, rsend, (k, i), PAD - rows_of(side, False))
            if side[0] == 0:
                rsend[k, i, pl.ds(PAD, 16), :] = along
            else:
                rsend[k, i, pl.ds(PAD, 8), :] = beside
            when_sent(side, lambda: round_copy(i, k).start())
        for i, side in enumerate(PARTNERS):
            absent(side, rrecv.at[k, i, halo_part(i, False)], 2 - 2 * lax.rem(k, 2))

    def receive(k):
        for i, side in enumerate(PARTNERS):
            when_sent(side, lambda: round_copy(i, k).wait_send())
        wait_all(sum(halo_part(i, False).size for i in range(N_PART)), 2 - 2 * lax.rem(k, 2))
        for i, side in enumerate(PARTNERS):
            if side not in FAR:
                unpack(side, False, rrecv, (k, i), adj, None, PAD - rows_of(side, False))
        at_row = lax.broadcasted_iota(jnp.int32, (8, LANES), 0)
        for f in range(2):
            for cx in range(2):
                item = 2 * f + cx

                def along(dy, shift):
                    return rrecv[k, PARTNERS.index((0, dy)), pl.ds(PAD + 4 * item + shift, 8), :]

                def beside(dy):
                    dx = 2 * cx - 1
                    at = PAD + (4 if dx < 0 else 0) + 2 * f
                    return rrecv[k, PARTNERS.index((dx, dy)), pl.ds(at - 2 * dy - 3, 8), :]

                one = jnp.where(at_row < 4, along(-1, 0), along(1, -4))
                two = jnp.where(at_row < 2, along(-2, 2), jnp.where(at_row < 6, ring[pl.ds(8 + 4 * item - 2, 8), :], along(2, -6)))
                three = jnp.where(at_row < 1, beside(-2), jnp.where(at_row < 3, beside(-1), beside(0)))
                three = jnp.where(at_row < 5, three, jnp.where(at_row < 7, beside(1), beside(2)))
                cres[item] = cres[item] - ((one + two) + three)
        for lo in range(16, 144, 16):
            here = pl.ds(lo, 16)
            z_p, s_p, z_c, s_c = couple(co, adj, lo, 16)
            res[0, here, :] = ext[COT, here, :] + s_p - co[BPP, here, :] * z_p - co[BPC, here, :] * z_c
            res[1, here, :] = ext[COT + 1, here, :] + s_c - co[BCP, here, :] * z_p - co[BCC, here, :] * z_c

    fine_solve(ext, COT)

    for i, side in enumerate(SIDES):
        when_sent(side, lambda: setup_copy(i).wait_send())
    for j, side in enumerate(NEAR):
        when_sent(side, lambda: coef_copy(j).wait_send())
        when_sent(FAR[j], lambda: edge_copy(j).wait_send())
    wait_all(4 * C_ROWS + 4 * 24, 1)

    def near(u):
        return NEAR.index((0, u))

    def inner(u, at, count):
        return (ksend[pl.ds(at, count), :] if u == 0 else krecv[near(u), pl.ds(at, count), :])

    def raw_of(u, slot):
        value = inner(u, C_RAW + 8 * slot, 8)
        return jnp.where(fits(0, u), value, -1.0) if u != 0 and slot in (0, 2, 5, 7) else value

    def beyond(dx, u, m):
        if u == 0:
            return ext[(MAT, HEAD, F0)[m], rows(-1 if dx < 0 else 8, 0), :]
        if abs(u) == 1:
            value = srecv[SIDES.index((dx, u)), pl.ds(24 + 8 * m, 8), :]
        else:
            value = xrecv[FAR.index((dx, u)), pl.ds(8 * m, 8), :]
        return jnp.where(fits(dx, u), value, -1.0) if m == 0 else value

    def between(mat_a, head_a, flag, mat_b, head_b):
        return one_face(look_up(mat_a)[0], head_a, look_up(mat_b)[0], head_b, flag)

    def put_rows(tile, u, value):
        value = four_sum(value)
        if u > -2:
            cedge[tile, pl.ds(2 * u + 3, 1), :] = value[0:1]
        if u < 2:
            cedge[tile, pl.ds(2 * u + 4, 1), :] = value[4:5]

    for tile in range(4, 10):
        cedge[tile] = jnp.zeros((8, LANES), jnp.float32)
    for u in range(-2, 3):
        trans, _, lower = between(*(beyond(-1, u, m) for m in range(3)), raw_of(u, 0), raw_of(u, 1))
        put_rows(0, u, trans)
        put_rows(1, u, lower)
        trans, upper, _ = between(raw_of(u, 2), raw_of(u, 3), raw_of(u, 4), beyond(1, u, 0), beyond(1, u, 1))
        put_rows(2, u, trans)
        put_rows(3, u, upper)
        if u < 2:
            values = between(raw_of(u, 7), raw_of(u, 8), raw_of(u, 9), raw_of(u + 1, 5), raw_of(u + 1, 6))
            for m in range(3):
                value = four_sum(values[m])
                for cx in range(2):
                    cedge[4 + 2 * m + cx, pl.ds(2 * u + 4, 1), :] = value[4 * cx : 4 * cx + 1]
    for tile in range(10):
        cedge[tile] = lane_sum(cedge[tile])
    for m in range(3):
        for cx in range(2):
            for u in range(-1, 3):
                cedge[4 + 2 * m + cx, pl.ds(2 * u + 3, 1), :] = inner(u, 34 + 2 * m + cx, 1)
    for item in range(N_INNER):

        def put_inner(where, value):
            if item < 13:
                cin[item, where, :] = value
            else:
                cres[item - 13, where, :] = value

        put_inner(pl.ds(0, 1), inner(-2, 2 * item + 1, 1))
        put_inner(pl.ds(1, 2), inner(-1, 2 * item, 2))
        put_inner(pl.ds(3, 2), inner(0, 2 * item, 2))
        put_inner(pl.ds(5, 2), inner(1, 2 * item, 2))
        put_inner(pl.ds(7, 1), inner(2, 2 * item, 1))

    place = lax.broadcasted_iota(jnp.int32, (8, LANES), 0)
    m_t, m_a, m_b = (cin[10 + m] for m in range(3))
    for cx in range(2):
        store, out, t_z, a_z, b_z = (cin[2 * m + cx] for m in range(5))
        t_y, a_y, b_y = (cedge[4 + 2 * m + cx] for m in range(3))
        under_t, under_b = (
            jnp.where(place == 0, jnp.broadcast_to(inner(-2, 34 + 2 * m + cx, 1), (8, LANES)), pltpu.roll(value, 1, 0))
            for m, value in ((0, t_y), (2, b_y))
        )
        side_t, side_out = (cedge[0], cedge[1]) if cx == 0 else (cedge[2], cedge[3])
        edge_sum = m_t + side_t + t_y + under_t + t_z + last_lane(t_z, AGG)
        edge_out = (m_a if cx == 0 else m_b) + side_out + a_y + under_b + a_z + last_lane(b_z, AGG)
        out = out + side_out + jnp.where(place % 2 == 0, a_y, under_b)
        cpp, cpc, ccp, ccc = store + edge_sum, -CPL_S * out, CPL_P * store, store + DISP * edge_sum + edge_out
        inside = cpp > 0.0
        determ = jnp.where(inside, cpp * ccc - cpc * ccp, 1.0)
        scale = jnp.where(inside, OMEGA_C / determ, 0.0)
        for b, value in enumerate((
            ccc * scale, -cpc * scale, -ccp * scale, cpp * scale,
            t_y, pltpu.roll(t_y, 1, 0), t_z, last_lane(t_z, AGG), m_t,
            DISP * t_y + a_y, pltpu.roll(DISP * t_y + b_y, 1, 0), DISP * t_z + a_z, last_lane(DISP * t_z + b_z, AGG),
            DISP * m_t + (m_a if cx == 0 else m_b),
        )):
            cco[b, cx] = value
    y_at = lax.broadcasted_iota(jnp.int32, (8, LANES), 0) % AGG
    z_at = lax.broadcasted_iota(jnp.int32, (8, LANES), 1) % AGG
    for x in range(8):
        here = rows(x, 0)
        to_next = [[co[TX + 2 * d, here, :] for d in range(3)], [DISP * face[3 * d, here, :] + face[3 * d + 2, here, :] for d in range(3)]]
        to_last = [
            [co[TXM + 2 * d, here, :] for d in range(3)],
            [co[SX, rows(x - 1, 0), :], co[SY, rows(x, -1), :], last_lane(co[SZ, here, :])],
        ]
        for f in range(2):
            own = co[BCC if f else BPP, here, :]
            if x % AGG != AGG - 1:
                own = own - to_next[f][0]
            if x % AGG != 0:
                own = own - to_last[f][0]
            y_next, y_last = (jnp.where(y_at == edge, v[f][1], 0.0) for edge, v in ((AGG - 1, to_next), (0, to_last)))
            z_next, z_last = (jnp.where(z_at == edge, v[f][2], 0.0) for edge, v in ((AGG - 1, to_next), (0, to_last)))
            own = own - (((to_next[f][1] - y_next) + (to_last[f][1] - y_last)) + ((to_next[f][2] - z_next) + (to_last[f][2] - z_last)))
            for m, value in enumerate((own, co[BCP if f else BPC, here, :], y_next, y_last, z_next, z_last)):
                wt[6 * f + m, x] = value
            if x % AGG == 0:
                wx[f, x // AGG, 0] = to_last[f][0]
            if x % AGG == AGG - 1:
                wx[f, x // AGG, 1] = to_next[f][0]

    update()
    send(0)

    def step(k, carry):
        receive(k - 1)
        fine_solve(res, 0)
        update()
        pl.when(k < ITERS - 1)(lambda: send(k))
        return carry

    lax.fori_loop(1, ITERS, step, 0)


def solution(mesh):
    n_grp, n_sub = mesh.shape["grp"], mesh.shape["sub"]

    def local(cotangent, head, materials, flags, perm_table, poro_table):
        def tile(*shape):
            return pltpu.VMEM(shape + (LANES,), jnp.float32)

        dma = pltpu.SemaphoreType.DMA
        vmem = pl.BlockSpec(memory_space=pltpu.VMEM)
        hbm = pl.BlockSpec(memory_space=pltpu.HBM)
        return pl.pallas_call(
            functools.partial(kernel, n_grp, n_sub),
            out_shape=pltpu.VMEM(cotangent.shape, jnp.float32),
            in_specs=[hbm] * 6,
            out_specs=vmem,
            scratch_shapes=[
                pltpu.VMEM(cotangent.shape, jnp.float32),
                pltpu.VMEM(head.shape, jnp.float32),
                pltpu.VMEM(materials.shape, jnp.int32),
                pltpu.VMEM(flags.shape, jnp.int32),
                pltpu.SMEM(perm_table.shape, jnp.float32),
                pltpu.SMEM(poro_table.shape, jnp.float32),
                tile(7, ROWS),
                tile(ROWS),
                tile(ROWS),
                tile(ROWS),
                tile(9, ROWS),
                tile(N_COEF, ROWS),
                tile(2, ROWS),
                tile(2, 8, 8),
                tile(2, ROWS),
                tile(2, ROWS),
                tile(2, ROWS),
                tile(2, ROWS),
                tile(8, 80),
                tile(8, 80),
                tile(ROUNDS, N_PART, R_ROWS),
                tile(ROUNDS, N_PART, R_ROWS),
                tile(2, 24),
                tile(4, 24),
                tile(C_ROWS),
                tile(4, C_ROWS),
                tile(13, 8),
                tile(10, 8),
                tile(32),
                tile(N_CBLK, 2, 8),
                tile(4, 8),
                tile(12, 8, 8),
                tile(2, 2, 2, 8),
                tile(C_ROWS),
                tile(4 * C_ROWS + 4 * 24),
                dma((N_PART + 2,)),
                dma((3,)),
            ],
            compiler_params=pltpu.CompilerParams(
                collective_id=0, has_side_effects=True, vmem_limit_bytes=32 * 1024 * 1024
            ),
        )(*(pltpu.with_memory_space_constraint(x, pltpu.HBM) for x in (cotangent, head, materials, flags, perm_table, poro_table)))

    return jax.shard_map(
        local,
        mesh=mesh,
        in_specs=(
            P(None, "grp", "sub", None),
            P("grp", "sub", None),
            P("grp", "sub", None),
            P(None, "grp", "sub", None),
            P(),
            P(),
        ),
        out_specs=P(None, "grp", "sub", None),
        check_vma=False,
    )
```

```python
import functools

import jax
import jax.numpy as jnp
from jax import lax
from jax.experimental import pallas as pl
from jax.experimental.pallas import tpu as pltpu
from jax.sharding import PartitionSpec as P

CX = 8
AGG = 4
ITERS = 4
DISP = 0.2
CPL_P = 0.5
CPL_S = 0.3
OMEGA = 0.7
OMEGA_C = 0.7
THETA = 0.5

PITCH = 12
BASE = 8
ROWS = 160
LANES = 128
MESH = pl.DeviceIdType.MESH

SIDES = [(-1, 0), (1, 0), (0, -1), (0, 1), (-1, -1), (-1, 1), (1, -1), (1, 1)]
FAR = [(-1, -2), (-1, 2), (1, -2), (1, 2), (0, -2), (0, 2)]
PARTNERS = FAR + SIDES[4:] + SIDES[:4]
NEAR = [(0, -2), (0, 2), (0, -1), (0, 1)]

MAT, HEAD, F0, F1, F2, COT = 0, 1, 2, 3, 4, 5
TX, TXM, TY, TYM, TZ, TZM, SX, SXM, SY, SYM, SZ, SZM, BPP, BPC, BCP, BCC, IPP, IPC, ICP, ICC = range(20)
N_COEF = 20
N_CBLK = 14
N_INNER = 17
C_ROWS = 120
C_RAW = 40
PAD = 40
R_ROWS = 64
ROUNDS = ITERS - 1
N_PART = 14


def row(x, y):
    return BASE + (x + 2) * PITCH + y + 2


def rows(x, y, count=8):
    return pl.ds(row(x, y), count)


def column(y):
    return pl.ds(row(0, y), 8, stride=PITCH)


def setup_slots(low, along):
    one, two = (-1, -2) if low else (8, 9)
    first = [(MAT, one), (HEAD, one), (along, one)]
    others = [(field, one) for field in (F0, F1, F2) if field != along]
    return first + others + [(MAT, two), (HEAD, two)] + ([(along, two)] if low else []) + [(COT, one), (COT + 1, one)]


def field_slots(low):
    return [(f, layer) for f in (0, 1) for layer in ((-2, -1) if low else (8, 9))]


def slots_of(side, setup):
    dx, dy = side
    if dx != 0:
        return setup_slots(dx < 0, F0) if setup else field_slots(dx < 0)
    return setup_slots(dy < 0, F1) if setup else field_slots(dy < 0)


def pack(side, setup, src, dst, lead, base=0):
    dx, dy = side
    for slot, (field, layer) in enumerate(slots_of(side, setup)):
        if dy == 0:
            dst[lead + (pl.ds(base + 8 * slot, 8),)] = src[field, rows(layer % 8, 0), :]
        elif dx == 0:
            dst[lead + (pl.ds(base + 8 * slot, 8),)] = src[field, column(layer % 8), :]
        else:
            dst[lead + (pl.ds(base + 2 * slot, 2),)] = src[field, rows(layer % 8, 6 if dy < 0 else 0, 2), :]


def unpack(side, setup, src, lead, dst, valid, base=0):
    dx, dy = side

    def seen(field, value):
        return jnp.where(valid, value, -1.0) if setup and field == MAT else value

    for slot, (field, layer) in enumerate(slots_of(side, setup)):
        if dy == 0:
            dst[field, rows(layer, 0), :] = seen(field, src[lead + (pl.ds(base + 8 * slot, 8),)])
        elif dx == 0:
            dst[field, column(layer), :] = seen(field, src[lead + (pl.ds(base + 8 * slot, 8),)])
        else:
            dst[field, rows(layer, -2 if dy < 0 else 8, 2), :] = seen(field, src[lead + (pl.ds(base + 2 * slot, 2),)])


def next_lane(value, by=1):
    return pltpu.roll(value, LANES - by, 1)


def last_lane(value, by=1):
    return pltpu.roll(value, by, 1)


def lane_sum(value):
    at = lax.broadcasted_iota(jnp.int32, value.shape, 1) % AGG
    one = jnp.where(at < 3, next_lane(value), last_lane(value, 3))
    two = jnp.where(at < 2, next_lane(value, 2), last_lane(value, 2))
    three = jnp.where(at < 1, next_lane(value, 3), last_lane(value))
    return (value + one) + (two + three)


def four_sum(value):
    return (value + pltpu.roll(value, 7, 0)) + (pltpu.roll(value, 6, 0) + pltpu.roll(value, 5, 0))


def couple(co, field, lo, n):
    here = pl.ds(lo, n)
    out = []
    for f, first in ((0, TX), (1, SX)):
        mid = field[f, here, :]
        one = co[first, here, :] * field[f, pl.ds(lo + PITCH, n), :] + co[first + 1, here, :] * field[f, pl.ds(lo - PITCH, n), :]
        two = co[first + 2, here, :] * field[f, pl.ds(lo + 1, n), :] + co[first + 3, here, :] * field[f, pl.ds(lo - 1, n), :]
        three = co[first + 4, here, :] * next_lane(mid) + co[first + 5, here, :] * last_lane(mid)
        out += [mid, (one + two) + three]
    return out


def kernel(
    n_grp,
    n_sub,
    cot_hbm,
    head_hbm,
    mat_hbm,
    flag_hbm,
    perm_hbm,
    poro_hbm,
    out_ref,
    cot_ref,
    head_ref,
    mat_ref,
    flag_ref,
    perm_tab,
    poro_tab,
    ext,
    perm,
    poro,
    mask,
    face,
    co,
    adj,
    inc,
    res,
    grd,
    mid,
    fin,
    ssend,
    srecv,
    rsend,
    rrecv,
    xsend,
    xrecv,
    ksend,
    krecv,
    cin,
    cedge,
    ring,
    cco,
    cres,
    wt,
    wx,
    zeros,
    counted,
    sent,
    came,
):
    g = lax.axis_index("grp")
    s = lax.axis_index("sub")

    def device(dx, dy):
        return {"grp": g + dx, "sub": s + dy}

    def fits(dx, dy):
        found = []
        for at, count, step in ((g, n_grp, dx), (s, n_sub, dy)):
            if step < 0:
                found.append(at >= -step)
            elif step > 0:
                found.append(at < count - step)
        return found[0] if len(found) == 1 else jnp.logical_and(*found)

    loads = [
        pltpu.make_async_copy(src, dst, sent.at[i])
        for i, (src, dst) in enumerate((
            (mat_hbm, mat_ref), (head_hbm, head_ref), (flag_hbm, flag_ref), (cot_hbm, cot_ref), (perm_hbm, perm_tab), (poro_hbm, poro_tab)
        ))
    ]
    for load in loads:
        load.start()

    barrier = pltpu.get_barrier_semaphore()
    expected = jnp.int32(0)
    for dx, dy in PARTNERS:
        there = fits(dx, dy)

        @pl.when(there)
        def _():
            pl.semaphore_signal(barrier, inc=1, device_id=device(dx, dy), device_id_type=MESH)

        expected = expected + there.astype(jnp.int32)

    def rows_of(side, setup):
        dx, dy = side
        if side in FAR:
            return 0
        if setup:
            count = len(slots_of(side, True)) * (2 if dx != 0 and dy != 0 else 8)
            return -(-count // 8) * 8
        return 8 if dx != 0 and dy != 0 else 32

    def halo_part(i, setup):
        side = SIDES[i] if setup else PARTNERS[i]
        halo = rows_of(side, setup)
        if setup:
            return pl.ds(0, halo + (24 if i >= 4 else 0))
        return pl.ds(PAD - halo, halo + (16 if side[0] == 0 else 8))

    def absent(side, dst, at):
        @pl.when(jnp.logical_not(fits(*side)))
        def _():
            pltpu.make_async_copy(zeros.at[pl.ds(0, dst.shape[0])], dst, came.at[at]).start()

    def wait_all(count, at):
        part = counted.at[pl.ds(0, count)]
        pltpu.make_async_copy(part, part, came.at[at]).wait()

    def setup_copy(i):
        dx, dy = SIDES[i]
        part = halo_part(i, True)
        at = PARTNERS.index((dx, dy))
        return pltpu.make_async_remote_copy(
            ssend.at[i, part], srecv.at[i, part], sent.at[at], came.at[0], device_id=device(-dx, -dy), device_id_type=MESH
        )

    def edge_copy(i):
        dx, dy = FAR[i]
        return pltpu.make_async_remote_copy(
            xsend.at[0 if dx < 0 else 1], xrecv.at[i], sent.at[i], came.at[1], device_id=device(-dx, -dy), device_id_type=MESH
        )

    def round_copy(i, k):
        dx, dy = PARTNERS[i]
        part = halo_part(i, False)
        return pltpu.make_async_remote_copy(
            rsend.at[k, i, part], rrecv.at[k, i, part], sent.at[i], came.at[2 - 2 * lax.rem(k, 2)], device_id=device(-dx, -dy), device_id_type=MESH
        )

    def coef_copy(j):
        dx, dy = NEAR[j]
        at = PARTNERS.index((dx, dy)) if abs(dy) == 2 else N_PART + j - 2
        return pltpu.make_async_remote_copy(
            ksend, krecv.at[j], sent.at[at], came.at[1], device_id=device(-dx, -dy), device_id_type=MESH
        )

    def when_sent(side, act):
        pl.when(fits(-side[0], -side[1]))(act)

    zero_rows = jnp.zeros((ROWS, LANES), jnp.float32)
    ext[MAT] = zero_rows - 1.0
    for f in range(1, 7):
        ext[f] = zero_rows
    perm[...] = zero_rows
    poro[...] = zero_rows
    for m in range(9):
        face[m, pl.ds(0, 32), :] = jnp.zeros((32, LANES), jnp.float32)
    for load in loads:
        load.wait()
    for x in range(8):
        ext[MAT, rows(x, 0), :] = mat_ref[x].astype(jnp.float32)
        ext[HEAD, rows(x, 0), :] = head_ref[x]
        for d in range(3):
            ext[F0 + d, rows(x, 0), :] = flag_ref[d, x].astype(jnp.float32)
        for f in range(2):
            ext[COT + f, rows(x, 0), :] = cot_ref[f, x]
    for i, x in enumerate((7, 0)):
        for m, field in enumerate((MAT, HEAD, F0)):
            xsend[i, pl.ds(8 * m, 8), :] = ext[field, rows(x, 0), :]
    for i, side in enumerate(SIDES):
        pack(side, True, ext, ssend, (i,))
        if i >= 4:
            ssend[i, pl.ds(24, 24), :] = xsend[0 if side[0] < 0 else 1]

    def look_up(mats):
        perm_here = jnp.zeros_like(mats)
        poro_here = jnp.zeros_like(mats)
        for level in range(perm_tab.shape[0]):
            same = mats == float(level)
            perm_here = jnp.where(same, perm_tab[level], perm_here)
            poro_here = jnp.where(same, poro_tab[level], poro_here)
        return perm_here, poro_here

    def one_face(perm_here, head_here, perm_next, head_next, upwind):
        both = perm_here + perm_next
        trans = 2.0 * perm_here * perm_next / jnp.where(both > 0.0, both, 1.0)
        flux = trans * (0.5 + jnp.abs(head_here - head_next))
        return trans, upwind * flux, (1.0 - upwind) * flux

    def look_up_rows(first, end, n):
        for lo in range(first, end, n):
            here = pl.ds(lo, n)
            perm[here, :], poro[here, :] = look_up(ext[MAT, here, :])

    def face_rows(first, end, n):
        for lo in range(first, end, n):
            here = pl.ds(lo, n)
            perm_here, head_here = perm[here, :], ext[HEAD, here, :]
            lane = lax.broadcasted_iota(jnp.int32, (n, LANES), 1)
            for d in range(3):
                if d < 2:
                    there = pl.ds(lo + (PITCH, 1)[d], n)
                    perm_next, head_next = perm[there, :], ext[HEAD, there, :]
                else:
                    perm_next = jnp.where(lane == LANES - 1, 0.0, next_lane(perm_here))
                    head_next = next_lane(head_here)
                values = one_face(perm_here, head_here, perm_next, head_next, ext[F0 + d, here, :])
                for m in range(3):
                    face[3 * d + m, here, :] = values[m]

    look_up_rows(32, 128, 32)
    face_rows(32, 128, 24)

    def put(ref, at, value):
        value = four_sum(value)
        ref[pl.ds(at, 1), :] = value[0:1]
        ref[pl.ds(at + 1, 1), :] = value[4:5]

    lane = lax.broadcasted_iota(jnp.int32, (8, LANES), 1)
    for cx in range(2):
        sums = [0.0] * 7
        for x in range(4 * cx, 4 * cx + 4):
            here = rows(x, 0)
            zs = [face[6 + m, here, :] for m in range(3)]
            out = face[1, here, :] + face[4, here, :] + zs[1]
            out = out + face[2, rows(x - 1, 0), :] + face[5, rows(x, -1), :] + last_lane(zs[2])
            news = [poro[here, :], out] + zs + [ext[COT + f, here, :] for f in range(2)]
            sums = [old + new for old, new in zip(sums, news)]
        for m in range(2, 5):
            sums[m] = jnp.where(lane % AGG == AGG - 1, sums[m], 0.0)
        for item, value in zip((0, 2, 4, 6, 8, 13, 15), sums):
            put(ksend, 2 * (item + cx), value)
    for m in range(3):
        put(ksend, 2 * (10 + m), face[m, rows(3, 0), :])
        put(ksend, 2 * (17 + m), face[3 + m, column(3), :])
    ksend[pl.ds(0, C_RAW), :] = lane_sum(ksend[pl.ds(0, C_RAW), :])
    raw = [
        (MAT, rows(0, 0)), (HEAD, rows(0, 0)), (MAT, rows(7, 0)), (HEAD, rows(7, 0)), (F0, rows(7, 0)),
        (MAT, column(0)), (HEAD, column(0)), (MAT, column(7)), (HEAD, column(7)), (F1, column(7)),
    ]
    for slot, (field, where) in enumerate(raw):
        ksend[pl.ds(C_RAW + 8 * slot, 8), :] = ext[field, where, :]
    pl.semaphore_wait(barrier, expected)
    for i in reversed(range(8)):
        when_sent(SIDES[i], lambda: setup_copy(i).start())
    for i in range(4):
        when_sent(FAR[i], lambda: edge_copy(i).start())

    for j in range(4):
        when_sent(NEAR[j], lambda: coef_copy(j).start())

    zeros[...] = jnp.zeros((C_ROWS, LANES), jnp.float32)
    for i, side in enumerate(SIDES):
        absent(side, srecv.at[i, halo_part(i, True)], 0)
    for i, side in enumerate(FAR[:4]):
        absent(side, xrecv.at[i], 1)
    for j, side in enumerate(NEAR):
        absent(side, krecv.at[j], 1)
    mask[...] = zero_rows
    for f in range(2):
        adj[f] = zero_rows
        grd[f] = zero_rows
        mid[f] = zero_rows
    for x in range(-1, 9):
        mask[rows(x, -1, 10), :] = jnp.ones((10, LANES), jnp.float32)


    wait_all(sum(halo_part(i, True).size for i in range(8)), 0)
    for i, side in enumerate(SIDES):
        unpack(side, True, srecv, (i,), ext, fits(*side))
    look_up_rows(0, ROWS, 32)
    face_rows(0, 144, 24)
    for lo in range(16, 144, 16):
        here = pl.ds(lo, 16)
        total = jnp.zeros((16, LANES), jnp.float32)
        out = total
        for d in range(3):
            trans, upper, lower = (face[3 * d + m, here, :] for m in range(3))
            if d < 2:
                back = pl.ds(lo - (PITCH, 1)[d], 16)
                trans_m, lower_m = face[3 * d, back, :], face[3 * d + 2, back, :]
            else:
                trans_m, lower_m = last_lane(trans), last_lane(lower)
            co[TX + 2 * d, here, :] = trans
            co[TX + 2 * d + 1, here, :] = trans_m
            co[SX + 2 * d, here, :] = DISP * trans + upper
            co[SX + 2 * d + 1, here, :] = DISP * trans_m + lower_m
            total = total + trans + trans_m
            out = out + upper + lower_m
        store = poro[here, :]
        bpp, bpc, bcp, bcc = store + total, -CPL_S * out, CPL_P * store, store + DISP * total + out
        inside = jnp.logical_and(store > 0.0, mask[here, :] > 0.0)
        determ = jnp.where(inside, bpp * bcc - bpc * bcp, 1.0)
        scale = jnp.where(inside, OMEGA / determ, 0.0)
        for at, value in (
            (BPP, bpp), (BPC, bpc), (BCP, bcp), (BCC, bcc),
            (IPP, bcc * scale), (IPC, -bpc * scale), (ICP, -bcp * scale), (ICC, bpp * scale),
        ):
            co[at, here, :] = value

    def fine_solve(src, at):
        for lo in range(16, 144, 32):
            here = pl.ds(lo, 32)
            r_p, r_c = src[at, here, :], src[at + 1, here, :]
            grd[0, here, :] = co[IPP, here, :] * r_p + co[IPC, here, :] * r_c
            grd[1, here, :] = co[ICP, here, :] * r_p + co[ICC, here, :] * r_c
        for lo in range(16, 144, 16):
            here = pl.ds(lo, 16)
            z_p, s_p, z_c, s_c = couple(co, grd, lo, 16)
            mid[0, here, :] = (2.0 - OMEGA) * z_p + co[IPP, here, :] * s_p + co[IPC, here, :] * s_c
            mid[1, here, :] = (2.0 - OMEGA) * z_c + co[ICP, here, :] * s_p + co[ICC, here, :] * s_c
        for lo in range(32, 128, 16):
            here = pl.ds(lo, 16)
            z_p, s_p, z_c, s_c = couple(co, mid, lo, 16)
            fin[0, here, :] = (1.0 - OMEGA) * z_p + grd[0, here, :] + co[IPP, here, :] * s_p + co[IPC, here, :] * s_c
            fin[1, here, :] = (1.0 - OMEGA) * z_c + grd[1, here, :] + co[ICP, here, :] * s_p + co[ICC, here, :] * s_c

    def coarse_solve():
        inv = [[cco[b, cx] for cx in range(2)] for b in range(4)]
        r = [[cres[2 * f + cx] for cx in range(2)] for f in range(2)]

        def inverse(v):
            return [[inv[2 * f][cx] * v[0][cx] + inv[2 * f + 1][cx] * v[1][cx] for cx in range(2)] for f in range(2)]

        base = inverse(r)
        z = base
        for sweep in range(3):
            acc = [[None] * 2 for f in range(2)]
            for f in range(2):
                for cx in range(2):
                    v = z[f][cx]
                    first = 4 + 5 * f
                    along = cco[first, cx] * pltpu.roll(v, 7, 0) + cco[first + 1, cx] * pltpu.roll(v, 1, 0)
                    down = cco[first + 2, cx] * next_lane(v, AGG) + cco[first + 3, cx] * last_lane(v, AGG)
                    acc[f][cx] = cco[first + 4, cx] * z[f][1 - cx] + (along + down)
            more = inverse(acc)
            z = [[((1.0 - OMEGA_C) * z[f][cx] + base[f][cx]) + more[f][cx] for cx in range(2)] for f in range(2)]
        upper = lax.broadcasted_iota(jnp.int32, (8, LANES), 0) < AGG
        return [
            [
                jnp.where(upper, jnp.broadcast_to(v[3:4], (8, LANES)), jnp.broadcast_to(v[4:5], (8, LANES)))
                for v in z[f]
            ]
            for f in range(2)
        ]

    def update():
        grown = coarse_solve()
        for f in range(2):
            for x in range(8):
                here = rows(x, 0)
                more = THETA * (fin[f, here, :] + grown[f][x // 4])
                new = adj[f, here, :] + more
                inc[f, x] = more
                adj[f, here, :] = new
                out_ref[f, x] = new

    def send(k):
        def place(at, value):
            ring[pl.ds(8 + at, 1), :] = value

        e = [[inc[f, x] for x in range(8)] for f in range(2)]
        for f in range(2):
            for cx in range(2):
                terms = [[], [], [], [], []]
                for x in range(4 * cx, 4 * cx + 4):
                    terms[0].append(wt[6 * f, x] * e[f][x] + wt[6 * f + 1, x] * e[1 - f][x])
                    for m in range(4):
                        terms[1 + m].append(wt[6 * f + 2 + m, x] * e[f][x])
                total, y_next, y_last, z_next, z_last = ((t[0] + t[1]) + (t[2] + t[3]) for t in terms)
                total = total - (last_lane(z_next) + next_lane(z_last))
                other = wx[f, 1, 0] * e[f][4] if cx == 0 else wx[f, 0, 1] * e[f][3]
                total = four_sum(total - other)
                at = 8 * f + 4 * cx
                place(at, -y_last[0:1])
                place(at + 1, total[0:1] - y_last[4:5])
                place(at + 2, total[4:5] - y_next[3:4])
                place(at + 3, -y_next[7:8])
            for at, value in ((16, wx[f, 0, 0] * e[f][0]), (20, wx[f, 1, 1] * e[f][7])):
                total = four_sum(value)
                place(at + 2 * f, -total[0:1])
                place(at + 2 * f + 1, -total[4:5])
        sums = lane_sum(ring[pl.ds(8, 24), :])
        ring[pl.ds(8, 24), :] = sums
        along, beside = sums[0:16], sums[16:24]
        for i, side in enumerate(PARTNERS):
            if side not in FAR:
                pack(side, False, adj, rsend, (k, i), PAD - rows_of(side, False))
            if side[0] == 0:
                rsend[k, i, pl.ds(PAD, 16), :] = along
            else:
                rsend[k, i, pl.ds(PAD, 8), :] = beside
            when_sent(side, lambda: round_copy(i, k).start())
        for i, side in enumerate(PARTNERS):
            absent(side, rrecv.at[k, i, halo_part(i, False)], 2 - 2 * lax.rem(k, 2))

    def receive(k):
        for i, side in enumerate(PARTNERS):
            when_sent(side, lambda: round_copy(i, k).wait_send())
        wait_all(sum(halo_part(i, False).size for i in range(N_PART)), 2 - 2 * lax.rem(k, 2))
        for i, side in enumerate(PARTNERS):
            if side not in FAR:
                unpack(side, False, rrecv, (k, i), adj, None, PAD - rows_of(side, False))
        at_row = lax.broadcasted_iota(jnp.int32, (8, LANES), 0)
        for f in range(2):
            for cx in range(2):
                item = 2 * f + cx

                def along(dy, shift):
                    return rrecv[k, PARTNERS.index((0, dy)), pl.ds(PAD + 4 * item + shift, 8), :]

                def beside(dy):
                    dx = 2 * cx - 1
                    at = PAD + (4 if dx < 0 else 0) + 2 * f
                    return rrecv[k, PARTNERS.index((dx, dy)), pl.ds(at - 2 * dy - 3, 8), :]

                one = jnp.where(at_row < 4, along(-1, 0), along(1, -4))
                two = jnp.where(at_row < 2, along(-2, 2), jnp.where(at_row < 6, ring[pl.ds(8 + 4 * item - 2, 8), :], along(2, -6)))
                three = jnp.where(at_row < 1, beside(-2), jnp.where(at_row < 3, beside(-1), beside(0)))
                three = jnp.where(at_row < 5, three, jnp.where(at_row < 7, beside(1), beside(2)))
                cres[item] = cres[item] - ((one + two) + three)
        for lo in range(16, 144, 16):
            here = pl.ds(lo, 16)
            z_p, s_p, z_c, s_c = couple(co, adj, lo, 16)
            res[0, here, :] = ext[COT, here, :] + s_p - co[BPP, here, :] * z_p - co[BPC, here, :] * z_c
            res[1, here, :] = ext[COT + 1, here, :] + s_c - co[BCP, here, :] * z_p - co[BCC, here, :] * z_c

    fine_solve(ext, COT)

    for i, side in enumerate(SIDES):
        when_sent(side, lambda: setup_copy(i).wait_send())
    for j, side in enumerate(NEAR):
        when_sent(side, lambda: coef_copy(j).wait_send())
        when_sent(FAR[j], lambda: edge_copy(j).wait_send())
    wait_all(4 * C_ROWS + 4 * 24, 1)

    def near(u):
        return NEAR.index((0, u))

    def inner(u, at, count):
        return (ksend[pl.ds(at, count), :] if u == 0 else krecv[near(u), pl.ds(at, count), :])

    def raw_of(u, slot):
        value = inner(u, C_RAW + 8 * slot, 8)
        return jnp.where(fits(0, u), value, -1.0) if u != 0 and slot in (0, 2, 5, 7) else value

    def beyond(dx, u, m):
        if u == 0:
            return ext[(MAT, HEAD, F0)[m], rows(-1 if dx < 0 else 8, 0), :]
        if abs(u) == 1:
            value = srecv[SIDES.index((dx, u)), pl.ds(24 + 8 * m, 8), :]
        else:
            value = xrecv[FAR.index((dx, u)), pl.ds(8 * m, 8), :]
        return jnp.where(fits(dx, u), value, -1.0) if m == 0 else value

    def between(mat_a, head_a, flag, mat_b, head_b):
        return one_face(look_up(mat_a)[0], head_a, look_up(mat_b)[0], head_b, flag)

    def put_rows(tile, u, value):
        value = four_sum(value)
        if u > -2:
            cedge[tile, pl.ds(2 * u + 3, 1), :] = value[0:1]
        if u < 2:
            cedge[tile, pl.ds(2 * u + 4, 1), :] = value[4:5]

    for tile in range(4, 10):
        cedge[tile] = jnp.zeros((8, LANES), jnp.float32)
    for u in range(-2, 3):
        trans, _, lower = between(*(beyond(-1, u, m) for m in range(3)), raw_of(u, 0), raw_of(u, 1))
        put_rows(0, u, trans)
        put_rows(1, u, lower)
        trans, upper, _ = between(raw_of(u, 2), raw_of(u, 3), raw_of(u, 4), beyond(1, u, 0), beyond(1, u, 1))
        put_rows(2, u, trans)
        put_rows(3, u, upper)
        if u < 2:
            values = between(raw_of(u, 7), raw_of(u, 8), raw_of(u, 9), raw_of(u + 1, 5), raw_of(u + 1, 6))
            for m in range(3):
                value = four_sum(values[m])
                for cx in range(2):
                    cedge[4 + 2 * m + cx, pl.ds(2 * u + 4, 1), :] = value[4 * cx : 4 * cx + 1]
    for tile in range(10):
        cedge[tile] = lane_sum(cedge[tile])
    for m in range(3):
        for cx in range(2):
            for u in range(-1, 3):
                cedge[4 + 2 * m + cx, pl.ds(2 * u + 3, 1), :] = inner(u, 34 + 2 * m + cx, 1)
    for item in range(N_INNER):

        def put_inner(where, value):
            if item < 13:
                cin[item, where, :] = value
            else:
                cres[item - 13, where, :] = value

        put_inner(pl.ds(0, 1), inner(-2, 2 * item + 1, 1))
        put_inner(pl.ds(1, 2), inner(-1, 2 * item, 2))
        put_inner(pl.ds(3, 2), inner(0, 2 * item, 2))
        put_inner(pl.ds(5, 2), inner(1, 2 * item, 2))
        put_inner(pl.ds(7, 1), inner(2, 2 * item, 1))

    place = lax.broadcasted_iota(jnp.int32, (8, LANES), 0)
    m_t, m_a, m_b = (cin[10 + m] for m in range(3))
    for cx in range(2):
        store, out, t_z, a_z, b_z = (cin[2 * m + cx] for m in range(5))
        t_y, a_y, b_y = (cedge[4 + 2 * m + cx] for m in range(3))
        under_t, under_b = (
            jnp.where(place == 0, jnp.broadcast_to(inner(-2, 34 + 2 * m + cx, 1), (8, LANES)), pltpu.roll(value, 1, 0))
            for m, value in ((0, t_y), (2, b_y))
        )
        side_t, side_out = (cedge[0], cedge[1]) if cx == 0 else (cedge[2], cedge[3])
        edge_sum = m_t + side_t + t_y + under_t + t_z + last_lane(t_z, AGG)
        edge_out = (m_a if cx == 0 else m_b) + side_out + a_y + under_b + a_z + last_lane(b_z, AGG)
        out = out + side_out + jnp.where(place % 2 == 0, a_y, under_b)
        cpp, cpc, ccp, ccc = store + edge_sum, -CPL_S * out, CPL_P * store, store + DISP * edge_sum + edge_out
        inside = cpp > 0.0
        determ = jnp.where(inside, cpp * ccc - cpc * ccp, 1.0)
        scale = jnp.where(inside, OMEGA_C / determ, 0.0)
        for b, value in enumerate((
            ccc * scale, -cpc * scale, -ccp * scale, cpp * scale,
            t_y, pltpu.roll(t_y, 1, 0), t_z, last_lane(t_z, AGG), m_t,
            DISP * t_y + a_y, pltpu.roll(DISP * t_y + b_y, 1, 0), DISP * t_z + a_z, last_lane(DISP * t_z + b_z, AGG),
            DISP * m_t + (m_a if cx == 0 else m_b),
        )):
            cco[b, cx] = value
    y_at = lax.broadcasted_iota(jnp.int32, (8, LANES), 0) % AGG
    z_at = lax.broadcasted_iota(jnp.int32, (8, LANES), 1) % AGG
    for x in range(8):
        here = rows(x, 0)
        to_next = [[co[TX + 2 * d, here, :] for d in range(3)], [DISP * face[3 * d, here, :] + face[3 * d + 2, here, :] for d in range(3)]]
        to_last = [
            [co[TXM + 2 * d, here, :] for d in range(3)],
            [co[SX, rows(x - 1, 0), :], co[SY, rows(x, -1), :], last_lane(co[SZ, here, :])],
        ]
        for f in range(2):
            own = co[BCC if f else BPP, here, :]
            if x % AGG != AGG - 1:
                own = own - to_next[f][0]
            if x % AGG != 0:
                own = own - to_last[f][0]
            y_next, y_last = (jnp.where(y_at == edge, v[f][1], 0.0) for edge, v in ((AGG - 1, to_next), (0, to_last)))
            z_next, z_last = (jnp.where(z_at == edge, v[f][2], 0.0) for edge, v in ((AGG - 1, to_next), (0, to_last)))
            own = own - (((to_next[f][1] - y_next) + (to_last[f][1] - y_last)) + ((to_next[f][2] - z_next) + (to_last[f][2] - z_last)))
            for m, value in enumerate((own, co[BCP if f else BPC, here, :], y_next, y_last, z_next, z_last)):
                wt[6 * f + m, x] = value
            if x % AGG == 0:
                wx[f, x // AGG, 0] = to_last[f][0]
            if x % AGG == AGG - 1:
                wx[f, x // AGG, 1] = to_next[f][0]

    update()
    send(0)

    def step(k, carry):
        receive(k - 1)
        fine_solve(res, 0)
        update()
        pl.when(k < ITERS - 1)(lambda: send(k))
        return carry

    lax.fori_loop(1, ITERS, step, 0)


def solution(mesh):
    n_grp, n_sub = mesh.shape["grp"], mesh.shape["sub"]

    def local(cotangent, head, materials, flags, perm_table, poro_table):
        def tile(*shape):
            return pltpu.VMEM(shape + (LANES,), jnp.float32)

        dma = pltpu.SemaphoreType.DMA
        vmem = pl.BlockSpec(memory_space=pltpu.VMEM)
        hbm = pl.BlockSpec(memory_space=pltpu.HBM)
        return pl.pallas_call(
            functools.partial(kernel, n_grp, n_sub),
            out_shape=pltpu.VMEM(cotangent.shape, jnp.float32),
            in_specs=[hbm] * 6,
            out_specs=vmem,
            scratch_shapes=[
                pltpu.VMEM(cotangent.shape, jnp.float32),
                pltpu.VMEM(head.shape, jnp.float32),
                pltpu.VMEM(materials.shape, jnp.int32),
                pltpu.VMEM(flags.shape, jnp.int32),
                pltpu.SMEM(perm_table.shape, jnp.float32),
                pltpu.SMEM(poro_table.shape, jnp.float32),
                tile(7, ROWS),
                tile(ROWS),
                tile(ROWS),
                tile(ROWS),
                tile(9, ROWS),
                tile(N_COEF, ROWS),
                tile(2, ROWS),
                tile(2, 8, 8),
                tile(2, ROWS),
                tile(2, ROWS),
                tile(2, ROWS),
                tile(2, ROWS),
                tile(8, 80),
                tile(8, 80),
                tile(ROUNDS, N_PART, R_ROWS),
                tile(ROUNDS, N_PART, R_ROWS),
                tile(2, 24),
                tile(4, 24),
                tile(C_ROWS),
                tile(4, C_ROWS),
                tile(13, 8),
                tile(10, 8),
                tile(32),
                tile(N_CBLK, 2, 8),
                tile(4, 8),
                tile(12, 8, 8),
                tile(2, 2, 2, 8),
                tile(C_ROWS),
                tile(4 * C_ROWS + 4 * 24),
                dma((N_PART + 2,)),
                dma((3,)),
            ],
            compiler_params=pltpu.CompilerParams(
                collective_id=0, has_side_effects=True, vmem_limit_bytes=32 * 1024 * 1024
            ),
        )(*(pltpu.with_memory_space_constraint(x, pltpu.HBM) for x in (cotangent, head, materials, flags, perm_table, poro_table)))

    return jax.shard_map(
        local,
        mesh=mesh,
        in_specs=(
            P(None, "grp", "sub", None),
            P("grp", "sub", None),
            P("grp", "sub", None),
            P(None, "grp", "sub", None),
            P(),
            P(),
        ),
        out_specs=P(None, "grp", "sub", None),
        check_vma=False,
    )
```

```python
import functools

import jax
import jax.numpy as jnp
from jax import lax
from jax.experimental import pallas as pl
from jax.experimental.pallas import tpu as pltpu
from jax.sharding import PartitionSpec as P

CX = 8
AGG = 4
ITERS = 4
DISP = 0.2
CPL_P = 0.5
CPL_S = 0.3
OMEGA = 0.7
OMEGA_C = 0.7
THETA = 0.5

PITCH = 12
BASE = 8
ROWS = 160
LANES = 128
MESH = pl.DeviceIdType.MESH

SIDES = [(-1, 0), (1, 0), (0, -1), (0, 1), (-1, -1), (-1, 1), (1, -1), (1, 1)]
FAR = [(-1, -2), (-1, 2), (1, -2), (1, 2), (0, -2), (0, 2)]
PARTNERS = FAR + SIDES[4:] + SIDES[:4]
NEAR = [(0, -2), (0, 2), (0, -1), (0, 1)]

MAT, HEAD, F0, F1, F2, COT = 0, 1, 2, 3, 4, 5
TX, TXM, TY, TYM, TZ, TZM, SX, SXM, SY, SYM, SZ, SZM, BPP, BPC, BCP, BCC, IPP, IPC, ICP, ICC = range(20)
N_COEF = 20
N_CBLK = 14
N_INNER = 17
C_ROWS = 120
C_RAW = 40
PAD = 40
R_ROWS = 64
ROUNDS = ITERS - 1
N_PART = 14


def row(x, y):
    return BASE + (x + 2) * PITCH + y + 2


def rows(x, y, count=8):
    return pl.ds(row(x, y), count)


def column(y):
    return pl.ds(row(0, y), 8, stride=PITCH)


def setup_slots(low, along):
    one, two = (-1, -2) if low else (8, 9)
    first = [(MAT, one), (HEAD, one), (along, one)]
    others = [(field, one) for field in (F0, F1, F2) if field != along]
    return first + others + [(MAT, two), (HEAD, two)] + ([(along, two)] if low else []) + [(COT, one), (COT + 1, one)]


def field_slots(low):
    return [(f, layer) for f in (0, 1) for layer in ((-2, -1) if low else (8, 9))]


def slots_of(side, setup):
    dx, dy = side
    if dx != 0:
        return setup_slots(dx < 0, F0) if setup else field_slots(dx < 0)
    return setup_slots(dy < 0, F1) if setup else field_slots(dy < 0)


def pack(side, setup, src, dst, lead, base=0):
    dx, dy = side
    for slot, (field, layer) in enumerate(slots_of(side, setup)):
        if dy == 0:
            dst[lead + (pl.ds(base + 8 * slot, 8),)] = src[field, rows(layer % 8, 0), :]
        elif dx == 0:
            dst[lead + (pl.ds(base + 8 * slot, 8),)] = src[field, column(layer % 8), :]
        else:
            dst[lead + (pl.ds(base + 2 * slot, 2),)] = src[field, rows(layer % 8, 6 if dy < 0 else 0, 2), :]


def unpack(side, setup, src, lead, dst, valid, base=0):
    dx, dy = side

    def seen(field, value):
        return jnp.where(valid, value, -1.0) if setup and field == MAT else value

    for slot, (field, layer) in enumerate(slots_of(side, setup)):
        if dy == 0:
            dst[field, rows(layer, 0), :] = seen(field, src[lead + (pl.ds(base + 8 * slot, 8),)])
        elif dx == 0:
            dst[field, column(layer), :] = seen(field, src[lead + (pl.ds(base + 8 * slot, 8),)])
        else:
            dst[field, rows(layer, -2 if dy < 0 else 8, 2), :] = seen(field, src[lead + (pl.ds(base + 2 * slot, 2),)])


def next_lane(value, by=1):
    return pltpu.roll(value, LANES - by, 1)


def last_lane(value, by=1):
    return pltpu.roll(value, by, 1)


def lane_sum(value):
    at = lax.broadcasted_iota(jnp.int32, value.shape, 1) % AGG
    one = jnp.where(at < 3, next_lane(value), last_lane(value, 3))
    two = jnp.where(at < 2, next_lane(value, 2), last_lane(value, 2))
    three = jnp.where(at < 1, next_lane(value, 3), last_lane(value))
    return (value + one) + (two + three)


def lane_pass(value):
    at = lax.broadcasted_iota(jnp.int32, value.shape, 1) % AGG
    back = jnp.where(at < 2, jnp.where(at < 1, last_lane(value), last_lane(value, 2)), jnp.where(at < 3, last_lane(value, 3), last_lane(value, 4)))
    ahead = jnp.where(at < 2, jnp.where(at < 1, next_lane(value, 4), next_lane(value, 3)), jnp.where(at < 3, next_lane(value, 2), next_lane(value)))
    return back + ahead


def four_sum(value):
    return (value + pltpu.roll(value, 7, 0)) + (pltpu.roll(value, 6, 0) + pltpu.roll(value, 5, 0))


def couple(co, field, lo, n):
    here = pl.ds(lo, n)
    out = []
    for f, first in ((0, TX), (1, SX)):
        mid = field[f, here, :]
        one = co[first, here, :] * field[f, pl.ds(lo + PITCH, n), :] + co[first + 1, here, :] * field[f, pl.ds(lo - PITCH, n), :]
        two = co[first + 2, here, :] * field[f, pl.ds(lo + 1, n), :] + co[first + 3, here, :] * field[f, pl.ds(lo - 1, n), :]
        three = co[first + 4, here, :] * next_lane(mid) + co[first + 5, here, :] * last_lane(mid)
        out += [mid, (one + two) + three]
    return out


def kernel(
    n_grp,
    n_sub,
    cot_hbm,
    head_hbm,
    mat_hbm,
    flag_hbm,
    perm_hbm,
    poro_hbm,
    out_ref,
    cot_ref,
    head_ref,
    mat_ref,
    flag_ref,
    perm_tab,
    poro_tab,
    ext,
    perm,
    poro,
    mask,
    face,
    co,
    adj,
    inc,
    res,
    grd,
    mid,
    fin,
    ssend,
    srecv,
    rsend,
    rrecv,
    xsend,
    xrecv,
    ksend,
    krecv,
    cin,
    cedge,
    ring,
    zring,
    cco,
    cres,
    wt,
    wx,
    zeros,
    counted,
    sent,
    came,
):
    g = lax.axis_index("grp")
    s = lax.axis_index("sub")

    def device(dx, dy):
        return {"grp": g + dx, "sub": s + dy}

    def fits(dx, dy):
        found = []
        for at, count, step in ((g, n_grp, dx), (s, n_sub, dy)):
            if step < 0:
                found.append(at >= -step)
            elif step > 0:
                found.append(at < count - step)
        return found[0] if len(found) == 1 else jnp.logical_and(*found)

    loads = [
        pltpu.make_async_copy(src, dst, sent.at[i])
        for i, (src, dst) in enumerate((
            (mat_hbm, mat_ref), (head_hbm, head_ref), (flag_hbm, flag_ref), (cot_hbm, cot_ref), (perm_hbm, perm_tab), (poro_hbm, poro_tab)
        ))
    ]
    for load in loads:
        load.start()

    barrier = pltpu.get_barrier_semaphore()
    expected = jnp.int32(0)
    for dx, dy in PARTNERS:
        there = fits(dx, dy)

        @pl.when(there)
        def _():
            pl.semaphore_signal(barrier, inc=1, device_id=device(dx, dy), device_id_type=MESH)

        expected = expected + there.astype(jnp.int32)

    def rows_of(side, setup):
        dx, dy = side
        if side in FAR:
            return 0
        if setup:
            count = len(slots_of(side, True)) * (2 if dx != 0 and dy != 0 else 8)
            return -(-count // 8) * 8
        return 8 if dx != 0 and dy != 0 else 32

    def halo_part(i, setup):
        side = SIDES[i] if setup else PARTNERS[i]
        halo = rows_of(side, setup)
        if setup:
            return pl.ds(0, halo + (24 if i >= 4 else 0))
        return pl.ds(PAD - halo, halo + (16 if side[0] == 0 else 8))

    def absent(side, dst, at):
        @pl.when(jnp.logical_not(fits(*side)))
        def _():
            pltpu.make_async_copy(zeros.at[pl.ds(0, dst.shape[0])], dst, came.at[at]).start()

    def wait_all(count, at):
        part = counted.at[pl.ds(0, count)]
        pltpu.make_async_copy(part, part, came.at[at]).wait()

    def setup_copy(i):
        dx, dy = SIDES[i]
        part = halo_part(i, True)
        at = PARTNERS.index((dx, dy))
        return pltpu.make_async_remote_copy(
            ssend.at[i, part], srecv.at[i, part], sent.at[at], came.at[0], device_id=device(-dx, -dy), device_id_type=MESH
        )

    def edge_copy(i):
        dx, dy = FAR[i]
        return pltpu.make_async_remote_copy(
            xsend.at[0 if dx < 0 else 1], xrecv.at[i], sent.at[i], came.at[1], device_id=device(-dx, -dy), device_id_type=MESH
        )

    def round_copy(i, k):
        dx, dy = PARTNERS[i]
        part = halo_part(i, False)
        return pltpu.make_async_remote_copy(
            rsend.at[k, i, part], rrecv.at[k, i, part], sent.at[i], came.at[2 - 2 * lax.rem(k, 2)], device_id=device(-dx, -dy), device_id_type=MESH
        )

    def coef_copy(j):
        dx, dy = NEAR[j]
        at = PARTNERS.index((dx, dy)) if abs(dy) == 2 else N_PART + j - 2
        return pltpu.make_async_remote_copy(
            ksend, krecv.at[j], sent.at[at], came.at[1], device_id=device(-dx, -dy), device_id_type=MESH
        )

    def when_sent(side, act):
        pl.when(fits(-side[0], -side[1]))(act)

    zero_rows = jnp.zeros((ROWS, LANES), jnp.float32)
    ext[MAT] = zero_rows - 1.0
    for f in range(1, 7):
        ext[f] = zero_rows
    perm[...] = zero_rows
    poro[...] = zero_rows
    for m in range(9):
        face[m, pl.ds(0, 32), :] = jnp.zeros((32, LANES), jnp.float32)
    for load in loads:
        load.wait()
    for x in range(8):
        ext[MAT, rows(x, 0), :] = mat_ref[x].astype(jnp.float32)
        ext[HEAD, rows(x, 0), :] = head_ref[x]
        for d in range(3):
            ext[F0 + d, rows(x, 0), :] = flag_ref[d, x].astype(jnp.float32)
        for f in range(2):
            ext[COT + f, rows(x, 0), :] = cot_ref[f, x]
    for i, x in enumerate((7, 0)):
        for m, field in enumerate((MAT, HEAD, F0)):
            xsend[i, pl.ds(8 * m, 8), :] = ext[field, rows(x, 0), :]
    for i, side in enumerate(SIDES):
        pack(side, True, ext, ssend, (i,))
        if i >= 4:
            ssend[i, pl.ds(24, 24), :] = xsend[0 if side[0] < 0 else 1]

    def look_up(mats):
        perm_here = jnp.zeros_like(mats)
        poro_here = jnp.zeros_like(mats)
        for level in range(perm_tab.shape[0]):
            same = mats == float(level)
            perm_here = jnp.where(same, perm_tab[level], perm_here)
            poro_here = jnp.where(same, poro_tab[level], poro_here)
        return perm_here, poro_here

    def one_face(perm_here, head_here, perm_next, head_next, upwind):
        both = perm_here + perm_next
        trans = 2.0 * perm_here * perm_next / jnp.where(both > 0.0, both, 1.0)
        flux = trans * (0.5 + jnp.abs(head_here - head_next))
        return trans, upwind * flux, (1.0 - upwind) * flux

    def look_up_rows(first, end, n):
        for lo in range(first, end, n):
            here = pl.ds(lo, n)
            perm[here, :], poro[here, :] = look_up(ext[MAT, here, :])

    def face_rows(first, end, n):
        for lo in range(first, end, n):
            here = pl.ds(lo, n)
            perm_here, head_here = perm[here, :], ext[HEAD, here, :]
            lane = lax.broadcasted_iota(jnp.int32, (n, LANES), 1)
            for d in range(3):
                if d < 2:
                    there = pl.ds(lo + (PITCH, 1)[d], n)
                    perm_next, head_next = perm[there, :], ext[HEAD, there, :]
                else:
                    perm_next = jnp.where(lane == LANES - 1, 0.0, next_lane(perm_here))
                    head_next = next_lane(head_here)
                values = one_face(perm_here, head_here, perm_next, head_next, ext[F0 + d, here, :])
                for m in range(3):
                    face[3 * d + m, here, :] = values[m]

    look_up_rows(32, 128, 32)
    face_rows(32, 128, 24)

    def put(ref, at, value):
        value = four_sum(value)
        ref[pl.ds(at, 1), :] = value[0:1]
        ref[pl.ds(at + 1, 1), :] = value[4:5]

    lane = lax.broadcasted_iota(jnp.int32, (8, LANES), 1)
    for cx in range(2):
        sums = [0.0] * 7
        for x in range(4 * cx, 4 * cx + 4):
            here = rows(x, 0)
            zs = [face[6 + m, here, :] for m in range(3)]
            out = face[1, here, :] + face[4, here, :] + zs[1]
            out = out + face[2, rows(x - 1, 0), :] + face[5, rows(x, -1), :] + last_lane(zs[2])
            news = [poro[here, :], out] + zs + [ext[COT + f, here, :] for f in range(2)]
            sums = [old + new for old, new in zip(sums, news)]
        for m in range(2, 5):
            sums[m] = jnp.where(lane % AGG == AGG - 1, sums[m], 0.0)
        for item, value in zip((0, 2, 4, 6, 8, 13, 15), sums):
            put(ksend, 2 * (item + cx), value)
    for m in range(3):
        put(ksend, 2 * (10 + m), face[m, rows(3, 0), :])
        put(ksend, 2 * (17 + m), face[3 + m, column(3), :])
    ksend[pl.ds(0, C_RAW), :] = lane_sum(ksend[pl.ds(0, C_RAW), :])
    raw = [
        (MAT, rows(0, 0)), (HEAD, rows(0, 0)), (MAT, rows(7, 0)), (HEAD, rows(7, 0)), (F0, rows(7, 0)),
        (MAT, column(0)), (HEAD, column(0)), (MAT, column(7)), (HEAD, column(7)), (F1, column(7)),
    ]
    for slot, (field, where) in enumerate(raw):
        ksend[pl.ds(C_RAW + 8 * slot, 8), :] = ext[field, where, :]
    pl.semaphore_wait(barrier, expected)
    for i in reversed(range(8)):
        when_sent(SIDES[i], lambda: setup_copy(i).start())
    for i in range(4):
        when_sent(FAR[i], lambda: edge_copy(i).start())

    for j in range(4):
        when_sent(NEAR[j], lambda: coef_copy(j).start())

    zeros[...] = jnp.zeros((C_ROWS, LANES), jnp.float32)
    for i, side in enumerate(SIDES):
        absent(side, srecv.at[i, halo_part(i, True)], 0)
    for i, side in enumerate(FAR[:4]):
        absent(side, xrecv.at[i], 1)
    for j, side in enumerate(NEAR):
        absent(side, krecv.at[j], 1)
    zring[...] = jnp.zeros((16, LANES), jnp.float32)
    mask[...] = zero_rows
    for f in range(2):
        adj[f] = zero_rows
        grd[f] = zero_rows
        mid[f] = zero_rows
    for x in range(-1, 9):
        mask[rows(x, -1, 10), :] = jnp.ones((10, LANES), jnp.float32)


    wait_all(sum(halo_part(i, True).size for i in range(8)), 0)
    for i, side in enumerate(SIDES):
        unpack(side, True, srecv, (i,), ext, fits(*side))
    look_up_rows(0, ROWS, 32)
    face_rows(0, 144, 24)
    for lo in range(16, 144, 16):
        here = pl.ds(lo, 16)
        total = jnp.zeros((16, LANES), jnp.float32)
        out = total
        for d in range(3):
            trans, upper, lower = (face[3 * d + m, here, :] for m in range(3))
            if d < 2:
                back = pl.ds(lo - (PITCH, 1)[d], 16)
                trans_m, lower_m = face[3 * d, back, :], face[3 * d + 2, back, :]
            else:
                trans_m, lower_m = last_lane(trans), last_lane(lower)
            co[TX + 2 * d, here, :] = trans
            co[TX + 2 * d + 1, here, :] = trans_m
            co[SX + 2 * d, here, :] = DISP * trans + upper
            co[SX + 2 * d + 1, here, :] = DISP * trans_m + lower_m
            total = total + trans + trans_m
            out = out + upper + lower_m
        store = poro[here, :]
        bpp, bpc, bcp, bcc = store + total, -CPL_S * out, CPL_P * store, store + DISP * total + out
        inside = jnp.logical_and(store > 0.0, mask[here, :] > 0.0)
        determ = jnp.where(inside, bpp * bcc - bpc * bcp, 1.0)
        scale = jnp.where(inside, OMEGA / determ, 0.0)
        for at, value in (
            (BPP, bpp), (BPC, bpc), (BCP, bcp), (BCC, bcc),
            (IPP, bcc * scale), (IPC, -bpc * scale), (ICP, -bcp * scale), (ICC, bpp * scale),
        ):
            co[at, here, :] = value

    def fine_solve(src, at):
        for lo in range(16, 144, 32):
            here = pl.ds(lo, 32)
            r_p, r_c = src[at, here, :], src[at + 1, here, :]
            grd[0, here, :] = co[IPP, here, :] * r_p + co[IPC, here, :] * r_c
            grd[1, here, :] = co[ICP, here, :] * r_p + co[ICC, here, :] * r_c
        for lo in range(16, 144, 16):
            here = pl.ds(lo, 16)
            z_p, s_p, z_c, s_c = couple(co, grd, lo, 16)
            mid[0, here, :] = (2.0 - OMEGA) * z_p + co[IPP, here, :] * s_p + co[IPC, here, :] * s_c
            mid[1, here, :] = (2.0 - OMEGA) * z_c + co[ICP, here, :] * s_p + co[ICC, here, :] * s_c
        for lo in range(32, 128, 16):
            here = pl.ds(lo, 16)
            z_p, s_p, z_c, s_c = couple(co, mid, lo, 16)
            fin[0, here, :] = (1.0 - OMEGA) * z_p + grd[0, here, :] + co[IPP, here, :] * s_p + co[IPC, here, :] * s_c
            fin[1, here, :] = (1.0 - OMEGA) * z_c + grd[1, here, :] + co[ICP, here, :] * s_p + co[ICC, here, :] * s_c

    def coarse_solve():
        inv = [[cco[b, cx] for cx in range(2)] for b in range(4)]
        r = [[cres[2 * f + cx] for cx in range(2)] for f in range(2)]

        def inverse(v):
            return [[inv[2 * f][cx] * v[0][cx] + inv[2 * f + 1][cx] * v[1][cx] for cx in range(2)] for f in range(2)]

        base = inverse(r)
        z = base
        for sweep in range(3):
            acc = [[None] * 2 for f in range(2)]
            for f in range(2):
                for cx in range(2):
                    v = z[f][cx]
                    first = 4 + 5 * f
                    along = cco[first, cx] * pltpu.roll(v, 7, 0) + cco[first + 1, cx] * pltpu.roll(v, 1, 0)
                    down = cco[first + 2, cx] * next_lane(v, AGG) + cco[first + 3, cx] * last_lane(v, AGG)
                    acc[f][cx] = cco[first + 4, cx] * z[f][1 - cx] + (along + down)
            more = inverse(acc)
            z = [[((1.0 - OMEGA_C) * z[f][cx] + base[f][cx]) + more[f][cx] for cx in range(2)] for f in range(2)]
        upper = lax.broadcasted_iota(jnp.int32, (8, LANES), 0) < AGG
        return [
            [
                jnp.where(upper, jnp.broadcast_to(v[3:4], (8, LANES)), jnp.broadcast_to(v[4:5], (8, LANES)))
                for v in z[f]
            ]
            for f in range(2)
        ]

    def update():
        grown = coarse_solve()
        for f in range(2):
            for x in range(8):
                here = rows(x, 0)
                more = THETA * (fin[f, here, :] + grown[f][x // 4])
                new = adj[f, here, :] + more
                inc[f, x] = more
                adj[f, here, :] = new
                out_ref[f, x] = new

    def send(k):
        def place(at, value):
            ring[pl.ds(8 + at, 1), :] = value

        e = [[inc[f, x] for x in range(8)] for f in range(2)]
        for f in range(2):
            for cx in range(2):
                terms = [[], [], [], [], []]
                for x in range(4 * cx, 4 * cx + 4):
                    terms[0].append(wt[6 * f, x] * e[f][x] + wt[6 * f + 1, x] * e[1 - f][x])
                    for m in range(4):
                        terms[1 + m].append(wt[6 * f + 2 + m, x] * e[f][x])
                total, y_next, y_last, z_next, z_last = ((t[0] + t[1]) + (t[2] + t[3]) for t in terms)
                passed = four_sum(z_next + z_last)
                zring[pl.ds(8 * f + 4 * cx + 1, 1), :] = passed[0:1]
                zring[pl.ds(8 * f + 4 * cx + 2, 1), :] = passed[4:5]
                other = wx[f, 1, 0] * e[f][4] if cx == 0 else wx[f, 0, 1] * e[f][3]
                total = four_sum(total - other)
                at = 8 * f + 4 * cx
                place(at, -y_last[0:1])
                place(at + 1, total[0:1] - y_last[4:5])
                place(at + 2, total[4:5] - y_next[3:4])
                place(at + 3, -y_next[7:8])
            for at, value in ((16, wx[f, 0, 0] * e[f][0]), (20, wx[f, 1, 1] * e[f][7])):
                total = four_sum(value)
                place(at + 2 * f, -total[0:1])
                place(at + 2 * f + 1, -total[4:5])
        along = lane_sum(ring[pl.ds(8, 16), :]) - lane_pass(zring[...])
        beside = lane_sum(ring[pl.ds(24, 8), :])
        ring[pl.ds(8, 16), :] = along
        for i, side in enumerate(PARTNERS):
            if side not in FAR:
                pack(side, False, adj, rsend, (k, i), PAD - rows_of(side, False))
            if side[0] == 0:
                rsend[k, i, pl.ds(PAD, 16), :] = along
            else:
                rsend[k, i, pl.ds(PAD, 8), :] = beside
            when_sent(side, lambda: round_copy(i, k).start())
        for i, side in enumerate(PARTNERS):
            absent(side, rrecv.at[k, i, halo_part(i, False)], 2 - 2 * lax.rem(k, 2))

    def receive(k):
        for i, side in enumerate(PARTNERS):
            when_sent(side, lambda: round_copy(i, k).wait_send())
        wait_all(sum(halo_part(i, False).size for i in range(N_PART)), 2 - 2 * lax.rem(k, 2))
        for i, side in enumerate(PARTNERS):
            if side not in FAR:
                unpack(side, False, rrecv, (k, i), adj, None, PAD - rows_of(side, False))
        at_row = lax.broadcasted_iota(jnp.int32, (8, LANES), 0)
        for f in range(2):
            for cx in range(2):
                item = 2 * f + cx

                def along(dy, shift):
                    return rrecv[k, PARTNERS.index((0, dy)), pl.ds(PAD + 4 * item + shift, 8), :]

                def beside(dy):
                    dx = 2 * cx - 1
                    at = PAD + (4 if dx < 0 else 0) + 2 * f
                    return rrecv[k, PARTNERS.index((dx, dy)), pl.ds(at - 2 * dy - 3, 8), :]

                one = jnp.where(at_row < 4, along(-1, 0), along(1, -4))
                two = jnp.where(at_row < 2, along(-2, 2), jnp.where(at_row < 6, ring[pl.ds(8 + 4 * item - 2, 8), :], along(2, -6)))
                three = jnp.where(at_row < 1, beside(-2), jnp.where(at_row < 3, beside(-1), beside(0)))
                three = jnp.where(at_row < 5, three, jnp.where(at_row < 7, beside(1), beside(2)))
                cres[item] = cres[item] - ((one + two) + three)
        for lo in range(16, 144, 16):
            here = pl.ds(lo, 16)
            z_p, s_p, z_c, s_c = couple(co, adj, lo, 16)
            res[0, here, :] = ext[COT, here, :] + s_p - co[BPP, here, :] * z_p - co[BPC, here, :] * z_c
            res[1, here, :] = ext[COT + 1, here, :] + s_c - co[BCP, here, :] * z_p - co[BCC, here, :] * z_c

    fine_solve(ext, COT)

    for i, side in enumerate(SIDES):
        when_sent(side, lambda: setup_copy(i).wait_send())
    for j, side in enumerate(NEAR):
        when_sent(side, lambda: coef_copy(j).wait_send())
        when_sent(FAR[j], lambda: edge_copy(j).wait_send())
    wait_all(4 * C_ROWS + 4 * 24, 1)

    def near(u):
        return NEAR.index((0, u))

    def inner(u, at, count):
        return (ksend[pl.ds(at, count), :] if u == 0 else krecv[near(u), pl.ds(at, count), :])

    def raw_of(u, slot):
        value = inner(u, C_RAW + 8 * slot, 8)
        return jnp.where(fits(0, u), value, -1.0) if u != 0 and slot in (0, 2, 5, 7) else value

    def beyond(dx, u, m):
        if u == 0:
            return ext[(MAT, HEAD, F0)[m], rows(-1 if dx < 0 else 8, 0), :]
        if abs(u) == 1:
            value = srecv[SIDES.index((dx, u)), pl.ds(24 + 8 * m, 8), :]
        else:
            value = xrecv[FAR.index((dx, u)), pl.ds(8 * m, 8), :]
        return jnp.where(fits(dx, u), value, -1.0) if m == 0 else value

    def between(mat_a, head_a, flag, mat_b, head_b):
        return one_face(look_up(mat_a)[0], head_a, look_up(mat_b)[0], head_b, flag)

    def put_rows(tile, u, value):
        value = four_sum(value)
        if u > -2:
            cedge[tile, pl.ds(2 * u + 3, 1), :] = value[0:1]
        if u < 2:
            cedge[tile, pl.ds(2 * u + 4, 1), :] = value[4:5]

    for tile in range(4, 10):
        cedge[tile] = jnp.zeros((8, LANES), jnp.float32)
    for u in range(-2, 3):
        trans, _, lower = between(*(beyond(-1, u, m) for m in range(3)), raw_of(u, 0), raw_of(u, 1))
        put_rows(0, u, trans)
        put_rows(1, u, lower)
        trans, upper, _ = between(raw_of(u, 2), raw_of(u, 3), raw_of(u, 4), beyond(1, u, 0), beyond(1, u, 1))
        put_rows(2, u, trans)
        put_rows(3, u, upper)
        if u < 2:
            values = between(raw_of(u, 7), raw_of(u, 8), raw_of(u, 9), raw_of(u + 1, 5), raw_of(u + 1, 6))
            for m in range(3):
                value = four_sum(values[m])
                for cx in range(2):
                    cedge[4 + 2 * m + cx, pl.ds(2 * u + 4, 1), :] = value[4 * cx : 4 * cx + 1]
    for tile in range(10):
        cedge[tile] = lane_sum(cedge[tile])
    for m in range(3):
        for cx in range(2):
            for u in range(-1, 3):
                cedge[4 + 2 * m + cx, pl.ds(2 * u + 3, 1), :] = inner(u, 34 + 2 * m + cx, 1)
    for item in range(N_INNER):

        def put_inner(where, value):
            if item < 13:
                cin[item, where, :] = value
            else:
                cres[item - 13, where, :] = value

        put_inner(pl.ds(0, 1), inner(-2, 2 * item + 1, 1))
        put_inner(pl.ds(1, 2), inner(-1, 2 * item, 2))
        put_inner(pl.ds(3, 2), inner(0, 2 * item, 2))
        put_inner(pl.ds(5, 2), inner(1, 2 * item, 2))
        put_inner(pl.ds(7, 1), inner(2, 2 * item, 1))

    place = lax.broadcasted_iota(jnp.int32, (8, LANES), 0)
    m_t, m_a, m_b = (cin[10 + m] for m in range(3))
    for cx in range(2):
        store, out, t_z, a_z, b_z = (cin[2 * m + cx] for m in range(5))
        t_y, a_y, b_y = (cedge[4 + 2 * m + cx] for m in range(3))
        under_t, under_b = (
            jnp.where(place == 0, jnp.broadcast_to(inner(-2, 34 + 2 * m + cx, 1), (8, LANES)), pltpu.roll(value, 1, 0))
            for m, value in ((0, t_y), (2, b_y))
        )
        side_t, side_out = (cedge[0], cedge[1]) if cx == 0 else (cedge[2], cedge[3])
        edge_sum = m_t + side_t + t_y + under_t + t_z + last_lane(t_z, AGG)
        edge_out = (m_a if cx == 0 else m_b) + side_out + a_y + under_b + a_z + last_lane(b_z, AGG)
        out = out + side_out + jnp.where(place % 2 == 0, a_y, under_b)
        cpp, cpc, ccp, ccc = store + edge_sum, -CPL_S * out, CPL_P * store, store + DISP * edge_sum + edge_out
        inside = cpp > 0.0
        determ = jnp.where(inside, cpp * ccc - cpc * ccp, 1.0)
        scale = jnp.where(inside, OMEGA_C / determ, 0.0)
        for b, value in enumerate((
            ccc * scale, -cpc * scale, -ccp * scale, cpp * scale,
            t_y, pltpu.roll(t_y, 1, 0), t_z, last_lane(t_z, AGG), m_t,
            DISP * t_y + a_y, pltpu.roll(DISP * t_y + b_y, 1, 0), DISP * t_z + a_z, last_lane(DISP * t_z + b_z, AGG),
            DISP * m_t + (m_a if cx == 0 else m_b),
        )):
            cco[b, cx] = value
    y_at = lax.broadcasted_iota(jnp.int32, (8, LANES), 0) % AGG
    z_at = lax.broadcasted_iota(jnp.int32, (8, LANES), 1) % AGG
    for x in range(8):
        here = rows(x, 0)
        to_next = [[co[TX + 2 * d, here, :] for d in range(3)], [DISP * face[3 * d, here, :] + face[3 * d + 2, here, :] for d in range(3)]]
        to_last = [
            [co[TXM + 2 * d, here, :] for d in range(3)],
            [co[SX, rows(x - 1, 0), :], co[SY, rows(x, -1), :], last_lane(co[SZ, here, :])],
        ]
        for f in range(2):
            own = co[BCC if f else BPP, here, :]
            if x % AGG != AGG - 1:
                own = own - to_next[f][0]
            if x % AGG != 0:
                own = own - to_last[f][0]
            y_next, y_last = (jnp.where(y_at == edge, v[f][1], 0.0) for edge, v in ((AGG - 1, to_next), (0, to_last)))
            z_next, z_last = (jnp.where(z_at == edge, v[f][2], 0.0) for edge, v in ((AGG - 1, to_next), (0, to_last)))
            own = own - (((to_next[f][1] - y_next) + (to_last[f][1] - y_last)) + ((to_next[f][2] - z_next) + (to_last[f][2] - z_last)))
            for m, value in enumerate((own, co[BCP if f else BPC, here, :], y_next, y_last, z_next, z_last)):
                wt[6 * f + m, x] = value
            if x % AGG == 0:
                wx[f, x // AGG, 0] = to_last[f][0]
            if x % AGG == AGG - 1:
                wx[f, x // AGG, 1] = to_next[f][0]

    update()
    send(0)

    def step(k, carry):
        receive(k - 1)
        fine_solve(res, 0)
        update()
        pl.when(k < ITERS - 1)(lambda: send(k))
        return carry

    lax.fori_loop(1, ITERS, step, 0)


def solution(mesh):
    n_grp, n_sub = mesh.shape["grp"], mesh.shape["sub"]

    def local(cotangent, head, materials, flags, perm_table, poro_table):
        def tile(*shape):
            return pltpu.VMEM(shape + (LANES,), jnp.float32)

        dma = pltpu.SemaphoreType.DMA
        vmem = pl.BlockSpec(memory_space=pltpu.VMEM)
        hbm = pl.BlockSpec(memory_space=pltpu.HBM)
        return pl.pallas_call(
            functools.partial(kernel, n_grp, n_sub),
            out_shape=pltpu.VMEM(cotangent.shape, jnp.float32),
            in_specs=[hbm] * 6,
            out_specs=vmem,
            scratch_shapes=[
                pltpu.VMEM(cotangent.shape, jnp.float32),
                pltpu.VMEM(head.shape, jnp.float32),
                pltpu.VMEM(materials.shape, jnp.int32),
                pltpu.VMEM(flags.shape, jnp.int32),
                pltpu.SMEM(perm_table.shape, jnp.float32),
                pltpu.SMEM(poro_table.shape, jnp.float32),
                tile(7, ROWS),
                tile(ROWS),
                tile(ROWS),
                tile(ROWS),
                tile(9, ROWS),
                tile(N_COEF, ROWS),
                tile(2, ROWS),
                tile(2, 8, 8),
                tile(2, ROWS),
                tile(2, ROWS),
                tile(2, ROWS),
                tile(2, ROWS),
                tile(8, 80),
                tile(8, 80),
                tile(ROUNDS, N_PART, R_ROWS),
                tile(ROUNDS, N_PART, R_ROWS),
                tile(2, 24),
                tile(4, 24),
                tile(C_ROWS),
                tile(4, C_ROWS),
                tile(13, 8),
                tile(10, 8),
                tile(32),
                tile(16),
                tile(N_CBLK, 2, 8),
                tile(4, 8),
                tile(12, 8, 8),
                tile(2, 2, 2, 8),
                tile(C_ROWS),
                tile(4 * C_ROWS + 4 * 24),
                dma((N_PART + 2,)),
                dma((3,)),
            ],
            compiler_params=pltpu.CompilerParams(
                collective_id=0, has_side_effects=True, vmem_limit_bytes=32 * 1024 * 1024
            ),
        )(*(pltpu.with_memory_space_constraint(x, pltpu.HBM) for x in (cotangent, head, materials, flags, perm_table, poro_table)))

    return jax.shard_map(
        local,
        mesh=mesh,
        in_specs=(
            P(None, "grp", "sub", None),
            P("grp", "sub", None),
            P("grp", "sub", None),
            P(None, "grp", "sub", None),
            P(),
            P(),
        ),
        out_specs=P(None, "grp", "sub", None),
        check_vma=False,
    )
```

```python
import functools

import jax
import jax.numpy as jnp
from jax import lax
from jax.experimental import pallas as pl
from jax.experimental.pallas import tpu as pltpu
from jax.sharding import PartitionSpec as P

CX = 8
AGG = 4
ITERS = 4
DISP = 0.2
CPL_P = 0.5
CPL_S = 0.3
OMEGA = 0.7
OMEGA_C = 0.7
THETA = 0.5

PITCH = 12
BASE = 8
ROWS = 160
LANES = 128
MESH = pl.DeviceIdType.MESH

SIDES = [(-1, 0), (1, 0), (0, -1), (0, 1), (-1, -1), (-1, 1), (1, -1), (1, 1)]
FAR = [(-1, -2), (-1, 2), (1, -2), (1, 2), (0, -2), (0, 2)]
PARTNERS = FAR + SIDES[4:] + SIDES[:4]
NEAR = [(0, -2), (0, 2), (0, -1), (0, 1)]

MAT, HEAD, F0, F1, F2, COT = 0, 1, 2, 3, 4, 5
TX, TXM, TY, TYM, TZ, TZM, SX, SXM, SY, SYM, SZ, SZM, BPP, BPC, BCP, BCC, IPP, IPC, ICP, ICC = range(20)
N_COEF = 20
N_CBLK = 14
N_INNER = 17
C_ROWS = 120
C_RAW = 40
PAD = 40
R_ROWS = 64
ROUNDS = ITERS - 1
N_PART = 14


def row(x, y):
    return BASE + (x + 2) * PITCH + y + 2


def rows(x, y, count=8):
    return pl.ds(row(x, y), count)


def column(y):
    return pl.ds(row(0, y), 8, stride=PITCH)


def setup_slots(low, along):
    one, two = (-1, -2) if low else (8, 9)
    first = [(MAT, one), (HEAD, one), (along, one)]
    others = [(field, one) for field in (F0, F1, F2) if field != along]
    return first + others + [(MAT, two), (HEAD, two)] + ([(along, two)] if low else []) + [(COT, one), (COT + 1, one)]


def field_slots(low):
    return [(f, layer) for f in (0, 1) for layer in ((-2, -1) if low else (8, 9))]


def slots_of(side, setup):
    dx, dy = side
    if dx != 0:
        return setup_slots(dx < 0, F0) if setup else field_slots(dx < 0)
    return setup_slots(dy < 0, F1) if setup else field_slots(dy < 0)


def pack(side, setup, src, dst, lead, base=0):
    dx, dy = side
    for slot, (field, layer) in enumerate(slots_of(side, setup)):
        if dy == 0:
            dst[lead + (pl.ds(base + 8 * slot, 8),)] = src[field, rows(layer % 8, 0), :]
        elif dx == 0:
            dst[lead + (pl.ds(base + 8 * slot, 8),)] = src[field, column(layer % 8), :]
        else:
            dst[lead + (pl.ds(base + 2 * slot, 2),)] = src[field, rows(layer % 8, 6 if dy < 0 else 0, 2), :]


def unpack(side, setup, src, lead, dst, valid, base=0):
    dx, dy = side

    def seen(field, value):
        return jnp.where(valid, value, -1.0) if setup and field == MAT else value

    for slot, (field, layer) in enumerate(slots_of(side, setup)):
        if dy == 0:
            dst[field, rows(layer, 0), :] = seen(field, src[lead + (pl.ds(base + 8 * slot, 8),)])
        elif dx == 0:
            dst[field, column(layer), :] = seen(field, src[lead + (pl.ds(base + 8 * slot, 8),)])
        else:
            dst[field, rows(layer, -2 if dy < 0 else 8, 2), :] = seen(field, src[lead + (pl.ds(base + 2 * slot, 2),)])


def next_lane(value, by=1):
    return pltpu.roll(value, LANES - by, 1)


def last_lane(value, by=1):
    return pltpu.roll(value, by, 1)


def lane_sum(value):
    at = lax.broadcasted_iota(jnp.int32, value.shape, 1) % AGG
    one = jnp.where(at < 3, next_lane(value), last_lane(value, 3))
    two = jnp.where(at < 2, next_lane(value, 2), last_lane(value, 2))
    three = jnp.where(at < 1, next_lane(value, 3), last_lane(value))
    return (value + one) + (two + three)


def lane_pass(value):
    at = lax.broadcasted_iota(jnp.int32, value.shape, 1) % AGG
    back = jnp.where(at < 2, jnp.where(at < 1, last_lane(value), last_lane(value, 2)), jnp.where(at < 3, last_lane(value, 3), last_lane(value, 4)))
    ahead = jnp.where(at < 2, jnp.where(at < 1, next_lane(value, 4), next_lane(value, 3)), jnp.where(at < 3, next_lane(value, 2), next_lane(value)))
    return back + ahead


def four_sum(value):
    return (value + pltpu.roll(value, 7, 0)) + (pltpu.roll(value, 6, 0) + pltpu.roll(value, 5, 0))


def couple(co, field, lo, n):
    here = pl.ds(lo, n)
    out = []
    for f, first in ((0, TX), (1, SX)):
        mid = field[f, here, :]
        one = co[first, here, :] * field[f, pl.ds(lo + PITCH, n), :] + co[first + 1, here, :] * field[f, pl.ds(lo - PITCH, n), :]
        two = co[first + 2, here, :] * field[f, pl.ds(lo + 1, n), :] + co[first + 3, here, :] * field[f, pl.ds(lo - 1, n), :]
        three = co[first + 4, here, :] * next_lane(mid) + co[first + 5, here, :] * last_lane(mid)
        out += [mid, (one + two) + three]
    return out


def kernel(
    n_grp,
    n_sub,
    cot_hbm,
    head_hbm,
    mat_hbm,
    flag_hbm,
    perm_hbm,
    poro_hbm,
    out_ref,
    cot_ref,
    head_ref,
    mat_ref,
    flag_ref,
    perm_tab,
    poro_tab,
    ext,
    perm,
    poro,
    mask,
    face,
    co,
    adj,
    inc,
    res,
    grd,
    mid,
    fin,
    ssend,
    srecv,
    rsend,
    rrecv,
    xsend,
    xrecv,
    ksend,
    krecv,
    cin,
    cedge,
    ring,
    zring,
    cco,
    cres,
    wt,
    wx,
    zeros,
    counted,
    sent,
    came,
):
    g = lax.axis_index("grp")
    s = lax.axis_index("sub")

    def device(dx, dy):
        return {"grp": g + dx, "sub": s + dy}

    def fits(dx, dy):
        found = []
        for at, count, step in ((g, n_grp, dx), (s, n_sub, dy)):
            if step < 0:
                found.append(at >= -step)
            elif step > 0:
                found.append(at < count - step)
        return found[0] if len(found) == 1 else jnp.logical_and(*found)

    loads = [
        pltpu.make_async_copy(src, dst, sent.at[i])
        for i, (src, dst) in enumerate((
            (mat_hbm, mat_ref), (head_hbm, head_ref), (flag_hbm, flag_ref), (cot_hbm, cot_ref), (perm_hbm, perm_tab), (poro_hbm, poro_tab)
        ))
    ]
    for load in loads:
        load.start()

    barrier = pltpu.get_barrier_semaphore()
    expected = jnp.int32(0)
    for dx, dy in PARTNERS:
        there = fits(dx, dy)

        @pl.when(there)
        def _():
            pl.semaphore_signal(barrier, inc=1, device_id=device(dx, dy), device_id_type=MESH)

        expected = expected + there.astype(jnp.int32)

    def rows_of(side, setup):
        dx, dy = side
        if side in FAR:
            return 0
        if setup:
            count = len(slots_of(side, True)) * (2 if dx != 0 and dy != 0 else 8)
            return -(-count // 8) * 8
        return 8 if dx != 0 and dy != 0 else 32

    def halo_part(i, setup):
        side = SIDES[i] if setup else PARTNERS[i]
        halo = rows_of(side, setup)
        if setup:
            return pl.ds(0, halo + (24 if i >= 4 else 0))
        return pl.ds(PAD - halo, halo + (16 if side[0] == 0 else 8))

    def absent(side, dst, at):
        @pl.when(jnp.logical_not(fits(*side)))
        def _():
            pltpu.make_async_copy(zeros.at[pl.ds(0, dst.shape[0])], dst, came.at[at]).start()

    def wait_all(count, at):
        part = counted.at[pl.ds(0, count)]
        pltpu.make_async_copy(part, part, came.at[at]).wait()

    def setup_copy(i):
        dx, dy = SIDES[i]
        part = halo_part(i, True)
        at = PARTNERS.index((dx, dy))
        return pltpu.make_async_remote_copy(
            ssend.at[i, part], srecv.at[i, part], sent.at[at], came.at[0], device_id=device(-dx, -dy), device_id_type=MESH
        )

    def edge_copy(i):
        dx, dy = FAR[i]
        return pltpu.make_async_remote_copy(
            xsend.at[0 if dx < 0 else 1], xrecv.at[i], sent.at[i], came.at[1], device_id=device(-dx, -dy), device_id_type=MESH
        )

    def round_copy(i, k):
        dx, dy = PARTNERS[i]
        part = halo_part(i, False)
        return pltpu.make_async_remote_copy(
            rsend.at[k, i, part], rrecv.at[k, i, part], sent.at[i], came.at[2 - 2 * lax.rem(k, 2)], device_id=device(-dx, -dy), device_id_type=MESH
        )

    def coef_copy(j):
        dx, dy = NEAR[j]
        at = PARTNERS.index((dx, dy)) if abs(dy) == 2 else N_PART + j - 2
        return pltpu.make_async_remote_copy(
            ksend, krecv.at[j], sent.at[at], came.at[1], device_id=device(-dx, -dy), device_id_type=MESH
        )

    def when_sent(side, act):
        pl.when(fits(-side[0], -side[1]))(act)

    zero_rows = jnp.zeros((ROWS, LANES), jnp.float32)
    ext[MAT] = zero_rows - 1.0
    for f in range(1, 7):
        ext[f] = zero_rows
    perm[...] = zero_rows
    poro[...] = zero_rows
    for m in range(9):
        face[m, pl.ds(0, 32), :] = jnp.zeros((32, LANES), jnp.float32)
    for load in loads:
        load.wait()
    for x in range(8):
        ext[MAT, rows(x, 0), :] = mat_ref[x].astype(jnp.float32)
        ext[HEAD, rows(x, 0), :] = head_ref[x]
        for d in range(3):
            ext[F0 + d, rows(x, 0), :] = flag_ref[d, x].astype(jnp.float32)
        for f in range(2):
            ext[COT + f, rows(x, 0), :] = cot_ref[f, x]
    for i, x in enumerate((7, 0)):
        for m, field in enumerate((MAT, HEAD, F0)):
            xsend[i, pl.ds(8 * m, 8), :] = ext[field, rows(x, 0), :]
    for i, side in enumerate(SIDES):
        pack(side, True, ext, ssend, (i,))
        if i >= 4:
            ssend[i, pl.ds(24, 24), :] = xsend[0 if side[0] < 0 else 1]

    def look_up(mats):
        perm_here = jnp.zeros_like(mats)
        poro_here = jnp.zeros_like(mats)
        for level in range(perm_tab.shape[0]):
            same = mats == float(level)
            perm_here = jnp.where(same, perm_tab[level], perm_here)
            poro_here = jnp.where(same, poro_tab[level], poro_here)
        return perm_here, poro_here

    def one_face(perm_here, head_here, perm_next, head_next, upwind):
        both = perm_here + perm_next
        trans = 2.0 * perm_here * perm_next / jnp.where(both > 0.0, both, 1.0)
        flux = trans * (0.5 + jnp.abs(head_here - head_next))
        return trans, upwind * flux, (1.0 - upwind) * flux

    def look_up_rows(first, end, n):
        for lo in range(first, end, n):
            here = pl.ds(lo, n)
            perm[here, :], poro[here, :] = look_up(ext[MAT, here, :])

    def face_rows(first, end, n):
        for lo in range(first, end, n):
            here = pl.ds(lo, n)
            perm_here, head_here = perm[here, :], ext[HEAD, here, :]
            lane = lax.broadcasted_iota(jnp.int32, (n, LANES), 1)
            for d in range(3):
                if d < 2:
                    there = pl.ds(lo + (PITCH, 1)[d], n)
                    perm_next, head_next = perm[there, :], ext[HEAD, there, :]
                else:
                    perm_next = jnp.where(lane == LANES - 1, 0.0, next_lane(perm_here))
                    head_next = next_lane(head_here)
                values = one_face(perm_here, head_here, perm_next, head_next, ext[F0 + d, here, :])
                for m in range(3):
                    face[3 * d + m, here, :] = values[m]

    look_up_rows(32, 128, 32)
    face_rows(32, 128, 24)

    def put(ref, at, value):
        value = four_sum(value)
        ref[pl.ds(at, 1), :] = value[0:1]
        ref[pl.ds(at + 1, 1), :] = value[4:5]

    lane = lax.broadcasted_iota(jnp.int32, (8, LANES), 1)
    for cx in range(2):
        sums = [0.0] * 7
        for x in range(4 * cx, 4 * cx + 4):
            here = rows(x, 0)
            zs = [face[6 + m, here, :] for m in range(3)]
            out = face[1, here, :] + face[4, here, :] + zs[1]
            out = out + face[2, rows(x - 1, 0), :] + face[5, rows(x, -1), :] + last_lane(zs[2])
            news = [poro[here, :], out] + zs + [ext[COT + f, here, :] for f in range(2)]
            sums = [old + new for old, new in zip(sums, news)]
        for m in range(2, 5):
            sums[m] = jnp.where(lane % AGG == AGG - 1, sums[m], 0.0)
        for item, value in zip((0, 2, 4, 6, 8, 13, 15), sums):
            put(ksend, 2 * (item + cx), value)
    for m in range(3):
        put(ksend, 2 * (10 + m), face[m, rows(3, 0), :])
        put(ksend, 2 * (17 + m), face[3 + m, column(3), :])
    ksend[pl.ds(0, C_RAW), :] = lane_sum(ksend[pl.ds(0, C_RAW), :])
    raw = [
        (MAT, rows(0, 0)), (HEAD, rows(0, 0)), (MAT, rows(7, 0)), (HEAD, rows(7, 0)), (F0, rows(7, 0)),
        (MAT, column(0)), (HEAD, column(0)), (MAT, column(7)), (HEAD, column(7)), (F1, column(7)),
    ]
    for slot, (field, where) in enumerate(raw):
        ksend[pl.ds(C_RAW + 8 * slot, 8), :] = ext[field, where, :]
    pl.semaphore_wait(barrier, expected)
    for i in reversed(range(8)):
        when_sent(SIDES[i], lambda: setup_copy(i).start())
    for i in range(4):
        when_sent(FAR[i], lambda: edge_copy(i).start())

    for j in range(4):
        when_sent(NEAR[j], lambda: coef_copy(j).start())

    zeros[...] = jnp.zeros((C_ROWS, LANES), jnp.float32)
    for i, side in enumerate(SIDES):
        absent(side, srecv.at[i, halo_part(i, True)], 0)
    for i, side in enumerate(FAR[:4]):
        absent(side, xrecv.at[i], 1)
    for j, side in enumerate(NEAR):
        absent(side, krecv.at[j], 1)
    zring[...] = jnp.zeros((16, LANES), jnp.float32)
    mask[...] = zero_rows
    for f in range(2):
        adj[f] = zero_rows
        grd[f] = zero_rows
        mid[f] = zero_rows
    for x in range(-1, 9):
        mask[rows(x, -1, 10), :] = jnp.ones((10, LANES), jnp.float32)


    wait_all(sum(halo_part(i, True).size for i in range(8)), 0)
    for i, side in enumerate(SIDES):
        unpack(side, True, srecv, (i,), ext, fits(*side))
    look_up_rows(0, ROWS, 32)
    face_rows(0, 144, 24)
    for lo in range(16, 144, 16):
        here = pl.ds(lo, 16)
        total = jnp.zeros((16, LANES), jnp.float32)
        out = total
        for d in range(3):
            trans, upper, lower = (face[3 * d + m, here, :] for m in range(3))
            if d < 2:
                back = pl.ds(lo - (PITCH, 1)[d], 16)
                trans_m, lower_m = face[3 * d, back, :], face[3 * d + 2, back, :]
            else:
                trans_m, lower_m = last_lane(trans), last_lane(lower)
            co[TX + 2 * d, here, :] = trans
            co[TX + 2 * d + 1, here, :] = trans_m
            co[SX + 2 * d, here, :] = DISP * trans + upper
            co[SX + 2 * d + 1, here, :] = DISP * trans_m + lower_m
            total = total + trans + trans_m
            out = out + upper + lower_m
        store = poro[here, :]
        bpp, bpc, bcp, bcc = store + total, -CPL_S * out, CPL_P * store, store + DISP * total + out
        inside = jnp.logical_and(store > 0.0, mask[here, :] > 0.0)
        determ = jnp.where(inside, bpp * bcc - bpc * bcp, 1.0)
        scale = jnp.where(inside, OMEGA / determ, 0.0)
        for at, value in (
            (BPP, bpp), (BPC, bpc), (BCP, bcp), (BCC, bcc),
            (IPP, bcc * scale), (IPC, -bpc * scale), (ICP, -bcp * scale), (ICC, bpp * scale),
        ):
            co[at, here, :] = value

    def fine_solve(src, at):
        for lo in range(16, 144, 32):
            here = pl.ds(lo, 32)
            r_p, r_c = src[at, here, :], src[at + 1, here, :]
            grd[0, here, :] = co[IPP, here, :] * r_p + co[IPC, here, :] * r_c
            grd[1, here, :] = co[ICP, here, :] * r_p + co[ICC, here, :] * r_c
        for lo in range(16, 144, 16):
            here = pl.ds(lo, 16)
            z_p, s_p, z_c, s_c = couple(co, grd, lo, 16)
            mid[0, here, :] = (2.0 - OMEGA) * z_p + co[IPP, here, :] * s_p + co[IPC, here, :] * s_c
            mid[1, here, :] = (2.0 - OMEGA) * z_c + co[ICP, here, :] * s_p + co[ICC, here, :] * s_c
        for lo in range(32, 128, 16):
            here = pl.ds(lo, 16)
            z_p, s_p, z_c, s_c = couple(co, mid, lo, 16)
            fin[0, here, :] = (1.0 - OMEGA) * z_p + grd[0, here, :] + co[IPP, here, :] * s_p + co[IPC, here, :] * s_c
            fin[1, here, :] = (1.0 - OMEGA) * z_c + grd[1, here, :] + co[ICP, here, :] * s_p + co[ICC, here, :] * s_c

    def coarse_solve():
        inv = [[cco[b, cx] for cx in range(2)] for b in range(4)]
        r = [[cres[2 * f + cx] for cx in range(2)] for f in range(2)]

        def inverse(v):
            return [[inv[2 * f][cx] * v[0][cx] + inv[2 * f + 1][cx] * v[1][cx] for cx in range(2)] for f in range(2)]

        base = inverse(r)
        z = base
        for sweep in range(3):
            acc = [[None] * 2 for f in range(2)]
            for f in range(2):
                for cx in range(2):
                    v = z[f][cx]
                    first = 4 + 5 * f
                    along = cco[first, cx] * pltpu.roll(v, 7, 0) + cco[first + 1, cx] * pltpu.roll(v, 1, 0)
                    down = cco[first + 2, cx] * next_lane(v, AGG) + cco[first + 3, cx] * last_lane(v, AGG)
                    acc[f][cx] = cco[first + 4, cx] * z[f][1 - cx] + (along + down)
            more = inverse(acc)
            z = [[((1.0 - OMEGA_C) * z[f][cx] + base[f][cx]) + more[f][cx] for cx in range(2)] for f in range(2)]
        upper = lax.broadcasted_iota(jnp.int32, (8, LANES), 0) < AGG
        return [
            [
                jnp.where(upper, jnp.broadcast_to(v[3:4], (8, LANES)), jnp.broadcast_to(v[4:5], (8, LANES)))
                for v in z[f]
            ]
            for f in range(2)
        ]

    def update():
        grown = coarse_solve()
        for f in range(2):
            for x in range(8):
                here = rows(x, 0)
                more = THETA * (fin[f, here, :] + grown[f][x // 4])
                new = adj[f, here, :] + more
                inc[f, x] = more
                adj[f, here, :] = new
                out_ref[f, x] = new

    def send(k):
        def place(at, value):
            ring[pl.ds(8 + at, 1), :] = value

        e = [[inc[f, x] for x in range(8)] for f in range(2)]
        for f in range(2):
            for cx in range(2):
                terms = [[], [], [], [], []]
                for x in range(4 * cx, 4 * cx + 4):
                    terms[0].append(wt[6 * f, x] * e[f][x] + wt[6 * f + 1, x] * e[1 - f][x])
                    for m in range(4):
                        terms[1 + m].append(wt[6 * f + 2 + m, x] * e[f][x])
                total, y_next, y_last, z_next, z_last = ((t[0] + t[1]) + (t[2] + t[3]) for t in terms)
                passed = four_sum(z_next + z_last)
                zring[pl.ds(8 * f + 4 * cx + 1, 1), :] = passed[0:1]
                zring[pl.ds(8 * f + 4 * cx + 2, 1), :] = passed[4:5]
                other = wx[f, 1, 0] * e[f][4] if cx == 0 else wx[f, 0, 1] * e[f][3]
                total = four_sum(total - other)
                at = 8 * f + 4 * cx
                place(at, -y_last[0:1])
                place(at + 1, total[0:1] - y_last[4:5])
                place(at + 2, total[4:5] - y_next[3:4])
                place(at + 3, -y_next[7:8])
            for at, value in ((16, wx[f, 0, 0] * e[f][0]), (20, wx[f, 1, 1] * e[f][7])):
                total = four_sum(value)
                place(at + 2 * f, -total[0:1])
                place(at + 2 * f + 1, -total[4:5])
        along = lane_sum(ring[pl.ds(8, 16), :]) - lane_pass(zring[...])
        beside = lane_sum(ring[pl.ds(24, 8), :])
        ring[pl.ds(8, 16), :] = along
        for i, side in enumerate(PARTNERS):
            if side not in FAR:
                pack(side, False, adj, rsend, (k, i), PAD - rows_of(side, False))
            if side[0] == 0:
                rsend[k, i, pl.ds(PAD, 16), :] = along
            else:
                rsend[k, i, pl.ds(PAD, 8), :] = beside
            when_sent(side, lambda: round_copy(i, k).start())
        for i, side in enumerate(PARTNERS):
            absent(side, rrecv.at[k, i, halo_part(i, False)], 2 - 2 * lax.rem(k, 2))

    def receive(k):
        for i, side in enumerate(PARTNERS):
            when_sent(side, lambda: round_copy(i, k).wait_send())
        wait_all(sum(halo_part(i, False).size for i in range(N_PART)), 2 - 2 * lax.rem(k, 2))
        at_row = lax.broadcasted_iota(jnp.int32, (8, LANES), 0)
        for f in range(2):
            for cx in range(2):
                item = 2 * f + cx

                def along(dy, shift):
                    return rrecv[k, PARTNERS.index((0, dy)), pl.ds(PAD + 4 * item + shift, 8), :]

                def beside(dy):
                    dx = 2 * cx - 1
                    at = PAD + (4 if dx < 0 else 0) + 2 * f
                    return rrecv[k, PARTNERS.index((dx, dy)), pl.ds(at - 2 * dy - 3, 8), :]

                one = jnp.where(at_row < 4, along(-1, 0), along(1, -4))
                two = jnp.where(at_row < 2, along(-2, 2), jnp.where(at_row < 6, ring[pl.ds(8 + 4 * item - 2, 8), :], along(2, -6)))
                three = jnp.where(at_row < 1, beside(-2), jnp.where(at_row < 3, beside(-1), beside(0)))
                three = jnp.where(at_row < 5, three, jnp.where(at_row < 7, beside(1), beside(2)))
                cres[item] = cres[item] - ((one + two) + three)
        for i, side in enumerate(PARTNERS):
            if side not in FAR:
                unpack(side, False, rrecv, (k, i), adj, None, PAD - rows_of(side, False))
        for lo in range(16, 144, 16):
            here = pl.ds(lo, 16)
            z_p, s_p, z_c, s_c = couple(co, adj, lo, 16)
            res[0, here, :] = ext[COT, here, :] + s_p - co[BPP, here, :] * z_p - co[BPC, here, :] * z_c
            res[1, here, :] = ext[COT + 1, here, :] + s_c - co[BCP, here, :] * z_p - co[BCC, here, :] * z_c

    fine_solve(ext, COT)

    for i, side in enumerate(SIDES):
        when_sent(side, lambda: setup_copy(i).wait_send())
    for j, side in enumerate(NEAR):
        when_sent(side, lambda: coef_copy(j).wait_send())
        when_sent(FAR[j], lambda: edge_copy(j).wait_send())
    wait_all(4 * C_ROWS + 4 * 24, 1)

    def near(u):
        return NEAR.index((0, u))

    def inner(u, at, count):
        return (ksend[pl.ds(at, count), :] if u == 0 else krecv[near(u), pl.ds(at, count), :])

    def raw_of(u, slot):
        value = inner(u, C_RAW + 8 * slot, 8)
        return jnp.where(fits(0, u), value, -1.0) if u != 0 and slot in (0, 2, 5, 7) else value

    def beyond(dx, u, m):
        if u == 0:
            return ext[(MAT, HEAD, F0)[m], rows(-1 if dx < 0 else 8, 0), :]
        if abs(u) == 1:
            value = srecv[SIDES.index((dx, u)), pl.ds(24 + 8 * m, 8), :]
        else:
            value = xrecv[FAR.index((dx, u)), pl.ds(8 * m, 8), :]
        return jnp.where(fits(dx, u), value, -1.0) if m == 0 else value

    def between(mat_a, head_a, flag, mat_b, head_b):
        return one_face(look_up(mat_a)[0], head_a, look_up(mat_b)[0], head_b, flag)

    def put_rows(tile, u, value):
        value = four_sum(value)
        if u > -2:
            cedge[tile, pl.ds(2 * u + 3, 1), :] = value[0:1]
        if u < 2:
            cedge[tile, pl.ds(2 * u + 4, 1), :] = value[4:5]

    for tile in range(4, 10):
        cedge[tile] = jnp.zeros((8, LANES), jnp.float32)
    for u in range(-2, 3):
        trans, _, lower = between(*(beyond(-1, u, m) for m in range(3)), raw_of(u, 0), raw_of(u, 1))
        put_rows(0, u, trans)
        put_rows(1, u, lower)
        trans, upper, _ = between(raw_of(u, 2), raw_of(u, 3), raw_of(u, 4), beyond(1, u, 0), beyond(1, u, 1))
        put_rows(2, u, trans)
        put_rows(3, u, upper)
        if u < 2:
            values = between(raw_of(u, 7), raw_of(u, 8), raw_of(u, 9), raw_of(u + 1, 5), raw_of(u + 1, 6))
            for m in range(3):
                value = four_sum(values[m])
                for cx in range(2):
                    cedge[4 + 2 * m + cx, pl.ds(2 * u + 4, 1), :] = value[4 * cx : 4 * cx + 1]
    for tile in range(10):
        cedge[tile] = lane_sum(cedge[tile])
    for m in range(3):
        for cx in range(2):
            for u in range(-1, 3):
                cedge[4 + 2 * m + cx, pl.ds(2 * u + 3, 1), :] = inner(u, 34 + 2 * m + cx, 1)
    for item in range(N_INNER):

        def put_inner(where, value):
            if item < 13:
                cin[item, where, :] = value
            else:
                cres[item - 13, where, :] = value

        put_inner(pl.ds(0, 1), inner(-2, 2 * item + 1, 1))
        put_inner(pl.ds(1, 2), inner(-1, 2 * item, 2))
        put_inner(pl.ds(3, 2), inner(0, 2 * item, 2))
        put_inner(pl.ds(5, 2), inner(1, 2 * item, 2))
        put_inner(pl.ds(7, 1), inner(2, 2 * item, 1))

    place = lax.broadcasted_iota(jnp.int32, (8, LANES), 0)
    m_t, m_a, m_b = (cin[10 + m] for m in range(3))
    for cx in range(2):
        store, out, t_z, a_z, b_z = (cin[2 * m + cx] for m in range(5))
        t_y, a_y, b_y = (cedge[4 + 2 * m + cx] for m in range(3))
        under_t, under_b = (
            jnp.where(place == 0, jnp.broadcast_to(inner(-2, 34 + 2 * m + cx, 1), (8, LANES)), pltpu.roll(value, 1, 0))
            for m, value in ((0, t_y), (2, b_y))
        )
        side_t, side_out = (cedge[0], cedge[1]) if cx == 0 else (cedge[2], cedge[3])
        edge_sum = m_t + side_t + t_y + under_t + t_z + last_lane(t_z, AGG)
        edge_out = (m_a if cx == 0 else m_b) + side_out + a_y + under_b + a_z + last_lane(b_z, AGG)
        out = out + side_out + jnp.where(place % 2 == 0, a_y, under_b)
        cpp, cpc, ccp, ccc = store + edge_sum, -CPL_S * out, CPL_P * store, store + DISP * edge_sum + edge_out
        inside = cpp > 0.0
        determ = jnp.where(inside, cpp * ccc - cpc * ccp, 1.0)
        scale = jnp.where(inside, OMEGA_C / determ, 0.0)
        for b, value in enumerate((
            ccc * scale, -cpc * scale, -ccp * scale, cpp * scale,
            t_y, pltpu.roll(t_y, 1, 0), t_z, last_lane(t_z, AGG), m_t,
            DISP * t_y + a_y, pltpu.roll(DISP * t_y + b_y, 1, 0), DISP * t_z + a_z, last_lane(DISP * t_z + b_z, AGG),
            DISP * m_t + (m_a if cx == 0 else m_b),
        )):
            cco[b, cx] = value
    y_at = lax.broadcasted_iota(jnp.int32, (8, LANES), 0) % AGG
    z_at = lax.broadcasted_iota(jnp.int32, (8, LANES), 1) % AGG
    for x in range(8):
        here = rows(x, 0)
        to_next = [[co[TX + 2 * d, here, :] for d in range(3)], [DISP * face[3 * d, here, :] + face[3 * d + 2, here, :] for d in range(3)]]
        to_last = [
            [co[TXM + 2 * d, here, :] for d in range(3)],
            [co[SX, rows(x - 1, 0), :], co[SY, rows(x, -1), :], last_lane(co[SZ, here, :])],
        ]
        for f in range(2):
            own = co[BCC if f else BPP, here, :]
            if x % AGG != AGG - 1:
                own = own - to_next[f][0]
            if x % AGG != 0:
                own = own - to_last[f][0]
            y_next, y_last = (jnp.where(y_at == edge, v[f][1], 0.0) for edge, v in ((AGG - 1, to_next), (0, to_last)))
            z_next, z_last = (jnp.where(z_at == edge, v[f][2], 0.0) for edge, v in ((AGG - 1, to_next), (0, to_last)))
            own = own - (((to_next[f][1] - y_next) + (to_last[f][1] - y_last)) + ((to_next[f][2] - z_next) + (to_last[f][2] - z_last)))
            for m, value in enumerate((own, co[BCP if f else BPC, here, :], y_next, y_last, z_next, z_last)):
                wt[6 * f + m, x] = value
            if x % AGG == 0:
                wx[f, x // AGG, 0] = to_last[f][0]
            if x % AGG == AGG - 1:
                wx[f, x // AGG, 1] = to_next[f][0]

    update()
    send(0)

    def step(k, carry):
        receive(k - 1)
        fine_solve(res, 0)
        update()
        pl.when(k < ITERS - 1)(lambda: send(k))
        return carry

    lax.fori_loop(1, ITERS, step, 0)


def solution(mesh):
    n_grp, n_sub = mesh.shape["grp"], mesh.shape["sub"]

    def local(cotangent, head, materials, flags, perm_table, poro_table):
        def tile(*shape):
            return pltpu.VMEM(shape + (LANES,), jnp.float32)

        dma = pltpu.SemaphoreType.DMA
        vmem = pl.BlockSpec(memory_space=pltpu.VMEM)
        hbm = pl.BlockSpec(memory_space=pltpu.HBM)
        return pl.pallas_call(
            functools.partial(kernel, n_grp, n_sub),
            out_shape=pltpu.VMEM(cotangent.shape, jnp.float32),
            in_specs=[hbm] * 6,
            out_specs=vmem,
            scratch_shapes=[
                pltpu.VMEM(cotangent.shape, jnp.float32),
                pltpu.VMEM(head.shape, jnp.float32),
                pltpu.VMEM(materials.shape, jnp.int32),
                pltpu.VMEM(flags.shape, jnp.int32),
                pltpu.SMEM(perm_table.shape, jnp.float32),
                pltpu.SMEM(poro_table.shape, jnp.float32),
                tile(7, ROWS),
                tile(ROWS),
                tile(ROWS),
                tile(ROWS),
                tile(9, ROWS),
                tile(N_COEF, ROWS),
                tile(2, ROWS),
                tile(2, 8, 8),
                tile(2, ROWS),
                tile(2, ROWS),
                tile(2, ROWS),
                tile(2, ROWS),
                tile(8, 80),
                tile(8, 80),
                tile(ROUNDS, N_PART, R_ROWS),
                tile(ROUNDS, N_PART, R_ROWS),
                tile(2, 24),
                tile(4, 24),
                tile(C_ROWS),
                tile(4, C_ROWS),
                tile(13, 8),
                tile(10, 8),
                tile(32),
                tile(16),
                tile(N_CBLK, 2, 8),
                tile(4, 8),
                tile(12, 8, 8),
                tile(2, 2, 2, 8),
                tile(C_ROWS),
                tile(4 * C_ROWS + 4 * 24),
                dma((N_PART + 2,)),
                dma((3,)),
            ],
            compiler_params=pltpu.CompilerParams(
                collective_id=0, has_side_effects=True, vmem_limit_bytes=32 * 1024 * 1024
            ),
        )(*(pltpu.with_memory_space_constraint(x, pltpu.HBM) for x in (cotangent, head, materials, flags, perm_table, poro_table)))

    return jax.shard_map(
        local,
        mesh=mesh,
        in_specs=(
            P(None, "grp", "sub", None),
            P("grp", "sub", None),
            P("grp", "sub", None),
            P(None, "grp", "sub", None),
            P(),
            P(),
        ),
        out_specs=P(None, "grp", "sub", None),
        check_vma=False,
    )
```
